256 devices in a mesh: dom: 64 (over z, x, core), sub: 4 (over y).
Axes of the slice: x: 4, y: 4, z: 8, core: 2. Of those that a mesh axis runs over, the one named last changes fastest.
Arguments:
- flow_pops: float32 [512, 19, 512], P(('dom', 'sub')), may hold values from 0 to 0.5, as said below
- bin_pops: float32 [512, 84, 512], P(('dom', 'sub')), may hold values from 0 to 1, as said below
- site_kind: int32 [512, 512], P(('dom', 'sub')), may hold values from 0 to 3, as said below
- neighbours: int32 [512, 18], P(('dom', 'sub')), may hold values from -1 to 511, as said below
- bin_rates: float32 [12], replicated, may hold values from 0.8 to 1.9
- settle: float32 [12], replicated, may hold values from 0.005 to 0.05
- inlet_conc: float32 [12], replicated, may hold values from 0.3 to 3
Outputs:
- flow_out: float32 [512, 19, 512], P(('dom', 'sub'))
- bins_out: float32 [512, 84, 512], P(('dom', 'sub'))
- deposit: float32 [512, 12], P(('dom', 'sub'))
The draws below stay inside these ranges and needn't reach their ends.
Inputs may be any that keep to these rules, and one draw needn't show every extreme that they name: `site_kind`: 0 solid, 1 fluid, 2 inlet (the first layer of sites along the segment), 3 outlet (the last). `neighbours`: relations are mutual; a block and its neighbour are held by devices at most 3 apart in the order of dom+sub, and that distance is reached. Blocks are numbered layer by layer along the segment, so a layer's blocks lie on two consecutive devices. `flow_pops`: positive. `bin_pops`: positive.
All inputs are finite; a program needn't handle non-finite values.
Results may differ from the reference program's by a relative error of at most 0.0003.
Values sent between devices are 32-bit elements; how exact they have to be, the bound alone decides.
A program may use at most 64 MiB of HBM per device.

```python
import math
import jax
import jax.numpy as jnp
import numpy as np

EDGE = 8
SIDE = 2
BINS = 12
STEPS = 2
SITES = 512
BLOCKS = 512
LAYERS = 128


velocities = np.array([[0, 0, 0], [1, 0, 0], [-1, 0, 0], [0, 1, 0], [0, -1, 0], [0, 0, 1], [0, 0, -1], [1, 1, 0], [-1, -1, 0], [1, -1, 0], [-1, 1, 0], [1, 0, 1], [-1, 0, -1], [1, 0, -1], [-1, 0, 1], [0, 1, 1], [0, -1, -1], [0, 1, -1], [0, -1, 1]])


weights_flow = [1.0 / 3.0] + [1.0 / 18.0] * 6 + [1.0 / 36.0] * 12


weights_seven = [0.25] + [0.125] * 6


def block_geometry(key):
    key = jax.random.fold_in(key, 101)
    order_key, layer_key, site_key = jax.random.split(key, 3)
    slot_count = SIDE * SIDE
    scores = jax.random.randint(order_key, (LAYERS, slot_count), 0, 2 ** 20) * slot_count + jnp.arange(slot_count)[None, :]
    parity = jnp.arange(LAYERS) % 2
    scores = scores.at[:, 0].set(jnp.where(parity == 0, -1, 2 ** 30))
    slot_of_rank = jnp.argsort(scores, axis=1).astype(jnp.int32)
    rank_of_slot = jnp.argsort(slot_of_rank, axis=1).astype(jnp.int32)
    block_ids = jnp.arange(BLOCKS)
    layer_num = block_ids // slot_count
    slot_num = slot_of_rank[layer_num, block_ids % slot_count]
    row_num = slot_num // SIDE
    col_num = slot_num % SIDE
    offsets = jnp.asarray(velocities[1:], jnp.int32)
    near_row = row_num[:, None] + offsets[None, :, 0]
    near_col = col_num[:, None] + offsets[None, :, 1]
    near_layer = layer_num[:, None] + offsets[None, :, 2]
    inside = (near_row >= 0) & (near_row < SIDE) & (near_col >= 0) & (near_col < SIDE) & (near_layer >= 0) & (near_layer < LAYERS)
    near_slot = jnp.clip(near_row, 0, SIDE - 1) * SIDE + jnp.clip(near_col, 0, SIDE - 1)
    safe_layer = jnp.clip(near_layer, 0, LAYERS - 1)
    near_ids = safe_layer * slot_count + rank_of_slot[safe_layer, near_slot]
    neighbours = jnp.where(inside, near_ids, -1).astype(jnp.int32)
    site_ids = jnp.arange(SITES)
    first_coord = site_ids // (EDGE * EDGE)
    second_coord = site_ids // EDGE % EDGE
    third_coord = site_ids % EDGE
    across = SIDE * EDGE
    pos_x = row_num[:, None] * EDGE + first_coord[None, :]
    pos_y = col_num[:, None] * EDGE + second_coord[None, :]
    pos_z = layer_num[:, None] * EDGE + third_coord[None, :]
    distance = (2 * pos_x + 1 - across) ** 2 + (2 * pos_y + 1 - across) ** 2
    radius = across * across * 81 // 100
    widening = jax.random.randint(layer_key, (LAYERS,), -(radius // 10), radius // 10 + 1)
    roughness = jax.random.randint(site_key, (BLOCKS, SITES), -(radius // 12), radius // 12 + 1)
    is_fluid = (distance < radius + widening[layer_num][:, None] + roughness).astype(jnp.int32)
    end_flags = 1 + (pos_z == 0).astype(jnp.int32) + 2 * (pos_z == LAYERS * EDGE - 1).astype(jnp.int32)
    return (neighbours, (is_fluid * end_flags).astype(jnp.int32))


def draw_neighbours(key, part):
    return block_geometry(key)[0]


def draw_site_kind(key, part):
    return block_geometry(key)[1]


def draw_flow_pops(key, part):
    key = jax.random.fold_in(key, 7)
    weights = jnp.asarray(weights_flow, jnp.float32)[None, :, None]
    lifting = 1.0 + 0.09 * jnp.asarray(velocities[:, 2], jnp.float32)[None, :, None]
    jitter = jnp.clip(0.1 * jax.random.normal(key, (BLOCKS, 19, SITES), jnp.float32), -0.25, 0.25)
    return weights * lifting * (1.0 + jitter)


def draw_bin_pops(key, part):
    key = jax.random.fold_in(key, 9)
    conc_key, jitter_key, scale_key = jax.random.split(key, 3)
    weights = jnp.asarray(weights_seven, jnp.float32)[None, None, :, None]
    concentration = jnp.exp(jax.random.uniform(conc_key, (BLOCKS, BINS, 1, SITES), jnp.float32, np.log(0.3), np.log(3.0)))
    jitter = jnp.clip(0.15 * jax.random.normal(jitter_key, (BLOCKS, BINS, 7, SITES), jnp.float32), -0.25, 0.25)
    values = weights * concentration * (1.0 + jitter)
    return values.reshape(BLOCKS, BINS * 7, SITES)


def setup_inputs(seed: int = 0) -> dict:
    key_of = jax.random.split(jax.random.key(seed), 8)
    return {
        "flow_pops": draw_flow_pops(jax.random.fold_in(key_of[7], 71), 0),
        "bin_pops": draw_bin_pops(jax.random.fold_in(key_of[7], 71), 0),
        "site_kind": draw_site_kind(jax.random.fold_in(key_of[7], 71), 0),
        "neighbours": draw_neighbours(jax.random.fold_in(key_of[7], 71), 0),
        "bin_rates": jnp.clip(jax.random.uniform(key_of[4], (BINS,), jnp.float32, 0.8, 1.9), 0.8, 1.9),
        "settle": jnp.clip(jnp.exp(jax.random.uniform(key_of[5], (BINS,), jnp.float32, math.log(0.005), math.log(0.05))), 0.005, 0.05),
        "inlet_conc": jnp.clip(jnp.exp(jax.random.uniform(key_of[6], (BINS,), jnp.float32, math.log(0.3), math.log(3.0))), 0.3, 3.0),
    }


velocities = np.array([[0, 0, 0], [1, 0, 0], [-1, 0, 0], [0, 1, 0], [0, -1, 0], [0, 0, 1], [0, 0, -1],
                       [1, 1, 0], [-1, -1, 0], [1, -1, 0], [-1, 1, 0], [1, 0, 1], [-1, 0, -1], [1, 0, -1],
                       [-1, 0, 1], [0, 1, 1], [0, -1, -1], [0, 1, -1], [0, -1, 1]])
weights_flow = [1.0 / 3.0] + [1.0 / 18.0] * 6 + [1.0 / 36.0] * 12
weights_seven = [0.25] + [0.125] * 6
opposite = [0, 2, 1, 4, 3, 6, 5, 8, 7, 10, 9, 12, 11, 14, 13, 16, 15, 18, 17]
omega_flow = 1.6
inlet_speed = 0.04


def site_tables(edge_len):
    site_count = edge_len ** 3
    square = edge_len * edge_len
    lattice = [[site_num // square, (site_num // edge_len) % edge_len, site_num % edge_len] for site_num in range(site_count)]
    vel_list = [[int(velocities[pop_num, axis_num]) for axis_num in range(3)] for pop_num in range(19)]
    face_sites = []
    out_rows = []
    for face_num in range(6):
        axis_num = face_num // 2
        sign_val = 1 - 2 * (face_num % 2)
        layer_val = edge_len - 1 if sign_val > 0 else 0
        face_sites.append(np.array([site_num for site_num in range(site_count) if lattice[site_num][axis_num] == layer_val], np.int32))
        out_rows.append([pop_num for pop_num in range(1, 19) if vel_list[pop_num][axis_num] == sign_val])
    edge_sites = []
    for edge_num in range(12):
        vector = vel_list[7 + edge_num]
        chosen = []
        for site_num in range(site_count):
            keep = True
            for axis_num in range(3):
                if vector[axis_num] != 0 and lattice[site_num][axis_num] != (edge_len - 1 if vector[axis_num] > 0 else 0):
                    keep = False
            if keep:
                chosen.append(site_num)
        edge_sites.append(np.array(chosen, np.int32))
    source = np.zeros((19, site_count), np.int32)
    source[0] = np.arange(site_count)
    for pop_num in range(1, 19):
        for site_num in range(site_count):
            shifted = [lattice[site_num][axis_num] - vel_list[pop_num][axis_num] for axis_num in range(3)]
            step_here = [value // edge_len for value in shifted]
            spot_here = [shifted[axis_num] - step_here[axis_num] * edge_len for axis_num in range(3)]
            moving = [axis_num for axis_num in range(3) if step_here[axis_num] != 0]
            if len(moving) == 0:
                source[pop_num, site_num] = (spot_here[0] * edge_len + spot_here[1]) * edge_len + spot_here[2]
            elif len(moving) == 1:
                axis_num = moving[0]
                face_num = 2 * axis_num + (0 if step_here[axis_num] > 0 else 1)
                others = [other_axis for other_axis in range(3) if other_axis != axis_num]
                source[pop_num, site_num] = site_count + face_num * square + spot_here[others[0]] * edge_len + spot_here[others[1]]
            else:
                edge_num = [edge_idx for edge_idx in range(12) if vel_list[7 + edge_idx] == step_here][0]
                free_axis = [other_axis for other_axis in range(3) if step_here[other_axis] == 0][0]
                source[pop_num, site_num] = site_count + 6 * square + edge_num * edge_len + spot_here[free_axis]
    return face_sites, out_rows, edge_sites, source


def components(count):
    return [jnp.asarray(velocities[:count, axis_num], jnp.float32) for axis_num in range(3)]


def moments(flow_now):
    density = jnp.sum(flow_now, axis=1)
    velocity = [jnp.sum(column[None, :, None] * flow_now, axis=1) / density for column in components(19)]
    return density, velocity


def flow_equilibrium(density, velocity):
    columns = components(19)
    along_c = columns[0][None, :, None] * velocity[0][:, None, :] + columns[1][None, :, None] * velocity[1][:, None, :] + columns[2][None, :, None] * velocity[2][:, None, :]
    speed_square = (velocity[0] * velocity[0] + velocity[1] * velocity[1] + velocity[2] * velocity[2])[:, None, :]
    weights = jnp.asarray(weights_flow, jnp.float32)[None, :, None]
    return weights * density[:, None, :] * (1.0 + 3.0 * along_c + 4.5 * along_c * along_c - 1.5 * speed_square)


def bin_drift(velocity, settle):
    return [velocity[0][:, None, :] + jnp.zeros_like(settle)[None, :, None], velocity[1][:, None, :] - settle[None, :, None], velocity[2][:, None, :] + jnp.zeros_like(settle)[None, :, None]]


def bin_equilibrium(concentration, drift_vel):
    columns = components(7)
    along_c = columns[0][None, None, :, None] * drift_vel[0][:, :, None, :] + columns[1][None, None, :, None] * drift_vel[1][:, :, None, :] + columns[2][None, None, :, None] * drift_vel[2][:, :, None, :]
    weights = jnp.asarray(weights_seven, jnp.float32)[None, None, :, None]
    return weights * concentration[:, :, None, :] * (1.0 + 4.0 * along_c)


def collide(flow_now, bins_now, bin_rates, settle):
    density, velocity = moments(flow_now)
    post_flow = flow_now + omega_flow * (flow_equilibrium(density, velocity) - flow_now)
    concentration = jnp.sum(bins_now, axis=2)
    target = bin_equilibrium(concentration, bin_drift(velocity, settle))
    post_bins = bins_now + bin_rates[None, :, None, None] * (target - bins_now)
    return post_flow, post_bins


def pack_faces(post_flow, post_bins, tables):
    face_sites, out_rows, edge_sites, source = tables
    face_parts = []
    for face_num in range(6):
        flow_rows = jnp.take(jnp.take(post_flow, np.array(out_rows[face_num]), axis=1), face_sites[face_num], axis=2)
        bin_rows = jnp.take(post_bins[:, :, 1 + face_num], face_sites[face_num], axis=2)
        face_parts.append(jnp.concatenate([flow_rows, bin_rows], axis=1))
    faces = jnp.concatenate(face_parts, axis=2)
    edges = jnp.concatenate([jnp.take(post_flow[:, 7 + edge_num], edge_sites[edge_num], axis=1) for edge_num in range(12)], axis=1)
    return faces, edges


def pack_kinds(site_kind, tables):
    face_sites, out_rows, edge_sites, source = tables
    faces = jnp.concatenate([jnp.take(site_kind, face_sites[face_num], axis=1) for face_num in range(6)], axis=1)
    edges = jnp.concatenate([jnp.take(site_kind, edge_sites[edge_num], axis=1) for edge_num in range(12)], axis=1)
    return faces, edges


def window_rows(neighbours, start, count):
    present = neighbours >= 0
    positions = jnp.clip(neighbours - start, 0, count - 1).astype(jnp.int32)
    return present, positions


def extend(post_flow, post_bins, neighbours, win_faces, win_edges, start, tables):
    face_sites, out_rows, edge_sites, source = tables
    edge_len = len(edge_sites[0])
    square = edge_len * edge_len
    blocks_here = post_flow.shape[0]
    bin_count = post_bins.shape[1]
    present, positions = window_rows(neighbours, start, win_faces.shape[0])
    got_faces = jnp.take(win_faces, positions[:, :6], axis=0)
    got_edges = jnp.take(win_edges, positions[:, 6:], axis=0)
    flow_parts = [post_flow]
    bin_parts = [post_bins]
    for face_num in range(6):
        facing = face_num ^ 1
        section = got_faces[:, face_num, :, facing * square:(facing + 1) * square]
        section = jnp.where(present[:, face_num, None, None], section, 0.0)
        flow_parts.append(jnp.zeros((blocks_here, 19, square), jnp.float32).at[:, np.array(out_rows[facing])].set(section[:, :5]))
        bin_parts.append(jnp.zeros((blocks_here, bin_count, 7, square), jnp.float32).at[:, :, 1 + facing].set(section[:, 5:]))
    for edge_num in range(12):
        facing = edge_num ^ 1
        section = got_edges[:, edge_num, facing * edge_len:(facing + 1) * edge_len]
        section = jnp.where(present[:, 6 + edge_num, None], section, 0.0)
        flow_parts.append(jnp.zeros((blocks_here, 19, edge_len), jnp.float32).at[:, 7 + facing].set(section))
    bin_parts.append(jnp.zeros((blocks_here, bin_count, 7, 12 * edge_len), jnp.float32))
    return jnp.concatenate(flow_parts, axis=2), jnp.concatenate(bin_parts, axis=3)


def extend_kind(site_kind, neighbours, win_kind_faces, win_kind_edges, start, tables):
    face_sites, out_rows, edge_sites, source = tables
    edge_len = len(edge_sites[0])
    square = edge_len * edge_len
    present, positions = window_rows(neighbours, start, win_kind_faces.shape[0])
    got_faces = jnp.take(win_kind_faces, positions[:, :6], axis=0)
    got_edges = jnp.take(win_kind_edges, positions[:, 6:], axis=0)
    parts = [site_kind]
    for face_num in range(6):
        facing = face_num ^ 1
        parts.append(jnp.where(present[:, face_num, None], got_faces[:, face_num, facing * square:(facing + 1) * square], 0))
    for edge_num in range(12):
        facing = edge_num ^ 1
        parts.append(jnp.where(present[:, 6 + edge_num, None], got_edges[:, edge_num, facing * edge_len:(facing + 1) * edge_len], 0))
    return jnp.concatenate(parts, axis=1)


def propagate(post_flow, post_bins, ext_flow, ext_bins, ext_kind, site_kind, tables):
    source = tables[3]
    interior = (site_kind == 1)[:, None, :]
    flow_rows = [post_flow[:, 0]]
    live_rows = []
    for pop_num in range(1, 19):
        source_live = jnp.take(ext_kind, source[pop_num], axis=1) > 0
        shifted = jnp.take(ext_flow[:, pop_num], source[pop_num], axis=1)
        flow_rows.append(jnp.where(source_live, shifted, post_flow[:, opposite[pop_num]]))
        live_rows.append(source_live)
    bin_rows = [post_bins[:, :, 0]]
    absorbed = jnp.zeros(post_bins.shape[:2], jnp.float32)
    for direction in range(1, 7):
        source_live = live_rows[direction - 1][:, None, :]
        shifted = jnp.take(ext_bins[:, :, direction], source[direction], axis=2)
        bin_rows.append(jnp.where(source_live, shifted, 0.0))
        leaving = post_bins[:, :, opposite[direction]]
        absorbed = absorbed + jnp.sum(jnp.where(interior & (~source_live), leaving, 0.0), axis=2)
    return jnp.stack(flow_rows, 1), jnp.stack(bin_rows, 2), absorbed


def boundary(flow_new, bins_new, flow_old, bins_old, site_kind, settle, inlet_conc):
    density, velocity = moments(flow_new)
    unit_density = jnp.ones_like(density)
    outlet_flow = flow_equilibrium(unit_density, velocity)
    concentration = jnp.sum(bins_new, axis=2)
    outlet_bins = bin_equilibrium(concentration, bin_drift(velocity, settle))
    at_rest = jnp.zeros_like(density)
    inlet_velocity = [at_rest, at_rest, at_rest + inlet_speed]
    inlet_flow = flow_equilibrium(unit_density, inlet_velocity)
    inlet_bins = bin_equilibrium(jnp.zeros_like(concentration) + inlet_conc[None, :, None], bin_drift(inlet_velocity, settle))
    flow_kind = site_kind[:, None, :]
    bin_kind = site_kind[:, None, None, :]
    flow_out = jnp.where(flow_kind == 2, inlet_flow, jnp.where(flow_kind == 3, outlet_flow, jnp.where(flow_kind == 1, flow_new, flow_old)))
    bins_out = jnp.where(bin_kind == 2, inlet_bins, jnp.where(bin_kind == 3, outlet_bins, jnp.where(bin_kind == 1, bins_new, bins_old)))
    return flow_out, bins_out


def reference(flow_pops, bin_pops, site_kind, neighbours, bin_rates, settle, inlet_conc):
    tables = site_tables(EDGE)
    flow_now = flow_pops
    bins_now = bin_pops.reshape(BLOCKS, BINS, 7, SITES)
    kind_faces, kind_edges = pack_kinds(site_kind, tables)
    ext_kind = extend_kind(site_kind, neighbours, kind_faces, kind_edges, 0, tables)
    deposit = jnp.zeros((BLOCKS, BINS), jnp.float32)
    for step_num in range(STEPS):
        post_flow, post_bins = collide(flow_now, bins_now, bin_rates, settle)
        faces, edges = pack_faces(post_flow, post_bins, tables)
        ext_flow, ext_bins = extend(post_flow, post_bins, neighbours, faces, edges, 0, tables)
        flow_new, bins_new, absorbed = propagate(post_flow, post_bins, ext_flow, ext_bins, ext_kind, site_kind, tables)
        deposit = deposit + absorbed
        flow_now, bins_now = boundary(flow_new, bins_new, flow_now, bins_now, site_kind, settle, inlet_conc)
    return flow_now, bins_now.reshape(BLOCKS, BINS * 7, SITES), deposit
```

```python
import functools

import jax
import jax.numpy as jnp
from jax import lax
from jax.experimental import pallas as pl
from jax.experimental.pallas import tpu as pltpu
from jax.sharding import PartitionSpec as P

VEL = [
    (0, 0, 0),
    (1, 0, 0),
    (-1, 0, 0),
    (0, 1, 0),
    (0, -1, 0),
    (0, 0, 1),
    (0, 0, -1),
    (1, 1, 0),
    (-1, -1, 0),
    (1, -1, 0),
    (-1, 1, 0),
    (1, 0, 1),
    (-1, 0, -1),
    (1, 0, -1),
    (-1, 0, 1),
    (0, 1, 1),
    (0, -1, -1),
    (0, 1, -1),
    (0, -1, 1),
]
WEIGHT = [1.0 / 3.0] + [1.0 / 18.0] * 6 + [1.0 / 36.0] * 12
OPP = [0, 2, 1, 4, 3, 6, 5, 8, 7, 10, 9, 12, 11, 14, 13, 16, 15, 18, 17]
OMEGA = 1.6
INLET = 0.04
BINS = 12
STEPS = 2
MESH = pl.DeviceIdType.MESH

FACE_POPS = [
    [q for q in range(1, 19) if VEL[q][d // 2] == 1 - 2 * (d % 2)] for d in range(6)
]
LIVE_SLOT = 5
BIN_SLOT = 6
PACKS = 3
LAT_ROWS, Z_ROWS = 4 * PACKS * 8, PACKS * 8


def lat_row(h):
    return 8 + LAT_ROWS * h


def z_row(way, h):
    return 8 + Z_ROWS * (2 * way + h)


def roll_lanes(x, shift):
    shift %= 128
    return x if shift == 0 else pltpu.roll(x, shift, 1)


def roll_rows(x, shift):
    shift %= 8
    return x if shift == 0 else pltpu.roll(x, shift, 0)


def kernel(
    layers,
    subs,
    flow_in,
    bins_in,
    kind_ref,
    near_ref,
    rates_ref,
    settle_ref,
    conc_ref,
    flow_out,
    bins_out,
    dep_ref,
    fbuf,
    gbuf,
    pf,
    pg,
    live_ref,
    dmask_ref,
    dacc,
    lat_0,
    lat_1,
    zwin_0,
    zwin_1,
    zsend,
    in_sem,
    out_sem,
    send_sem,
    recv_sem,
):
    lats, zwins = (lat_0, lat_1), (zwin_0, zwin_1)
    me = lax.axis_index("dom") * subs + lax.axis_index("sub")
    layer = me // 2
    half = me % 2
    has_up = layer < layers - 1
    has_down = layer > 0

    def device(g):
        return (g // subs, g % subs)

    mate = 2 * layer + 1 - half

    loads = [
        pltpu.make_async_copy(flow_in, fbuf, in_sem.at[0]),
        pltpu.make_async_copy(bins_in, gbuf, in_sem.at[1]),
    ]
    for copy in loads:
        copy.start()

    barrier = pltpu.get_barrier_semaphore()
    pl.semaphore_signal(barrier, inc=1, device_id=device(mate), device_id_type=MESH)

    @pl.when(has_up)
    def _():
        for h in range(2):
            pl.semaphore_signal(
                barrier, inc=1, device_id=device(2 * layer + 2 + h), device_id_type=MESH
            )

    @pl.when(has_down)
    def _():
        for h in range(2):
            pl.semaphore_signal(
                barrier, inc=1, device_id=device(2 * layer - 2 + h), device_id_type=MESH
            )

    sub = lax.broadcasted_iota(jnp.int32, (8, 128), 0)
    lane = lax.broadcasted_iota(jnp.int32, (8, 128), 1)
    jj = (lane >> 3) & 7
    kk = lane & 7
    low = lane < 64
    even = (sub & 1) == 0
    quarter = sub >> 1
    at = {
        (0, 0): (quarter == 0) & low,
        (0, 7): (quarter == 3) & (lane >= 64),
        (1, 0): jj == 0,
        (1, 7): jj == 7,
        (2, 0): kk == 0,
        (2, 7): kk == 7,
    }

    kind = kind_ref[...]
    alive = jnp.where(kind > 0, 1.0, 0.0)
    is_in = kind == 2
    is_out = kind == 3
    is_fluid = kind == 1

    def moments(f):
        rho = f[0]
        for q in range(1, 19):
            rho = rho + f[q]
        inv = 1.0 / rho
        vel = []
        for axis in range(3):
            plus = [f[q] for q in range(19) if VEL[q][axis] == 1]
            minus = [f[q] for q in range(19) if VEL[q][axis] == -1]
            vel.append((functools.reduce(jnp.add, plus) - functools.reduce(jnp.add, minus)) * inv)
        return rho, vel

    def equilibrium(scale, vel):
        base = 1.0 - 1.5 * (vel[0] * vel[0] + vel[1] * vel[1] + vel[2] * vel[2])
        scaled = {w: scale * w for w in set(WEIGHT)}
        out = [None] * 19
        out[0] = scaled[WEIGHT[0]] * base
        for q in range(1, 19, 2):
            along = None
            for axis in range(3):
                if VEL[q][axis] != 0:
                    term = vel[axis]
                    if along is None:
                        along = term if VEL[q][axis] > 0 else -term
                    else:
                        along = along + term if VEL[q][axis] > 0 else along - term
            even = base + 4.5 * along * along
            odd = 3.0 * along
            out[q] = scaled[WEIGHT[q]] * (even + odd)
            out[q + 1] = scaled[WEIGHT[q]] * (even - odd)
        return out

    def put(packs, d, slot, x):
        axis, minus = d // 2, d % 2
        v, m = slot // 8, slot % 8
        if axis == 0:
            t, h = m // 2, m % 2
            src_row, src_half = (0, 0) if minus else (3, 1)
            x = roll_rows(roll_lanes(x, 64 * (h - src_half)), 2 * (t - src_row))
            mask = (quarter == t) & (low if h == 0 else lane >= 64)
        else:
            src = 0 if minus else 7
            x = roll_lanes(x, (m - src) * (8 if axis == 1 else 1))
            mask = (jj if axis == 1 else kk) == m
        packs[v] = x if packs[v] is None else jnp.where(mask, x, packs[v])

    def gather(ref, row, stride, base, q):
        parts = []
        for b in range(2):
            w = jnp.clip(near_ref[b, q - 1] - base, 0, 3)
            parts.append(ref[pl.ds(row + stride * (w >> 1) + (w & 1) - b, 8), :])
        return jnp.where(even, parts[0], parts[1])

    def present(q):
        return jnp.where(even, near_ref[0, q - 1], near_ref[1, q - 1]) >= 0

    def x_shift(r, cx):
        if cx == 0:
            return r
        moved = roll_rows(r, 2 * cx)
        return jnp.where(low, moved, r) if cx > 0 else jnp.where(low, r, moved)

    def local(a, q):
        cx, cy, cz = VEL[q]
        return x_shift(roll_lanes(a, 64 * abs(cx) + 8 * cy + cz), cx)

    def unpack(d, slot, tile, q):
        cx, cy, cz = VEL[q]
        m = slot % 8
        plus = d % 2 == 0
        if d // 2 == 0:
            t, h = m // 2, m % 2
            to_row, to_half = (0, 0) if plus else (3, 1)
            return roll_rows(roll_lanes(tile, 64 * (to_half - h) + 8 * cy + cz), 2 * (to_row - t))
        to = 0 if plus else 7
        if d // 2 == 1:
            return x_shift(roll_lanes(tile, 64 * abs(cx) + 8 * (to - m) + cz), cx)
        return x_shift(roll_lanes(tile, 64 * abs(cx) + 8 * cy + to - m), cx)

    def unpack_edge(d, slot, tile, q):
        cx, cy, cz = VEL[q]
        m = slot % 8
        to = 0 if d % 2 == 0 else 7
        shift = 8 * (to - m) if d // 2 == 1 else to - m
        if cx != 0:
            return roll_rows(roll_lanes(tile, shift + 64), -6 * cx)
        return roll_lanes(tile, shift - 56 * cy)

    def face_of(axis, sign):
        return 2 * axis + (0 if sign > 0 else 1)

    def edge_face(q):
        axis = 2 if VEL[q][2] != 0 else 1
        return face_of(axis, VEL[q][axis])

    def lo(axis, sign):
        return at[(axis, 0 if sign > 0 else 7)]

    def stream(a, q, slot_of, face_tile, edge_tile):
        out = local(a, q)
        axes = [axis for axis in range(3) if VEL[q][axis] != 0]
        for axis in axes:
            d = face_of(axis, VEL[q][axis])
            slot = slot_of(d)
            out = jnp.where(
                lo(axis, VEL[q][axis]), unpack(d, slot, face_tile(d, slot // 8), q), out
            )
        if len(axes) == 2:
            d = edge_face(q)
            slot = slot_of(d)
            mask = lo(axes[0], VEL[q][axes[0]]) & lo(axes[1], VEL[q][axes[1]])
            out = jnp.where(mask, unpack_edge(d, slot, edge_tile(q), q), out)
        return out

    def copies(step):
        def mate_copy():
            span = pl.ds(lat_row(half), LAT_ROWS)
            return pltpu.make_async_remote_copy(
                src_ref=lats[step].at[span],
                dst_ref=lats[step].at[span],
                send_sem=send_sem.at[step, 0],
                recv_sem=recv_sem.at[step, 0],
                device_id=device(mate),
                device_id_type=MESH,
            )

        def mate_in():
            span = pl.ds(lat_row(1 - half), LAT_ROWS)
            return pltpu.make_async_remote_copy(
                src_ref=lats[step].at[span],
                dst_ref=lats[step].at[span],
                send_sem=send_sem.at[step, 0],
                recv_sem=recv_sem.at[step, 0],
                device_id=device(mate),
                device_id_type=MESH,
            )

        def z_copy(way, h):
            span = pl.ds(z_row(way, half), Z_ROWS)
            return pltpu.make_async_remote_copy(
                src_ref=zsend.at[step, way],
                dst_ref=zwins[step].at[span],
                send_sem=send_sem.at[step, 1 + 2 * way + h],
                recv_sem=recv_sem.at[step, 1 + 2 * way + half],
                device_id=device(2 * layer + (2 if way == 0 else -2) + h),
                device_id_type=MESH,
            )

        def z_in(way, h):
            return pltpu.make_async_remote_copy(
                src_ref=zsend.at[step, way],
                dst_ref=zwins[step].at[pl.ds(z_row(way, h), Z_ROWS)],
                send_sem=send_sem.at[step, 1 + 2 * way + h],
                recv_sem=recv_sem.at[step, 1 + 2 * way + h],
                device_id=device(2 * layer + (-2 if way == 0 else 2) + h),
                device_id_type=MESH,
            )

        return mate_copy, mate_in, z_copy, z_in

    loads[0].wait()

    for step in range(STEPS):
        first = step == 0
        mate_copy, mate_in, z_copy, z_in = copies(step)

        f = [fbuf[q] for q in range(19)]
        rho, vel = moments(f)
        target = equilibrium(OMEGA * rho, vel)
        for q in range(19):
            pf[q] = (1.0 - OMEGA) * f[q] + target[q]

        if first:
            loads[1].wait()

        x4, y4, z4 = [4.0 * u for u in vel]
        for n in range(BINS):
            rate = rates_ref[n]
            keep = 1.0 - rate
            g = [gbuf[7 * n + i] for i in range(7)]
            conc = functools.reduce(jnp.add, g)
            part = (0.125 * rate) * conc
            pg[7 * n] = keep * g[0] + (part + part)
            for axis, u4 in ((0, x4), (1, y4 - 4.0 * settle_ref[n]), (2, z4)):
                lean = part * u4
                pg[7 * n + 1 + 2 * axis] = keep * g[1 + 2 * axis] + (part + lean)
                pg[7 * n + 2 + 2 * axis] = keep * g[2 + 2 * axis] + (part - lean)

        def packed(d):
            packs = [None] * PACKS
            for s, q in enumerate(FACE_POPS[d]):
                put(packs, d, s, pf[q])
            put(packs, d, LIVE_SLOT, alive)
            for n in range(BINS):
                put(packs, d, BIN_SLOT + n, pg[7 * n + 1 + d])
            return packs

        for way in range(2):
            for v, tile in enumerate(packed(4 + way)):
                zsend[step, way, pl.ds(8 * v, 8), :] = tile

        if first:
            pl.semaphore_wait(barrier, 1 + 2 * jnp.where(has_up, 1, 0) + 2 * jnp.where(has_down, 1, 0))

        @pl.when(has_up)
        def _():
            for h in range(2):
                z_copy(0, h).start()

        @pl.when(has_down)
        def _():
            for h in range(2):
                z_copy(1, h).start()

        own = lat_row(half)
        for d in range(4):
            for v, tile in enumerate(packed(d)):
                lats[step][pl.ds(pl.multiple_of(own + 8 * (PACKS * d + v), 8), 8), :] = tile

        mate_copy().start()

        mate_in().wait_recv()

        @pl.when(has_down)
        def _():
            for h in range(2):
                z_in(0, h).wait_recv()

        @pl.when(has_up)
        def _():
            for h in range(2):
                z_in(1, h).wait_recv()

        memo = {}

        def tile_of(q, d, v):
            if (q, d, v) not in memo:
                if d >= 4:
                    base = 4 * layer + (-4 if d == 4 else 4)
                    tile = gather(zwins[step], z_row(d - 4, 0) + 8 * v, Z_ROWS, base, q)
                else:
                    row = lat_row(0) + 8 * (PACKS * d + v)
                    tile = gather(lats[step], row, LAT_ROWS, 4 * layer, q)
                if v == 0:
                    tile = jnp.where(present(q), tile, 0.0)
                memo[(q, d, v)] = tile
            return memo[(q, d, v)]

        def face_tile(d, v):
            return tile_of(OPP[1 + d], d, v)

        def edge_tile(q):
            return tile_of(OPP[q], edge_face(q), 0)

        if first:
            for q in range(1, 19):
                lq = stream(alive, q, lambda d: LIVE_SLOT, face_tile, edge_tile)
                live_ref[q - 1] = lq
                if q <= 6:
                    dmask_ref[q - 1] = jnp.where(is_fluid & (lq < 0.5), 1.0, 0.0)

        new = [pf[0]]
        for q in range(1, 19):
            moved = stream(pf[q], q, lambda d: FACE_POPS[d].index(q), face_tile, edge_tile)
            new.append(jnp.where(live_ref[q - 1] > 0.5, moved, pf[OPP[q]]))
        rho, vel = moments(new)
        base = equilibrium(jnp.ones_like(rho), vel)
        for q in range(19):
            inlet = WEIGHT[q] * (
                1.0
                + 3.0 * VEL[q][2] * INLET
                + 4.5 * (VEL[q][2] * INLET) ** 2
                - 1.5 * INLET * INLET
            )
            old = fbuf[q]
            fbuf[q] = jnp.where(
                is_fluid, new[q], jnp.where(is_out, base[q], jnp.where(is_in, inlet, old))
            )

        x4, y4, z4 = [4.0 * u for u in vel]
        for n in range(BINS):
            fall = 4.0 * settle_ref[n]
            level = conc_ref[n]
            new = [pg[7 * n]]
            absorbed = None
            for i in range(1, 7):
                moved = stream(pg[7 * n + i], i, lambda d: BIN_SLOT + n, face_tile, edge_tile)
                new.append(jnp.where(live_ref[i - 1] > 0.5, moved, 0.0))
                term = dmask_ref[i - 1] * pg[7 * n + OPP[i]]
                absorbed = term if absorbed is None else absorbed + term
            dacc[n] = absorbed if first else dacc[n] + absorbed
            conc = functools.reduce(jnp.add, new)
            part = 0.125 * conc
            outlet = [part + part]
            inlet = [0.25 * level]
            for u4, s4 in ((x4, 0.0), (y4 - fall, -fall), (z4, 4.0 * INLET)):
                lean = part * u4
                outlet += [part + lean, part - lean]
                inlet += [0.125 * level * (1.0 + s4), 0.125 * level * (1.0 - s4)]
            for i in range(7):
                old = gbuf[7 * n + i]
                gbuf[7 * n + i] = jnp.where(
                    is_fluid,
                    new[i],
                    jnp.where(is_out, outlet[i], jnp.where(is_in, inlet[i], old)),
                )

    stores = [
        pltpu.make_async_copy(fbuf, flow_out, out_sem.at[0]),
        pltpu.make_async_copy(gbuf, bins_out, out_sem.at[1]),
    ]
    for copy in stores:
        copy.start()

    table = jnp.zeros((8, 128), jnp.float32)
    for n in range(BINS):
        table = jnp.where(lane == n, jnp.sum(dacc[n], axis=1, keepdims=True), table)
    table = table + roll_rows(table, 2)
    table = table + roll_rows(table, 4)
    dep_ref[...] = table[:2, :BINS]

    for step in range(STEPS):
        mate_copy, mate_in, z_copy, z_in = copies(step)
        mate_copy().wait_send()

        @pl.when(has_up)
        def _():
            for h in range(2):
                z_copy(0, h).wait_send()

        @pl.when(has_down)
        def _():
            for h in range(2):
                z_copy(1, h).wait_send()

    for copy in stores:
        copy.wait()


def tiled(x):
    x = x.reshape(2, -1, 4, 128)
    return x.transpose(1, 2, 0, 3).reshape(-1, 8, 128)


def untiled(x):
    return x.reshape(-1, 4, 2, 128).transpose(2, 0, 1, 3).reshape(2, -1, 512)


def on_device(flow_pops, bin_pops, site_kind, neighbours, bin_rates, settle, inlet_conc):
    subs = lax.axis_size("sub")
    layers = lax.axis_size("dom") * subs // 2
    any_space = pl.BlockSpec(memory_space=pl.ANY)
    vmem = pl.BlockSpec(memory_space=pltpu.VMEM)
    smem = pl.BlockSpec(memory_space=pltpu.SMEM)
    f32 = jnp.float32
    flow, bins, deposit = pl.pallas_call(
        functools.partial(kernel, layers, subs),
        out_shape=(
            jax.ShapeDtypeStruct((19, 8, 128), f32),
            jax.ShapeDtypeStruct((7 * BINS, 8, 128), f32),
            jax.ShapeDtypeStruct((2, BINS), f32),
        ),
        in_specs=[any_space, any_space, vmem, smem, smem, smem, smem],
        out_specs=(any_space, any_space, vmem),
        scratch_shapes=[
            pltpu.VMEM((19, 8, 128), f32),
            pltpu.VMEM((7 * BINS, 8, 128), f32),
            pltpu.VMEM((19, 8, 128), f32),
            pltpu.VMEM((7 * BINS, 8, 128), f32),
            pltpu.VMEM((18, 8, 128), f32),
            pltpu.VMEM((6, 8, 128), f32),
            pltpu.VMEM((BINS, 8, 128), f32),
            pltpu.VMEM((lat_row(2) + 8, 128), f32),
            pltpu.VMEM((lat_row(2) + 8, 128), f32),
            pltpu.VMEM((z_row(2, 0) + 8, 128), f32),
            pltpu.VMEM((z_row(2, 0) + 8, 128), f32),
            pltpu.VMEM((STEPS, 2, Z_ROWS, 128), f32),
            pltpu.SemaphoreType.DMA((2,)),
            pltpu.SemaphoreType.DMA((2,)),
            pltpu.SemaphoreType.DMA((STEPS, 5)),
            pltpu.SemaphoreType.DMA((STEPS, 5)),
        ],
        compiler_params=pltpu.CompilerParams(
            collective_id=0, has_side_effects=True, vmem_limit_bytes=32 * 1024 * 1024
        ),
    )(
        tiled(flow_pops),
        tiled(bin_pops),
        tiled(site_kind)[0],
        neighbours,
        bin_rates,
        settle,
        inlet_conc,
    )
    return untiled(flow), untiled(bins), deposit


def solution(mesh):
    cut = ("dom", "sub")
    return jax.shard_map(
        on_device,
        mesh=mesh,
        in_specs=(P(cut, None, None), P(cut, None, None), P(cut, None), P(cut, None), P(), P(), P()),
        out_specs=(P(cut, None, None), P(cut, None, None), P(cut, None)),
        check_vma=False,
    )
```

```python
import functools

import jax
import jax.numpy as jnp
from jax import lax
from jax.experimental import pallas as pl
from jax.experimental.pallas import tpu as pltpu
from jax.sharding import PartitionSpec as P

VEL = [
    (0, 0, 0),
    (1, 0, 0),
    (-1, 0, 0),
    (0, 1, 0),
    (0, -1, 0),
    (0, 0, 1),
    (0, 0, -1),
    (1, 1, 0),
    (-1, -1, 0),
    (1, -1, 0),
    (-1, 1, 0),
    (1, 0, 1),
    (-1, 0, -1),
    (1, 0, -1),
    (-1, 0, 1),
    (0, 1, 1),
    (0, -1, -1),
    (0, 1, -1),
    (0, -1, 1),
]
WEIGHT = [1.0 / 3.0] + [1.0 / 18.0] * 6 + [1.0 / 36.0] * 12
OPP = [0, 2, 1, 4, 3, 6, 5, 8, 7, 10, 9, 12, 11, 14, 13, 16, 15, 18, 17]
OMEGA = 1.6
INLET = 0.04
BINS = 12
STEPS = 2
MESH = pl.DeviceIdType.MESH

FACE_POPS = [
    [q for q in range(1, 19) if VEL[q][d // 2] == 1 - 2 * (d % 2)] for d in range(6)
]
LIVE_SLOT = 5
BIN_SLOT = 6
PACKS = 3
LAT_ROWS, Z_ROWS = 4 * PACKS * 8, PACKS * 8


def lat_row(h):
    return 8 + LAT_ROWS * h


def z_row(way, h):
    return 8 + Z_ROWS * (2 * way + h)


def roll_lanes(x, shift):
    shift %= 128
    return x if shift == 0 else pltpu.roll(x, shift, 1)


def roll_rows(x, shift):
    shift %= 8
    return x if shift == 0 else pltpu.roll(x, shift, 0)


def kernel(
    layers,
    subs,
    flow_in,
    bins_in,
    kind_in,
    near_in,
    rates_in,
    settle_in,
    conc_in,
    fbuf,
    gbuf,
    dep_ref,
    kind_ref,
    near_ref,
    rates_ref,
    settle_ref,
    conc_ref,
    pf,
    pg,
    live_ref,
    dmask_ref,
    dacc,
    lat_0,
    lat_1,
    zwin_0,
    zwin_1,
    zsend,
    in_sem,
    send_sem,
    recv_sem,
):
    lats, zwins = (lat_0, lat_1), (zwin_0, zwin_1)
    me = lax.axis_index("dom") * subs + lax.axis_index("sub")
    layer = me // 2
    half = me % 2
    has_up = layer < layers - 1
    has_down = layer > 0

    def device(g):
        return (g // subs, g % subs)

    mate = 2 * layer + 1 - half

    pairs = [
        (flow_in, fbuf),
        (kind_in, kind_ref),
        (bins_in, gbuf),
        (rates_in, rates_ref),
        (settle_in, settle_ref),
        (conc_in, conc_ref),
        (near_in, near_ref),
    ]
    loads = [pltpu.make_async_copy(a, b, in_sem.at[n]) for n, (a, b) in enumerate(pairs)]
    for copy in loads:
        copy.start()

    barrier = pltpu.get_barrier_semaphore()
    pl.semaphore_signal(barrier, inc=1, device_id=device(mate), device_id_type=MESH)

    @pl.when(has_up)
    def _():
        for h in range(2):
            pl.semaphore_signal(
                barrier, inc=1, device_id=device(2 * layer + 2 + h), device_id_type=MESH
            )

    @pl.when(has_down)
    def _():
        for h in range(2):
            pl.semaphore_signal(
                barrier, inc=1, device_id=device(2 * layer - 2 + h), device_id_type=MESH
            )

    sub = lax.broadcasted_iota(jnp.int32, (8, 128), 0)
    lane = lax.broadcasted_iota(jnp.int32, (8, 128), 1)
    jj = (lane >> 3) & 7
    kk = lane & 7
    low = lane < 64
    even = (sub & 1) == 0
    quarter = sub >> 1
    at = {
        (0, 0): (quarter == 0) & low,
        (0, 7): (quarter == 3) & (lane >= 64),
        (1, 0): jj == 0,
        (1, 7): jj == 7,
        (2, 0): kk == 0,
        (2, 7): kk == 7,
    }

    loads[0].wait()
    loads[1].wait()
    kind = kind_ref[...]
    alive = jnp.where(kind > 0, 1.0, 0.0)
    is_in = kind == 2
    is_out = kind == 3
    is_fluid = kind == 1

    def moments(f):
        rho = f[0]
        for q in range(1, 19):
            rho = rho + f[q]
        inv = 1.0 / rho
        vel = []
        for axis in range(3):
            plus = [f[q] for q in range(19) if VEL[q][axis] == 1]
            minus = [f[q] for q in range(19) if VEL[q][axis] == -1]
            vel.append((functools.reduce(jnp.add, plus) - functools.reduce(jnp.add, minus)) * inv)
        return rho, vel

    def equilibrium(scale, vel):
        base = 1.0 - 1.5 * (vel[0] * vel[0] + vel[1] * vel[1] + vel[2] * vel[2])
        scaled = {w: scale * w for w in set(WEIGHT)}
        out = [None] * 19
        out[0] = scaled[WEIGHT[0]] * base
        for q in range(1, 19, 2):
            along = None
            for axis in range(3):
                if VEL[q][axis] != 0:
                    term = vel[axis]
                    if along is None:
                        along = term if VEL[q][axis] > 0 else -term
                    else:
                        along = along + term if VEL[q][axis] > 0 else along - term
            even = base + 4.5 * along * along
            odd = 3.0 * along
            out[q] = scaled[WEIGHT[q]] * (even + odd)
            out[q + 1] = scaled[WEIGHT[q]] * (even - odd)
        return out

    def put(packs, d, slot, x):
        axis, minus = d // 2, d % 2
        v, m = slot // 8, slot % 8
        if axis == 0:
            t, h = m // 2, m % 2
            src_row, src_half = (0, 0) if minus else (3, 1)
            x = roll_rows(roll_lanes(x, 64 * (h - src_half)), 2 * (t - src_row))
            mask = (quarter == t) & (low if h == 0 else lane >= 64)
        else:
            src = 0 if minus else 7
            x = roll_lanes(x, (m - src) * (8 if axis == 1 else 1))
            mask = (jj if axis == 1 else kk) == m
        packs[v] = x if packs[v] is None else jnp.where(mask, x, packs[v])

    def gather(ref, row, stride, base, q):
        parts = []
        for b in range(2):
            w = jnp.clip(near_ref[b, q - 1] - base, 0, 3)
            parts.append(ref[pl.ds(row + stride * (w >> 1) + (w & 1) - b, 8), :])
        return jnp.where(even, parts[0], parts[1])

    def present(q):
        return jnp.where(even, near_ref[0, q - 1], near_ref[1, q - 1]) >= 0

    def x_shift(r, cx):
        if cx == 0:
            return r
        moved = roll_rows(r, 2 * cx)
        return jnp.where(low, moved, r) if cx > 0 else jnp.where(low, r, moved)

    def local(a, q):
        cx, cy, cz = VEL[q]
        return x_shift(roll_lanes(a, 64 * abs(cx) + 8 * cy + cz), cx)

    def unpack(d, slot, tile, q):
        cx, cy, cz = VEL[q]
        m = slot % 8
        plus = d % 2 == 0
        if d // 2 == 0:
            t, h = m // 2, m % 2
            to_row, to_half = (0, 0) if plus else (3, 1)
            return roll_rows(roll_lanes(tile, 64 * (to_half - h) + 8 * cy + cz), 2 * (to_row - t))
        to = 0 if plus else 7
        if d // 2 == 1:
            return x_shift(roll_lanes(tile, 64 * abs(cx) + 8 * (to - m) + cz), cx)
        return x_shift(roll_lanes(tile, 64 * abs(cx) + 8 * cy + to - m), cx)

    def unpack_edge(d, slot, tile, q):
        cx, cy, cz = VEL[q]
        m = slot % 8
        to = 0 if d % 2 == 0 else 7
        shift = 8 * (to - m) if d // 2 == 1 else to - m
        if cx != 0:
            return roll_rows(roll_lanes(tile, shift + 64), -6 * cx)
        return roll_lanes(tile, shift - 56 * cy)

    def face_of(axis, sign):
        return 2 * axis + (0 if sign > 0 else 1)

    def edge_face(q):
        axis = 2 if VEL[q][2] != 0 else 1
        return face_of(axis, VEL[q][axis])

    def lo(axis, sign):
        return at[(axis, 0 if sign > 0 else 7)]

    def stream(a, q, slot_of, face_tile, edge_tile):
        out = local(a, q)
        axes = [axis for axis in range(3) if VEL[q][axis] != 0]
        for axis in axes:
            d = face_of(axis, VEL[q][axis])
            slot = slot_of(d)
            out = jnp.where(
                lo(axis, VEL[q][axis]), unpack(d, slot, face_tile(d, slot // 8), q), out
            )
        if len(axes) == 2:
            d = edge_face(q)
            slot = slot_of(d)
            mask = lo(axes[0], VEL[q][axes[0]]) & lo(axes[1], VEL[q][axes[1]])
            out = jnp.where(mask, unpack_edge(d, slot, edge_tile(q), q), out)
        return out

    def copies(step):
        def mate_copy():
            span = pl.ds(lat_row(half), LAT_ROWS)
            return pltpu.make_async_remote_copy(
                src_ref=lats[step].at[span],
                dst_ref=lats[step].at[span],
                send_sem=send_sem.at[step, 0],
                recv_sem=recv_sem.at[step, 0],
                device_id=device(mate),
                device_id_type=MESH,
            )

        def mate_in():
            span = pl.ds(lat_row(1 - half), LAT_ROWS)
            return pltpu.make_async_remote_copy(
                src_ref=lats[step].at[span],
                dst_ref=lats[step].at[span],
                send_sem=send_sem.at[step, 0],
                recv_sem=recv_sem.at[step, 0],
                device_id=device(mate),
                device_id_type=MESH,
            )

        def z_copy(way, h):
            span = pl.ds(z_row(way, half), Z_ROWS)
            return pltpu.make_async_remote_copy(
                src_ref=zsend.at[step, way],
                dst_ref=zwins[step].at[span],
                send_sem=send_sem.at[step, 1 + 2 * way + h],
                recv_sem=recv_sem.at[step, 1 + 2 * way + half],
                device_id=device(2 * layer + (2 if way == 0 else -2) + h),
                device_id_type=MESH,
            )

        def z_in(way, h):
            return pltpu.make_async_remote_copy(
                src_ref=zsend.at[step, way],
                dst_ref=zwins[step].at[pl.ds(z_row(way, h), Z_ROWS)],
                send_sem=send_sem.at[step, 1 + 2 * way + h],
                recv_sem=recv_sem.at[step, 1 + 2 * way + h],
                device_id=device(2 * layer + (-2 if way == 0 else 2) + h),
                device_id_type=MESH,
            )

        return mate_copy, mate_in, z_copy, z_in

    for step in range(STEPS):
        first = step == 0
        mate_copy, mate_in, z_copy, z_in = copies(step)

        f = [fbuf[q] for q in range(19)]
        rho, vel = moments(f)
        target = equilibrium(OMEGA * rho, vel)
        for q in range(19):
            pf[q] = (1.0 - OMEGA) * f[q] + target[q]

        if first:
            for copy in loads[2:]:
                copy.wait()

        x4, y4, z4 = [4.0 * u for u in vel]
        for n in range(BINS):
            rate = rates_ref[n]
            keep = 1.0 - rate
            g = [gbuf[7 * n + i] for i in range(7)]
            conc = functools.reduce(jnp.add, g)
            part = (0.125 * rate) * conc
            pg[7 * n] = keep * g[0] + (part + part)
            for axis, u4 in ((0, x4), (1, y4 - 4.0 * settle_ref[n]), (2, z4)):
                lean = part * u4
                pg[7 * n + 1 + 2 * axis] = keep * g[1 + 2 * axis] + (part + lean)
                pg[7 * n + 2 + 2 * axis] = keep * g[2 + 2 * axis] + (part - lean)

        def packed(d):
            packs = [None] * PACKS
            for s, q in enumerate(FACE_POPS[d]):
                put(packs, d, s, pf[q])
            put(packs, d, LIVE_SLOT, alive)
            for n in range(BINS):
                put(packs, d, BIN_SLOT + n, pg[7 * n + 1 + d])
            return packs

        for way in range(2):
            for v, tile in enumerate(packed(4 + way)):
                zsend[step, way, pl.ds(8 * v, 8), :] = tile

        if first:
            pl.semaphore_wait(barrier, 1 + 2 * jnp.where(has_up, 1, 0) + 2 * jnp.where(has_down, 1, 0))

        @pl.when(has_up)
        def _():
            for h in range(2):
                z_copy(0, h).start()

        @pl.when(has_down)
        def _():
            for h in range(2):
                z_copy(1, h).start()

        own = lat_row(half)
        for d in range(4):
            for v, tile in enumerate(packed(d)):
                lats[step][pl.ds(pl.multiple_of(own + 8 * (PACKS * d + v), 8), 8), :] = tile

        mate_copy().start()

        mate_in().wait_recv()

        @pl.when(has_down)
        def _():
            for h in range(2):
                z_in(0, h).wait_recv()

        @pl.when(has_up)
        def _():
            for h in range(2):
                z_in(1, h).wait_recv()

        memo = {}

        def tile_of(q, d, v):
            if (q, d, v) not in memo:
                if d >= 4:
                    base = 4 * layer + (-4 if d == 4 else 4)
                    tile = gather(zwins[step], z_row(d - 4, 0) + 8 * v, Z_ROWS, base, q)
                else:
                    row = lat_row(0) + 8 * (PACKS * d + v)
                    tile = gather(lats[step], row, LAT_ROWS, 4 * layer, q)
                if v == 0:
                    tile = jnp.where(present(q), tile, 0.0)
                memo[(q, d, v)] = tile
            return memo[(q, d, v)]

        def face_tile(d, v):
            return tile_of(OPP[1 + d], d, v)

        def edge_tile(q):
            return tile_of(OPP[q], edge_face(q), 0)

        if first:
            for q in range(1, 19):
                lq = stream(alive, q, lambda d: LIVE_SLOT, face_tile, edge_tile)
                live_ref[q - 1] = lq
                if q <= 6:
                    dmask_ref[q - 1] = jnp.where(is_fluid & (lq < 0.5), 1.0, 0.0)

        new = [pf[0]]
        for q in range(1, 19):
            moved = stream(pf[q], q, lambda d: FACE_POPS[d].index(q), face_tile, edge_tile)
            new.append(jnp.where(live_ref[q - 1] > 0.5, moved, pf[OPP[q]]))
        rho, vel = moments(new)
        base = equilibrium(jnp.ones_like(rho), vel)
        for q in range(19):
            inlet = WEIGHT[q] * (
                1.0
                + 3.0 * VEL[q][2] * INLET
                + 4.5 * (VEL[q][2] * INLET) ** 2
                - 1.5 * INLET * INLET
            )
            old = fbuf[q]
            fbuf[q] = jnp.where(
                is_fluid, new[q], jnp.where(is_out, base[q], jnp.where(is_in, inlet, old))
            )

        x4, y4, z4 = [4.0 * u for u in vel]
        for n in range(BINS):
            fall = 4.0 * settle_ref[n]
            level = conc_ref[n]
            new = [pg[7 * n]]
            absorbed = None
            for i in range(1, 7):
                moved = stream(pg[7 * n + i], i, lambda d: BIN_SLOT + n, face_tile, edge_tile)
                new.append(jnp.where(live_ref[i - 1] > 0.5, moved, 0.0))
                term = dmask_ref[i - 1] * pg[7 * n + OPP[i]]
                absorbed = term if absorbed is None else absorbed + term
            dacc[n] = absorbed if first else dacc[n] + absorbed
            conc = functools.reduce(jnp.add, new)
            part = 0.125 * conc
            outlet = [part + part]
            inlet = [0.25 * level]
            for u4, s4 in ((x4, 0.0), (y4 - fall, -fall), (z4, 4.0 * INLET)):
                lean = part * u4
                outlet += [part + lean, part - lean]
                inlet += [0.125 * level * (1.0 + s4), 0.125 * level * (1.0 - s4)]
            for i in range(7):
                old = gbuf[7 * n + i]
                gbuf[7 * n + i] = jnp.where(
                    is_fluid,
                    new[i],
                    jnp.where(is_out, outlet[i], jnp.where(is_in, inlet[i], old)),
                )

    table = jnp.zeros((8, 128), jnp.float32)
    for n in range(BINS):
        table = jnp.where(lane == n, jnp.sum(dacc[n], axis=1, keepdims=True), table)
    table = table + roll_rows(table, 2)
    table = table + roll_rows(table, 4)
    dep_ref[...] = table[:2, :BINS]

    for step in range(STEPS):
        mate_copy, mate_in, z_copy, z_in = copies(step)
        mate_copy().wait_send()

        @pl.when(has_up)
        def _():
            for h in range(2):
                z_copy(0, h).wait_send()

        @pl.when(has_down)
        def _():
            for h in range(2):
                z_copy(1, h).wait_send()


def write_out(flow, bins, deposit, flow_out, bins_out, dep_out, sem):
    pairs = [(bins, bins_out), (flow, flow_out), (deposit, dep_out)]
    copies = [pltpu.make_async_copy(a, b, sem.at[n]) for n, (a, b) in enumerate(pairs)]
    for copy in copies:
        copy.start()
    for copy in copies:
        copy.wait()


def tiled(x):
    x = x.reshape(2, -1, 4, 128)
    return x.transpose(1, 2, 0, 3).reshape(-1, 8, 128)


def untiled(x):
    return x.reshape(-1, 4, 2, 128).transpose(2, 0, 1, 3).reshape(2, -1, 512)


def on_device(flow_pops, bin_pops, site_kind, neighbours, bin_rates, settle, inlet_conc):
    subs = lax.axis_size("sub")
    layers = lax.axis_size("dom") * subs // 2
    hbm = pl.BlockSpec(memory_space=pltpu.HBM)
    vmem = pl.BlockSpec(memory_space=pltpu.VMEM)
    f32 = jnp.float32
    shapes = (
        jax.ShapeDtypeStruct((19, 8, 128), f32),
        jax.ShapeDtypeStruct((7 * BINS, 8, 128), f32),
        jax.ShapeDtypeStruct((2, BINS), f32),
    )
    done = pl.pallas_call(
        functools.partial(kernel, layers, subs),
        out_shape=shapes,
        in_specs=[hbm] * 7,
        out_specs=(vmem, vmem, vmem),
        scratch_shapes=[
            pltpu.VMEM((8, 128), jnp.int32),
            pltpu.SMEM((2, 18), jnp.int32),
            pltpu.SMEM((BINS,), f32),
            pltpu.SMEM((BINS,), f32),
            pltpu.SMEM((BINS,), f32),
            pltpu.VMEM((19, 8, 128), f32),
            pltpu.VMEM((7 * BINS, 8, 128), f32),
            pltpu.VMEM((18, 8, 128), f32),
            pltpu.VMEM((6, 8, 128), f32),
            pltpu.VMEM((BINS, 8, 128), f32),
            pltpu.VMEM((lat_row(2) + 8, 128), f32),
            pltpu.VMEM((lat_row(2) + 8, 128), f32),
            pltpu.VMEM((z_row(2, 0) + 8, 128), f32),
            pltpu.VMEM((z_row(2, 0) + 8, 128), f32),
            pltpu.VMEM((STEPS, 2, Z_ROWS, 128), f32),
            pltpu.SemaphoreType.DMA((7,)),
            pltpu.SemaphoreType.DMA((STEPS, 5)),
            pltpu.SemaphoreType.DMA((STEPS, 5)),
        ],
        compiler_params=pltpu.CompilerParams(
            collective_id=0, has_side_effects=True, vmem_limit_bytes=16 * 1024 * 1024
        ),
    )(
        *[
            pltpu.with_memory_space_constraint(x, pltpu.HBM)
            for x in (
                tiled(flow_pops),
                tiled(bin_pops),
                tiled(site_kind)[0],
                neighbours,
                bin_rates,
                settle,
                inlet_conc,
            )
        ]
    )
    flow, bins, deposit = pl.pallas_call(
        write_out,
        out_shape=shapes,
        in_specs=[vmem, vmem, vmem],
        out_specs=(hbm, hbm, hbm),
        scratch_shapes=[pltpu.SemaphoreType.DMA((3,))],
        compiler_params=pltpu.CompilerParams(vmem_limit_bytes=16 * 1024 * 1024),
    )(*done)
    return untiled(flow), untiled(bins), deposit


def solution(mesh):
    cut = ("dom", "sub")
    return jax.shard_map(
        on_device,
        mesh=mesh,
        in_specs=(P(cut, None, None), P(cut, None, None), P(cut, None), P(cut, None), P(), P(), P()),
        out_specs=(P(cut, None, None), P(cut, None, None), P(cut, None)),
        check_vma=False,
    )
```

```python
import functools

import jax
import jax.numpy as jnp
from jax import lax
from jax.experimental import pallas as pl
from jax.experimental.pallas import tpu as pltpu
from jax.sharding import PartitionSpec as P

VEL = [
    (0, 0, 0),
    (1, 0, 0),
    (-1, 0, 0),
    (0, 1, 0),
    (0, -1, 0),
    (0, 0, 1),
    (0, 0, -1),
    (1, 1, 0),
    (-1, -1, 0),
    (1, -1, 0),
    (-1, 1, 0),
    (1, 0, 1),
    (-1, 0, -1),
    (1, 0, -1),
    (-1, 0, 1),
    (0, 1, 1),
    (0, -1, -1),
    (0, 1, -1),
    (0, -1, 1),
]
WEIGHT = [1.0 / 3.0] + [1.0 / 18.0] * 6 + [1.0 / 36.0] * 12
OPP = [0, 2, 1, 4, 3, 6, 5, 8, 7, 10, 9, 12, 11, 14, 13, 16, 15, 18, 17]
OMEGA = 1.6
INLET = 0.04
BINS = 12
MESH = pl.DeviceIdType.MESH

FACE_POPS = [
    [q for q in range(1, 19) if VEL[q][d // 2] == 1 - 2 * (d % 2)] for d in range(6)
]
LIVE_SLOT = 5
BIN_SLOT = 6
PACKS = 3
PART = 5
LAT_ROWS, Z_ROWS, PART_ROWS = 2 * PACKS * 8, PACKS * 8, PART * 8
LATERAL = [(0, 0), (1, 0), (-1, 0), (0, 1), (0, -1)]


def lat_row(h):
    return 8 + LAT_ROWS * h


def own_row(h, way):
    return 8 + Z_ROWS * (2 * h + way)


def z_row(way, h):
    return 8 + Z_ROWS * (2 * way + h)


def part_row(way, h):
    return 8 + PART_ROWS * (2 * way + h)


def slot_at(d, lateral):
    return [VEL[q][:2] for q in FACE_POPS[d]].index(lateral)


def roll_lanes(x, shift):
    shift %= 128
    return x if shift == 0 else pltpu.roll(x, shift, 1)


def roll_rows(x, shift):
    shift %= 8
    return x if shift == 0 else pltpu.roll(x, shift, 0)


def kernel(
    layers,
    subs,
    flow_in,
    bins_in,
    kind_in,
    near_in,
    rates_in,
    settle_in,
    conc_in,
    fbuf,
    gbuf,
    dep_ref,
    kind_ref,
    near_ref,
    rates_ref,
    settle_ref,
    conc_ref,
    pf,
    pg,
    sf,
    sg,
    live_ref,
    dmask_ref,
    dacc,
    lat_0,
    lat_1,
    own_z,
    zwin,
    pwin,
    psend,
    ghost,
    in_sem,
    send_sem,
    recv_sem,
    mate_send,
    mate_recv,
):
    lats = (lat_0, lat_1)
    me = lax.axis_index("dom") * subs + lax.axis_index("sub")
    layer = me // 2
    half = me % 2
    mate = 2 * layer + 1 - half
    far = 1 - (me % subs) // 2

    def device(g):
        return (g // subs, g % subs)

    def beyond(way):
        return layer + 1 - 2 * way

    def each_way(do):
        for way in (far, 1 - far):
            there = beyond(way)
            pl.when((there >= 0) & (there < layers))(functools.partial(do, way))

    barrier = pltpu.get_barrier_semaphore()

    def greet(way):
        for h in range(2):
            pl.semaphore_signal(
                barrier, inc=1, device_id=device(2 * beyond(way) + h), device_id_type=MESH
            )

    each_way(greet)
    pl.semaphore_signal(barrier, inc=1, device_id=device(mate), device_id_type=MESH)

    pairs = [
        (flow_in, fbuf),
        (kind_in, kind_ref),
        (bins_in, gbuf),
        (rates_in, rates_ref),
        (settle_in, settle_ref),
        (conc_in, conc_ref),
        (near_in, near_ref),
    ]
    loads = [pltpu.make_async_copy(a, b, in_sem.at[n]) for n, (a, b) in enumerate(pairs)]
    for copy in loads:
        copy.start()

    sub = lax.broadcasted_iota(jnp.int32, (8, 128), 0)
    lane = lax.broadcasted_iota(jnp.int32, (8, 128), 1)
    jj = (lane >> 3) & 7
    kk = lane & 7
    low = lane < 64
    even = (sub & 1) == 0
    quarter = sub >> 1
    at = {
        (0, 0): (quarter == 0) & low,
        (0, 7): (quarter == 3) & (lane >= 64),
        (1, 0): jj == 0,
        (1, 7): jj == 7,
        (2, 0): kk == 0,
        (2, 7): kk == 7,
    }

    loads[0].wait()
    loads[1].wait()
    kind = kind_ref[...]
    alive = jnp.where(kind > 0, 1.0, 0.0)
    is_in = kind == 2
    is_out = kind == 3
    is_fluid = kind == 1

    def moments(f):
        rho = f[0]
        for q in range(1, 19):
            rho = rho + f[q]
        inv = 1.0 / rho
        vel = []
        for axis in range(3):
            plus = [f[q] for q in range(19) if VEL[q][axis] == 1]
            minus = [f[q] for q in range(19) if VEL[q][axis] == -1]
            vel.append((functools.reduce(jnp.add, plus) - functools.reduce(jnp.add, minus)) * inv)
        return rho, vel

    def equilibrium(scale, vel):
        base = 1.0 - 1.5 * (vel[0] * vel[0] + vel[1] * vel[1] + vel[2] * vel[2])
        scaled = {w: scale * w for w in set(WEIGHT)}
        out = [None] * 19
        out[0] = scaled[WEIGHT[0]] * base
        for q in range(1, 19, 2):
            along = None
            for axis in range(3):
                if VEL[q][axis] != 0:
                    term = vel[axis]
                    if along is None:
                        along = term if VEL[q][axis] > 0 else -term
                    else:
                        along = along + term if VEL[q][axis] > 0 else along - term
            even = base + 4.5 * along * along
            odd = 3.0 * along
            out[q] = scaled[WEIGHT[q]] * (even + odd)
            out[q + 1] = scaled[WEIGHT[q]] * (even - odd)
        return out

    def put(packs, d, slot, x):
        axis, minus = d // 2, d % 2
        v, m = slot // 8, slot % 8
        if axis == 0:
            t, h = m // 2, m % 2
            src_row, src_half = (0, 0) if minus else (3, 1)
            x = roll_rows(roll_lanes(x, 64 * (h - src_half)), 2 * (t - src_row))
            mask = (quarter == t) & (low if h == 0 else lane >= 64)
        else:
            src = 0 if minus else 7
            x = roll_lanes(x, (m - src) * (8 if axis == 1 else 1))
            mask = (jj if axis == 1 else kk) == m
        packs[v] = x if packs[v] is None else jnp.where(mask, x, packs[v])

    def gather(ref, row, stride, blocks):
        parts = [
            ref[pl.ds(row + stride * (w >> 1) + (w & 1) - b, 8), :] for b, w in enumerate(blocks)
        ]
        return jnp.where(even, parts[0], parts[1])

    def nearby(q, base):
        return [jnp.clip(near_ref[b, q - 1] - base, 0, 3) for b in range(2)]

    def present(q):
        return jnp.where(even, near_ref[0, q - 1], near_ref[1, q - 1]) >= 0

    def x_shift(r, cx):
        if cx == 0:
            return r
        moved = roll_rows(r, 2 * cx)
        return jnp.where(low, moved, r) if cx > 0 else jnp.where(low, r, moved)

    def local(a, q):
        cx, cy, cz = VEL[q]
        return x_shift(roll_lanes(a, 64 * abs(cx) + 8 * cy + cz), cx)

    def unpack(d, slot, tile, q):
        cx, cy, cz = VEL[q]
        m = slot % 8
        plus = d % 2 == 0
        if d // 2 == 0:
            t, h = m // 2, m % 2
            to_row, to_half = (0, 0) if plus else (3, 1)
            return roll_rows(roll_lanes(tile, 64 * (to_half - h) + 8 * cy + cz), 2 * (to_row - t))
        to = 0 if plus else 7
        if d // 2 == 1:
            return x_shift(roll_lanes(tile, 64 * abs(cx) + 8 * (to - m) + cz), cx)
        return x_shift(roll_lanes(tile, 64 * abs(cx) + 8 * cy + to - m), cx)

    def unpack_edge(d, slot, tile, q):
        cx, cy, cz = VEL[q]
        m = slot % 8
        to = 0 if d % 2 == 0 else 7
        shift = 8 * (to - m) if d // 2 == 1 else to - m
        if cx != 0:
            return roll_rows(roll_lanes(tile, shift + 64), -6 * cx)
        return roll_lanes(tile, shift - 56 * cy)

    def face_of(axis, sign):
        return 2 * axis + (0 if sign > 0 else 1)

    def edge_face(q):
        axis = 2 if VEL[q][2] != 0 else 1
        return face_of(axis, VEL[q][axis])

    def lo(axis, sign):
        return at[(axis, 0 if sign > 0 else 7)]

    def stream(a, q, slot_of, face_tile, edge_tile):
        out = local(a, q)
        axes = [axis for axis in range(3) if VEL[q][axis] != 0]
        for axis in axes:
            d = face_of(axis, VEL[q][axis])
            slot = slot_of(d)
            out = jnp.where(
                lo(axis, VEL[q][axis]), unpack(d, slot, face_tile(d, slot // 8), q), out
            )
        if len(axes) == 2:
            d = edge_face(q)
            slot = slot_of(d)
            mask = lo(axes[0], VEL[q][axes[0]]) & lo(axes[1], VEL[q][axes[1]])
            out = jnp.where(mask, unpack_edge(d, slot, edge_tile(q), q), out)
        return out

    def mate_copy(n, ref, row, rows, h):
        span = pl.ds(row(h), rows)
        return pltpu.make_async_remote_copy(
            src_ref=ref.at[span],
            dst_ref=ref.at[span],
            send_sem=mate_send.at[n],
            recv_sem=mate_recv.at[n],
            device_id=device(mate),
            device_id_type=MESH,
        )

    def mate_copies(h):
        return (
            mate_copy(0, lat_0, lat_row, LAT_ROWS, h),
            mate_copy(1, own_z, lambda h: own_row(h, 0), 2 * Z_ROWS, h),
            mate_copy(2, lat_1, lat_row, LAT_ROWS, h),
        )

    def z_copy(n, way, h):
        src = (own_z.at[pl.ds(own_row(half, way), Z_ROWS)], psend.at[way])[n]
        dst = (
            zwin.at[pl.ds(z_row(way, half), Z_ROWS)],
            pwin.at[pl.ds(part_row(way, half), PART_ROWS)],
        )[n]
        return pltpu.make_async_remote_copy(
            src_ref=src,
            dst_ref=dst,
            send_sem=send_sem.at[n, 2 * way + h],
            recv_sem=recv_sem.at[n, 2 * way + half],
            device_id=device(2 * beyond(way) + h),
            device_id_type=MESH,
        )

    def z_in(n, way, h):
        src = (own_z.at[pl.ds(own_row(half, way), Z_ROWS)], psend.at[way])[n]
        dst = (
            zwin.at[pl.ds(z_row(way, h), Z_ROWS)],
            pwin.at[pl.ds(part_row(way, h), PART_ROWS)],
        )[n]
        return pltpu.make_async_remote_copy(
            src_ref=src,
            dst_ref=dst,
            send_sem=send_sem.at[n, 2 * way + h],
            recv_sem=recv_sem.at[n, 2 * way + h],
            device_id=device(2 * beyond(1 - way) + h),
            device_id_type=MESH,
        )

    def send_z(n):
        def do(way):
            for h in range(2):
                z_copy(n, way, h).start()

        each_way(do)

    def receive_z(n):
        def do(way):
            for h in range(2):
                z_in(n, 1 - way, h).wait_recv()

        each_way(do)

    def collide(first):
        f = [fbuf[q] for q in range(19)]
        rho, vel = moments(f)
        target = equilibrium(OMEGA * rho, vel)
        for q in range(19):
            pf[q] = (1.0 - OMEGA) * f[q] + target[q]
        if first:
            for copy in loads[2:]:
                copy.wait()
        x4, y4, z4 = [4.0 * u for u in vel]
        for n in range(BINS):
            rate = rates_ref[n]
            keep = 1.0 - rate
            g = [gbuf[7 * n + i] for i in range(7)]
            conc = functools.reduce(jnp.add, g)
            part = (0.125 * rate) * conc
            pg[7 * n] = keep * g[0] + (part + part)
            for axis, u4 in ((0, x4), (1, y4 - 4.0 * settle_ref[n]), (2, z4)):
                lean = part * u4
                pg[7 * n + 1 + 2 * axis] = keep * g[1 + 2 * axis] + (part + lean)
                pg[7 * n + 2 + 2 * axis] = keep * g[2 + 2 * axis] + (part - lean)

    def pack_z(way):
        d = 4 + way
        packs = [None] * PACKS
        for s, q in enumerate(FACE_POPS[d]):
            put(packs, d, s, pf[q])
        put(packs, d, LIVE_SLOT, alive)
        for n in range(BINS):
            put(packs, d, BIN_SLOT + n, pg[7 * n + 1 + d])
        for v, tile in enumerate(packs):
            own_z[pl.ds(pl.multiple_of(own_row(half, way) + 8 * v, 8), 8), :] = tile

    def pack_lateral(ref):
        for axis in range(2):
            sides = []
            for d in (2 * axis, 2 * axis + 1):
                packs = [None] * PACKS
                for s, q in enumerate(FACE_POPS[d]):
                    put(packs, d, s, pf[q])
                put(packs, d, LIVE_SLOT, alive)
                for n in range(BINS):
                    put(packs, d, BIN_SLOT + n, pg[7 * n + 1 + d])
                sides.append(packs)
            ahead = present(1 + 2 * axis)
            row = lat_row(half) + 8 * PACKS * axis
            for v in range(PACKS):
                ref[pl.ds(pl.multiple_of(row + 8 * v, 8), 8), :] = jnp.where(
                    ahead, sides[0][v], sides[1][v]
                )

    def absent_as_zero(q, v, tile):
        return jnp.where(present(q), tile, 0.0) if v == 0 else tile

    def windows(lat, z_tile):
        memo = {}

        def tile_of(q, d, v):
            if (q, d, v) not in memo:
                if d >= 4:
                    tile = z_tile(q, d - 4, v)
                else:
                    row = lat_row(0) + 8 * (PACKS * (d // 2) + v)
                    tile = gather(lat, row, LAT_ROWS, nearby(q, 4 * layer))
                memo[(q, d, v)] = absent_as_zero(q, v, tile)
            return memo[(q, d, v)]

        return (
            lambda d, v: tile_of(OPP[1 + d], d, v),
            lambda q: tile_of(OPP[q], edge_face(q), 0),
        )

    def flow_slot(q):
        return lambda d: FACE_POPS[d].index(q)

    def bin_slot(n):
        return lambda d: BIN_SLOT + n

    def live_slot(d):
        return LIVE_SLOT

    def absorb(first):
        for n in range(BINS):
            terms = [dmask_ref[i - 1] * pg[7 * n + OPP[i]] for i in range(1, 7)]
            total = functools.reduce(jnp.add, terms)
            dacc[n] = total if first else dacc[n] + total

    def settle_flow(new):
        rho, vel = moments(new)
        base = equilibrium(jnp.ones_like(rho), vel)
        for q in range(19):
            inlet = WEIGHT[q] * (
                1.0
                + 3.0 * VEL[q][2] * INLET
                + 4.5 * (VEL[q][2] * INLET) ** 2
                - 1.5 * INLET * INLET
            )
            old = fbuf[q]
            fbuf[q] = jnp.where(
                is_fluid, new[q], jnp.where(is_out, base[q], jnp.where(is_in, inlet, old))
            )
        return [4.0 * u for u in vel]

    def settle_bins(n, new, x4, y4, z4):
        fall = 4.0 * settle_ref[n]
        level = conc_ref[n]
        part = 0.125 * functools.reduce(jnp.add, new)
        outlet = [part + part]
        inlet = [0.25 * level]
        for u4, s4 in ((x4, 0.0), (y4 - fall, -fall), (z4, 4.0 * INLET)):
            lean = part * u4
            outlet += [part + lean, part - lean]
            inlet += [0.125 * level * (1.0 + s4), 0.125 * level * (1.0 - s4)]
        for i in range(7):
            old = gbuf[7 * n + i]
            gbuf[7 * n + i] = jnp.where(
                is_fluid, new[i], jnp.where(is_out, outlet[i], jnp.where(is_in, inlet[i], old))
            )

    collide(True)
    for way in range(2):
        pack_z(way)
    ends = jnp.where(layer < layers - 1, 1, 0) + jnp.where(layer > 0, 1, 0)
    pl.semaphore_wait(barrier, 1 + 2 * ends)
    send_z(0)
    pack_lateral(lat_0)
    out_1, out_z, out_2 = mate_copies(half)
    in_1, in_z, in_2 = mate_copies(1 - half)
    out_1.start()
    out_z.start()

    def z_tile(q, way, v):
        base = 4 * layer + (-4 if way == 0 else 4)
        return gather(zwin, z_row(way, 0) + 8 * v, Z_ROWS, nearby(q, base))

    in_1.wait_recv()
    face_tile, edge_tile = windows(lat_0, z_tile)

    def within(a, q, slot_of):
        out = local(a, q)
        axes = [axis for axis in range(2) if VEL[q][axis] != 0]
        for axis in axes:
            d = face_of(axis, VEL[q][axis])
            moved = unpack(d, slot_of(d), face_tile(d, slot_of(d) // 8), q)
            out = jnp.where(lo(axis, VEL[q][axis]), moved, out)
        if len(axes) == 2:
            d = edge_face(q)
            mask = lo(0, VEL[q][0]) & lo(1, VEL[q][1])
            out = jnp.where(mask, unpack_edge(d, slot_of(d), edge_tile(q), q), out)
        return out

    def across(a, q, slot_of):
        cx, cy, cz = VEL[q]
        if cz == 0:
            return a
        d = face_of(2, cz)
        slot = slot_of(d)
        moved = unpack(d, slot, face_tile(d, slot // 8), q)
        for axis in range(2):
            if VEL[q][axis] != 0:
                moved = jnp.where(
                    lo(axis, VEL[q][axis]), unpack_edge(d, slot, edge_tile(q), q), moved
                )
        return jnp.where(lo(2, cz), moved, a)

    flow = [pf[0]]
    for q in range(1, 19):
        lq = within(alive, q, live_slot)
        live_ref[q - 1] = lq
        flow.append(jnp.where(lq > 0.5, within(pf[q], q, flow_slot(q)), pf[OPP[q]]))
        sf[q] = flow[q]

    def total(rows, pick):
        return functools.reduce(jnp.add, [rows[q] for q in range(len(rows)) if pick(VEL[q])])

    level_sum = [
        total(flow, lambda c: c[2] == 0),
        total(flow, lambda c: c[0] == 1 and c[2] == 0)
        - total(flow, lambda c: c[0] == -1 and c[2] == 0),
        total(flow, lambda c: c[1] == 1 and c[2] == 0)
        - total(flow, lambda c: c[1] == -1 and c[2] == 0),
    ]
    parts = [[None] * PART for way in range(2)]

    def put_part(way, tile, m, x):
        packs = [None] * PART
        packs[tile] = parts[way][tile]
        put(packs, 4 + way, 8 * tile + m, x)
        parts[way][tile] = packs[tile]

    for way in range(2):
        sign = 1 - 2 * way
        rows = FACE_POPS[4 + way]
        for s, q in enumerate(rows):
            put_part(way, 0, s, flow[q])
        put_part(way, 0, LIVE_SLOT, level_sum[0] + functools.reduce(jnp.add, [flow[q] for q in rows]))
        x_sum = flow[rows[slot_at(4 + way, (1, 0))]] - flow[rows[slot_at(4 + way, (-1, 0))]]
        y_sum = flow[rows[slot_at(4 + way, (0, 1))]] - flow[rows[slot_at(4 + way, (0, -1))]]
        put_part(way, 3, 2, level_sum[1] + x_sum)
        put_part(way, 3, 3, level_sum[2] + y_sum)
    for n in range(BINS):
        g = [pg[7 * n]]
        for i in range(1, 7):
            moved = within(pg[7 * n + i], i, bin_slot(n))
            g.append(jnp.where(live_ref[i - 1] > 0.5, moved, 0.0))
            sg[6 * n + i - 1] = g[i]
        flat = functools.reduce(jnp.add, g[:5])
        v, m = (BIN_SLOT + n) // 8, (BIN_SLOT + n) % 8
        for way in range(2):
            put_part(way, v, m, g[5 + way])
            put_part(way, 4 if v == 1 else 3, m, flat + g[5 + way])
    for way in range(2):
        for v in range(PART):
            psend[way, pl.ds(8 * v, 8), :] = parts[way][v]
    send_z(1)

    receive_z(0)
    new = [pf[0]]
    for q in range(1, 19):
        if VEL[q][2] == 0:
            new.append(sf[q])
            continue
        lq = across(live_ref[q - 1], q, live_slot)
        live_ref[q - 1] = lq
        border = lo(2, VEL[q][2])
        moved = across(sf[q], q, flow_slot(q))
        new.append(jnp.where(border & (lq < 0.5), pf[OPP[q]], moved))
    for i in range(1, 7):
        dmask_ref[i - 1] = jnp.where(is_fluid & (live_ref[i - 1] < 0.5), 1.0, 0.0)
    absorb(True)
    x4, y4, z4 = settle_flow(new)
    for n in range(BINS):
        new = [pg[7 * n]] + [sg[6 * n + i] for i in range(4)]
        for i in (5, 6):
            moved = across(sg[6 * n + i - 1], i, bin_slot(n))
            new.append(jnp.where(live_ref[i - 1] > 0.5, moved, 0.0))
        settle_bins(n, new, x4, y4, z4)
    collide(False)
    pack_lateral(lat_1)
    out_2.start()

    place = [
        (
            jnp.where(near_ref[b, 1] >= 0, 1, 0),
            jnp.where(near_ref[b, 3] >= 0, 1, 0),
        )
        for b in range(2)
    ]

    def blocks_by_place(dz, base):
        def pick(wanted):
            ids = [near_ref[0, VEL.index(c) - 1] for c in wanted]
            return jnp.clip(functools.reduce(jnp.maximum, ids) - base, 0, 3)

        here = 2 * half if dz == 0 else pick([(0, 0, dz)])
        along_x = pick([(1, 0, dz), (-1, 0, dz)])
        along_y = pick([(0, 1, dz), (0, -1, dz)])
        last = jnp.clip(6 - here - along_x - along_y, 0, 3)
        px, py = place[0]
        return [
            [
                jnp.where(
                    px == x, jnp.where(py == y, here, along_y), jnp.where(py == y, along_x, last)
                )
                for y in range(2)
            ]
            for x in range(2)
        ]

    in_z.wait_recv()
    receive_z(1)
    mine = blocks_by_place(0, 4 * layer)
    theirs = [blocks_by_place(-1, 4 * layer - 4), blocks_by_place(1, 4 * layer + 4)]
    spots = [(way, y) for way in range(2) for y in range(2)]

    def column(ids, y):
        return [ids[0][y], ids[1][y]]

    arriving, leaving, partial = {}, {}, {}
    for way, y in spots:
        for v in range(PACKS):
            row = own_row(0, 1 - way) + 8 * v
            arriving[way, y, v] = gather(own_z, row, 2 * Z_ROWS, column(mine, y))
        leaving[way, y] = gather(zwin, z_row(way, 0), Z_ROWS, column(theirs[way], y))
        for v in range(PART):
            row = part_row(way, 0) + 8 * v
            partial[way, y, v] = gather(pwin, row, PART_ROWS, column(theirs[way], y))

    def plane(tile_at, slot_of_way):
        out = None
        for way, y in spots:
            s = 2 * way + y
            moved = roll_lanes(tile_at(way, y), s - slot_of_way(way))
            out = moved if out is None else jnp.where(kk == s, moved, out)
        return out

    at_y = kk & 1

    def plane_shift(x, lateral):
        cx, cy = lateral
        if cx != 0:
            turned = roll_lanes(x, 64)
            edge = lo(0, cx)
            inner = edge & (~even if cx > 0 else even)
            out = jnp.where(inner, roll_rows(turned, 3 * cx), x_shift(turned, cx))
            return out, edge & (even if cx > 0 else ~even)
        if cy != 0:
            edge = lo(1, cy)
            inner = edge & ((at_y == 1) if cy > 0 else (at_y == 0))
            out = jnp.where(inner, roll_lanes(x, -55 * cy), roll_lanes(x, 8 * cy))
            return out, edge & ((at_y == 0) if cy > 0 else (at_y == 1))
        return x, None

    def back(lateral):
        return (-lateral[0], -lateral[1])

    source_live = plane(lambda way, y: arriving[way, y, 0], lambda way: LIVE_SLOT)
    came, left = {}, {}
    for c in LATERAL:
        left[c] = plane(lambda way, y: partial[way, y, 0], lambda way: slot_at(4 + way, c))
        x = plane(lambda way, y: arriving[way, y, 0], lambda way: slot_at(5 - way, c))
        bounce = plane(lambda way, y: leaving[way, y], lambda way: slot_at(4 + way, back(c)))
        moved, outside = plane_shift(x, c)
        lives, _ = plane_shift(source_live, c)
        lives = lives > 0.5
        if outside is not None:
            lives = lives & ~outside
        came[c] = jnp.where(lives, moved, bounce)
    came_sum = functools.reduce(jnp.add, came.values())
    left_sum = functools.reduce(jnp.add, left.values())
    rho = came_sum + plane(lambda way, y: partial[way, y, 0], lambda way: LIVE_SLOT)
    inv = 1.0 / rho
    ux = plane(lambda way, y: partial[way, y, 3], lambda way: 2) + (came[1, 0] - came[-1, 0])
    uy = plane(lambda way, y: partial[way, y, 3], lambda way: 3) + (came[0, 1] - came[0, -1])
    ux, uy, un = ux * inv, uy * inv, (left_sum - came_sum) * inv
    still = 1.0 - 1.5 * (ux * ux + uy * uy + un * un)
    post = {}
    for c in LATERAL:
        along = un
        if c[0] != 0:
            along = along + c[0] * ux
        if c[1] != 0:
            along = along + c[1] * uy
        weight = OMEGA * (WEIGHT[1] if c == (0, 0) else WEIGHT[7])
        feq = (weight * rho) * (still + 3.0 * along + 4.5 * along * along)
        post[c] = (1.0 - OMEGA) * left[c] + feq

    def spread(x, s):
        x = jnp.where(kk == 0, roll_lanes(x, -s), 0.0)
        for shift in (1, 2, 4):
            x = x + roll_lanes(x, shift)
        return x

    rate_rows = []
    for v in range(PACKS):
        row = jnp.zeros((8, 128), jnp.float32)
        for n in range(BINS):
            if (BIN_SLOT + n) // 8 == v:
                row = jnp.where(kk == (BIN_SLOT + n) % 8, rates_ref[n], row)
        rate_rows.append(row)
    for way, y in spots:
        s = 2 * way + y
        lean = 1.0 + 4.0 * spread(un, s)
        lives = spread(source_live, s) > 0.5
        for v in range(PACKS):
            conc = partial[way, y, 4 if v == 1 else 3] + jnp.where(lives, arriving[way, y, v], 0.0)
            rate = rate_rows[v]
            tile = (1.0 - rate) * partial[way, y, v] + (0.125 * rate) * conc * lean
            if v == 0:
                for c in LATERAL:
                    m = slot_at(4 + way, c)
                    tile = jnp.where(kk == m, roll_lanes(post[c], m - s), tile)
            ghost[pl.ds(z_row(way, y) + 8 * v, 8), :] = tile

    def ghost_tile(q, way, v):
        cx, cy, cz = VEL[q]
        blocks = []
        for px, py in place:
            blocks.append(2 * (1 - py if cy != 0 else py) + (1 - px if cx != 0 else px))
        return gather(ghost, z_row(way, 0) + 8 * v, Z_ROWS, blocks)

    in_2.wait_recv()
    face_tile, edge_tile = windows(lat_1, ghost_tile)
    absorb(False)
    new = [pf[0]]
    for q in range(1, 19):
        moved = stream(pf[q], q, flow_slot(q), face_tile, edge_tile)
        new.append(jnp.where(live_ref[q - 1] > 0.5, moved, pf[OPP[q]]))
    x4, y4, z4 = settle_flow(new)
    for n in range(BINS):
        new = [pg[7 * n]]
        for i in range(1, 7):
            moved = stream(pg[7 * n + i], i, bin_slot(n), face_tile, edge_tile)
            new.append(jnp.where(live_ref[i - 1] > 0.5, moved, 0.0))
        settle_bins(n, new, x4, y4, z4)

    table = jnp.zeros((8, 128), jnp.float32)
    for n in range(BINS):
        table = jnp.where(lane == n, jnp.sum(dacc[n], axis=1, keepdims=True), table)
    table = table + roll_rows(table, 2)
    table = table + roll_rows(table, 4)
    dep_ref[...] = table[:2, :BINS]

    for copy in (out_1, out_z, out_2):
        copy.wait_send()

    def sent(way):
        for n in range(2):
            for h in range(2):
                z_copy(n, way, h).wait_send()

    each_way(sent)


def write_out(flow, bins, deposit, flow_out, bins_out, dep_out, sem):
    pairs = [(bins, bins_out), (flow, flow_out), (deposit, dep_out)]
    copies = [pltpu.make_async_copy(a, b, sem.at[n]) for n, (a, b) in enumerate(pairs)]
    for copy in copies:
        copy.start()
    for copy in copies:
        copy.wait()


def tiled(x):
    x = x.reshape(2, -1, 4, 128)
    return x.transpose(1, 2, 0, 3).reshape(-1, 8, 128)


def untiled(x):
    return x.reshape(-1, 4, 2, 128).transpose(2, 0, 1, 3).reshape(2, -1, 512)


def on_device(flow_pops, bin_pops, site_kind, neighbours, bin_rates, settle, inlet_conc):
    subs = lax.axis_size("sub")
    layers = lax.axis_size("dom") * subs // 2
    hbm = pl.BlockSpec(memory_space=pltpu.HBM)
    vmem = pl.BlockSpec(memory_space=pltpu.VMEM)
    f32 = jnp.float32
    shapes = (
        jax.ShapeDtypeStruct((19, 8, 128), f32),
        jax.ShapeDtypeStruct((7 * BINS, 8, 128), f32),
        jax.ShapeDtypeStruct((2, BINS), f32),
    )
    done = pl.pallas_call(
        functools.partial(kernel, layers, subs),
        out_shape=shapes,
        in_specs=[hbm] * 7,
        out_specs=(vmem, vmem, vmem),
        scratch_shapes=[
            pltpu.VMEM((8, 128), jnp.int32),
            pltpu.SMEM((2, 18), jnp.int32),
            pltpu.SMEM((BINS,), f32),
            pltpu.SMEM((BINS,), f32),
            pltpu.SMEM((BINS,), f32),
            pltpu.VMEM((19, 8, 128), f32),
            pltpu.VMEM((7 * BINS, 8, 128), f32),
            pltpu.VMEM((19, 8, 128), f32),
            pltpu.VMEM((6 * BINS, 8, 128), f32),
            pltpu.VMEM((18, 8, 128), f32),
            pltpu.VMEM((6, 8, 128), f32),
            pltpu.VMEM((BINS, 8, 128), f32),
            pltpu.VMEM((lat_row(2) + 8, 128), f32),
            pltpu.VMEM((lat_row(2) + 8, 128), f32),
            pltpu.VMEM((own_row(2, 0) + 8, 128), f32),
            pltpu.VMEM((z_row(2, 0) + 8, 128), f32),
            pltpu.VMEM((part_row(2, 0) + 8, 128), f32),
            pltpu.VMEM((2, PART_ROWS, 128), f32),
            pltpu.VMEM((z_row(2, 0) + 8, 128), f32),
            pltpu.SemaphoreType.DMA((7,)),
            pltpu.SemaphoreType.DMA((2, 4)),
            pltpu.SemaphoreType.DMA((2, 4)),
            pltpu.SemaphoreType.DMA((3,)),
            pltpu.SemaphoreType.DMA((3,)),
        ],
        compiler_params=pltpu.CompilerParams(
            collective_id=0, has_side_effects=True, vmem_limit_bytes=16 * 1024 * 1024
        ),
    )(
        *[
            pltpu.with_memory_space_constraint(x, pltpu.HBM)
            for x in (
                tiled(flow_pops),
                tiled(bin_pops),
                tiled(site_kind)[0],
                neighbours,
                bin_rates,
                settle,
                inlet_conc,
            )
        ]
    )
    flow, bins, deposit = pl.pallas_call(
        write_out,
        out_shape=shapes,
        in_specs=[vmem, vmem, vmem],
        out_specs=(hbm, hbm, hbm),
        scratch_shapes=[pltpu.SemaphoreType.DMA((3,))],
        compiler_params=pltpu.CompilerParams(vmem_limit_bytes=16 * 1024 * 1024),
    )(*done)
    return untiled(flow), untiled(bins), deposit


def solution(mesh):
    cut = ("dom", "sub")
    return jax.shard_map(
        on_device,
        mesh=mesh,
        in_specs=(P(cut, None, None), P(cut, None, None), P(cut, None), P(cut, None), P(), P(), P()),
        out_specs=(P(cut, None, None), P(cut, None, None), P(cut, None)),
        check_vma=False,
    )
```

```python
import functools

import jax
import jax.numpy as jnp
from jax import lax
from jax.experimental import pallas as pl
from jax.experimental.pallas import tpu as pltpu
from jax.sharding import PartitionSpec as P

VEL = [
    (0, 0, 0),
    (1, 0, 0),
    (-1, 0, 0),
    (0, 1, 0),
    (0, -1, 0),
    (0, 0, 1),
    (0, 0, -1),
    (1, 1, 0),
    (-1, -1, 0),
    (1, -1, 0),
    (-1, 1, 0),
    (1, 0, 1),
    (-1, 0, -1),
    (1, 0, -1),
    (-1, 0, 1),
    (0, 1, 1),
    (0, -1, -1),
    (0, 1, -1),
    (0, -1, 1),
]
WEIGHT = [1.0 / 3.0] + [1.0 / 18.0] * 6 + [1.0 / 36.0] * 12
OPP = [0, 2, 1, 4, 3, 6, 5, 8, 7, 10, 9, 12, 11, 14, 13, 16, 15, 18, 17]
OMEGA = 1.6
INLET = 0.04
BINS = 12
MESH = pl.DeviceIdType.MESH

FACE_POPS = [
    [q for q in range(1, 19) if VEL[q][d // 2] == 1 - 2 * (d % 2)] for d in range(6)
]
LIVE_SLOT = 5
BIN_SLOT = 6
PACKS = 3
PART = 5
LAT_ROWS, Z_ROWS, PART_ROWS = 2 * PACKS * 8, PACKS * 8, PART * 8
LATERAL = [(0, 0), (1, 0), (-1, 0), (0, 1), (0, -1)]


def lat_row(h):
    return 8 + LAT_ROWS * h


def own_row(h, way):
    return 8 + Z_ROWS * (2 * h + way)


def z_row(way, h):
    return 8 + Z_ROWS * (2 * way + h)


def part_row(way, h):
    return 8 + PART_ROWS * (2 * way + h)


def slot_at(d, lateral):
    return [VEL[q][:2] for q in FACE_POPS[d]].index(lateral)


def roll_lanes(x, shift):
    shift %= 128
    return x if shift == 0 else pltpu.roll(x, shift, 1)


def roll_rows(x, shift):
    shift %= 8
    return x if shift == 0 else pltpu.roll(x, shift, 0)


def kernel(
    layers,
    subs,
    flow_in,
    bins_in,
    kind_in,
    near_in,
    rates_in,
    settle_in,
    conc_in,
    fbuf,
    gbuf,
    dep_ref,
    kind_ref,
    near_ref,
    rates_ref,
    settle_ref,
    conc_ref,
    pf,
    pg,
    sf,
    sg,
    live_ref,
    dmask_ref,
    dacc,
    lat_0,
    lat_1,
    own_z,
    zwin,
    pwin,
    psend,
    ghost,
    came_ref,
    in_sem,
    send_sem,
    recv_sem,
    mate_send,
    mate_recv,
):
    lats = (lat_0, lat_1)
    me = lax.axis_index("dom") * subs + lax.axis_index("sub")
    layer = me // 2
    half = me % 2
    mate = 2 * layer + 1 - half
    far = 1 - (me % subs) // 2

    def device(g):
        return (g // subs, g % subs)

    def beyond(way):
        return layer + 1 - 2 * way

    def each_way(do):
        for way in (far, 1 - far):
            there = beyond(way)
            pl.when((there >= 0) & (there < layers))(functools.partial(do, way))

    barrier = pltpu.get_barrier_semaphore()

    def greet(way):
        for h in range(2):
            pl.semaphore_signal(
                barrier, inc=1, device_id=device(2 * beyond(way) + h), device_id_type=MESH
            )

    each_way(greet)
    pl.semaphore_signal(barrier, inc=1, device_id=device(mate), device_id_type=MESH)

    pairs = [
        (flow_in, fbuf),
        (kind_in, kind_ref),
        (bins_in, gbuf),
        (rates_in, rates_ref),
        (settle_in, settle_ref),
        (conc_in, conc_ref),
        (near_in, near_ref),
    ]
    loads = [pltpu.make_async_copy(a, b, in_sem.at[n]) for n, (a, b) in enumerate(pairs)]
    for copy in loads:
        copy.start()

    sub = lax.broadcasted_iota(jnp.int32, (8, 128), 0)
    lane = lax.broadcasted_iota(jnp.int32, (8, 128), 1)
    jj = (lane >> 3) & 7
    kk = lane & 7
    low = lane < 64
    even = (sub & 1) == 0
    quarter = sub >> 1
    at = {
        (0, 0): (quarter == 0) & low,
        (0, 7): (quarter == 3) & (lane >= 64),
        (1, 0): jj == 0,
        (1, 7): jj == 7,
        (2, 0): kk == 0,
        (2, 7): kk == 7,
    }

    loads[0].wait()
    loads[1].wait()
    kind = kind_ref[...]
    alive = jnp.where(kind > 0, 1.0, 0.0)
    is_in = kind == 2
    is_out = kind == 3
    is_fluid = kind == 1

    def moments(f):
        rho = f[0]
        for q in range(1, 19):
            rho = rho + f[q]
        inv = 1.0 / rho
        vel = []
        for axis in range(3):
            plus = [f[q] for q in range(19) if VEL[q][axis] == 1]
            minus = [f[q] for q in range(19) if VEL[q][axis] == -1]
            vel.append((functools.reduce(jnp.add, plus) - functools.reduce(jnp.add, minus)) * inv)
        return rho, vel

    def equilibrium(scale, vel):
        base = 1.0 - 1.5 * (vel[0] * vel[0] + vel[1] * vel[1] + vel[2] * vel[2])
        scaled = {w: scale * w for w in set(WEIGHT)}
        out = [None] * 19
        out[0] = scaled[WEIGHT[0]] * base
        for q in range(1, 19, 2):
            along = None
            for axis in range(3):
                if VEL[q][axis] != 0:
                    term = vel[axis]
                    if along is None:
                        along = term if VEL[q][axis] > 0 else -term
                    else:
                        along = along + term if VEL[q][axis] > 0 else along - term
            even = base + 4.5 * along * along
            odd = 3.0 * along
            out[q] = scaled[WEIGHT[q]] * (even + odd)
            out[q + 1] = scaled[WEIGHT[q]] * (even - odd)
        return out

    def put(packs, d, slot, x):
        axis, minus = d // 2, d % 2
        v, m = slot // 8, slot % 8
        if axis == 0:
            t, h = m // 2, m % 2
            src_row, src_half = (0, 0) if minus else (3, 1)
            x = roll_rows(roll_lanes(x, 64 * (h - src_half)), 2 * (t - src_row))
            mask = (quarter == t) & (low if h == 0 else lane >= 64)
        else:
            src = 0 if minus else 7
            x = roll_lanes(x, (m - src) * (8 if axis == 1 else 1))
            mask = (jj if axis == 1 else kk) == m
        packs[v] = x if packs[v] is None else jnp.where(mask, x, packs[v])

    def gather(ref, row, stride, blocks):
        parts = [
            ref[pl.ds(row + stride * (w >> 1) + (w & 1) - b, 8), :] for b, w in enumerate(blocks)
        ]
        return jnp.where(even, parts[0], parts[1])

    def nearby(q, base):
        return [jnp.clip(near_ref[b, q - 1] - base, 0, 3) for b in range(2)]

    def present(q):
        return jnp.where(even, near_ref[0, q - 1], near_ref[1, q - 1]) >= 0

    def x_shift(r, cx):
        if cx == 0:
            return r
        moved = roll_rows(r, 2 * cx)
        return jnp.where(low, moved, r) if cx > 0 else jnp.where(low, r, moved)

    def local(a, q):
        cx, cy, cz = VEL[q]
        return x_shift(roll_lanes(a, 64 * abs(cx) + 8 * cy + cz), cx)

    def unpack(d, slot, tile, q):
        cx, cy, cz = VEL[q]
        m = slot % 8
        plus = d % 2 == 0
        if d // 2 == 0:
            t, h = m // 2, m % 2
            to_row, to_half = (0, 0) if plus else (3, 1)
            return roll_rows(roll_lanes(tile, 64 * (to_half - h) + 8 * cy + cz), 2 * (to_row - t))
        to = 0 if plus else 7
        if d // 2 == 1:
            return x_shift(roll_lanes(tile, 64 * abs(cx) + 8 * (to - m) + cz), cx)
        return x_shift(roll_lanes(tile, 64 * abs(cx) + 8 * cy + to - m), cx)

    def unpack_edge(d, slot, tile, q):
        cx, cy, cz = VEL[q]
        m = slot % 8
        to = 0 if d % 2 == 0 else 7
        shift = 8 * (to - m) if d // 2 == 1 else to - m
        if cx != 0:
            return roll_rows(roll_lanes(tile, shift + 64), -6 * cx)
        return roll_lanes(tile, shift - 56 * cy)

    def face_of(axis, sign):
        return 2 * axis + (0 if sign > 0 else 1)

    def edge_face(q):
        axis = 2 if VEL[q][2] != 0 else 1
        return face_of(axis, VEL[q][axis])

    def lo(axis, sign):
        return at[(axis, 0 if sign > 0 else 7)]

    def stream(a, q, slot_of, face_tile, edge_tile):
        out = a
        axes = [axis for axis in range(3) if VEL[q][axis] != 0]
        for axis in axes:
            d = face_of(axis, VEL[q][axis])
            slot = slot_of(d)
            out = jnp.where(
                lo(axis, VEL[q][axis]), unpack(d, slot, face_tile(d, slot // 8), q), out
            )
        if len(axes) == 2:
            d = edge_face(q)
            slot = slot_of(d)
            mask = lo(axes[0], VEL[q][axes[0]]) & lo(axes[1], VEL[q][axes[1]])
            out = jnp.where(mask, unpack_edge(d, slot, edge_tile(q), q), out)
        return out

    def mate_copy(n, ref, row, rows, h):
        span = pl.ds(row(h), rows)
        return pltpu.make_async_remote_copy(
            src_ref=ref.at[span],
            dst_ref=ref.at[span],
            send_sem=mate_send.at[n],
            recv_sem=mate_recv.at[n],
            device_id=device(mate),
            device_id_type=MESH,
        )

    def mate_copies(h):
        return (
            mate_copy(0, lat_0, lat_row, LAT_ROWS, h),
            mate_copy(1, own_z, lambda h: own_row(h, 0), 2 * Z_ROWS, h),
            mate_copy(2, lat_1, lat_row, LAT_ROWS, h),
        )

    def z_copy(n, way, h):
        src = (own_z.at[pl.ds(own_row(half, way), Z_ROWS)], psend.at[way])[n]
        dst = (
            zwin.at[pl.ds(z_row(way, half), Z_ROWS)],
            pwin.at[pl.ds(part_row(way, half), PART_ROWS)],
        )[n]
        return pltpu.make_async_remote_copy(
            src_ref=src,
            dst_ref=dst,
            send_sem=send_sem.at[n, 2 * way + h],
            recv_sem=recv_sem.at[n, 2 * way + half],
            device_id=device(2 * beyond(way) + h),
            device_id_type=MESH,
        )

    def z_in(n, way, h):
        src = (own_z.at[pl.ds(own_row(half, way), Z_ROWS)], psend.at[way])[n]
        dst = (
            zwin.at[pl.ds(z_row(way, h), Z_ROWS)],
            pwin.at[pl.ds(part_row(way, h), PART_ROWS)],
        )[n]
        return pltpu.make_async_remote_copy(
            src_ref=src,
            dst_ref=dst,
            send_sem=send_sem.at[n, 2 * way + h],
            recv_sem=recv_sem.at[n, 2 * way + h],
            device_id=device(2 * beyond(1 - way) + h),
            device_id_type=MESH,
        )

    def send_z(n):
        def do(way):
            for h in range(2):
                z_copy(n, way, h).start()

        each_way(do)

    def receive_z(n):
        def do(way):
            for h in range(2):
                z_in(n, 1 - way, h).wait_recv()

        each_way(do)

    def collide(first):
        f = [fbuf[q] for q in range(19)]
        rho, vel = moments(f)
        target = equilibrium(OMEGA * rho, vel)
        for q in range(19):
            pf[q] = (1.0 - OMEGA) * f[q] + target[q]
        if first:
            for copy in loads[2:]:
                copy.wait()
        x4, y4, z4 = [4.0 * u for u in vel]
        for n in range(BINS):
            rate = rates_ref[n]
            keep = 1.0 - rate
            g = [gbuf[7 * n + i] for i in range(7)]
            conc = functools.reduce(jnp.add, g)
            part = (0.125 * rate) * conc
            pg[7 * n] = keep * g[0] + (part + part)
            for axis, u4 in ((0, x4), (1, y4 - 4.0 * settle_ref[n]), (2, z4)):
                lean = part * u4
                pg[7 * n + 1 + 2 * axis] = keep * g[1 + 2 * axis] + (part + lean)
                pg[7 * n + 2 + 2 * axis] = keep * g[2 + 2 * axis] + (part - lean)

    def pack_z(way):
        d = 4 + way
        packs = [None] * PACKS
        for s, q in enumerate(FACE_POPS[d]):
            put(packs, d, s, pf[q])
        put(packs, d, LIVE_SLOT, alive)
        for n in range(BINS):
            put(packs, d, BIN_SLOT + n, pg[7 * n + 1 + d])
        for v, tile in enumerate(packs):
            own_z[pl.ds(pl.multiple_of(own_row(half, way) + 8 * v, 8), 8), :] = tile

    def pack_lateral(ref):
        for axis in range(2):
            sides = []
            for d in (2 * axis, 2 * axis + 1):
                packs = [None] * PACKS
                for s, q in enumerate(FACE_POPS[d]):
                    put(packs, d, s, pf[q])
                put(packs, d, LIVE_SLOT, alive)
                for n in range(BINS):
                    put(packs, d, BIN_SLOT + n, pg[7 * n + 1 + d])
                sides.append(packs)
            ahead = present(1 + 2 * axis)
            row = lat_row(half) + 8 * PACKS * axis
            for v in range(PACKS):
                ref[pl.ds(pl.multiple_of(row + 8 * v, 8), 8), :] = jnp.where(
                    ahead, sides[0][v], sides[1][v]
                )

    def absent_as_zero(q, v, tile):
        return jnp.where(present(q), tile, 0.0) if v == 0 else tile

    def windows(lat, z_tile):
        memo = {}

        def tile_of(q, d, v):
            if (q, d, v) not in memo:
                if d >= 4:
                    tile = z_tile(q, d - 4, v)
                else:
                    row = lat_row(0) + 8 * (PACKS * (d // 2) + v)
                    tile = gather(lat, row, LAT_ROWS, nearby(q, 4 * layer))
                memo[(q, d, v)] = absent_as_zero(q, v, tile)
            return memo[(q, d, v)]

        return (
            lambda d, v: tile_of(OPP[1 + d], d, v),
            lambda q: tile_of(OPP[q], edge_face(q), 0),
        )

    def flow_slot(q):
        return lambda d: FACE_POPS[d].index(q)

    def bin_slot(n):
        return lambda d: BIN_SLOT + n

    def live_slot(d):
        return LIVE_SLOT

    def absorb(first):
        for n in range(BINS):
            terms = [dmask_ref[i - 1] * pg[7 * n + OPP[i]] for i in range(1, 7)]
            total = functools.reduce(jnp.add, terms)
            dacc[n] = total if first else dacc[n] + total

    def settle_flow(new):
        rho, vel = moments(new)
        base = equilibrium(jnp.ones_like(rho), vel)
        for q in range(19):
            inlet = WEIGHT[q] * (
                1.0
                + 3.0 * VEL[q][2] * INLET
                + 4.5 * (VEL[q][2] * INLET) ** 2
                - 1.5 * INLET * INLET
            )
            old = fbuf[q]
            fbuf[q] = jnp.where(
                is_fluid, new[q], jnp.where(is_out, base[q], jnp.where(is_in, inlet, old))
            )
        return [4.0 * u for u in vel]

    def settle_bins(n, new, x4, y4, z4):
        fall = 4.0 * settle_ref[n]
        level = conc_ref[n]
        part = 0.125 * functools.reduce(jnp.add, new)
        outlet = [part + part]
        inlet = [0.25 * level]
        for u4, s4 in ((x4, 0.0), (y4 - fall, -fall), (z4, 4.0 * INLET)):
            lean = part * u4
            outlet += [part + lean, part - lean]
            inlet += [0.125 * level * (1.0 + s4), 0.125 * level * (1.0 - s4)]
        for i in range(7):
            old = gbuf[7 * n + i]
            gbuf[7 * n + i] = jnp.where(
                is_fluid, new[i], jnp.where(is_out, outlet[i], jnp.where(is_in, inlet[i], old))
            )

    def move_inside():
        for q in range(1, 19):
            sf[q] = local(pf[q], q)
        for n in range(BINS):
            for i in range(1, 7):
                sg[6 * n + i - 1] = local(pg[7 * n + i], i)

    collide(True)
    for way in range(2):
        pack_z(way)
    pack_lateral(lat_0)
    ends = jnp.where(layer < layers - 1, 1, 0) + jnp.where(layer > 0, 1, 0)
    pl.semaphore_wait(barrier, 1 + 2 * ends)
    send_z(0)
    out_1, out_z, out_2 = mate_copies(half)
    in_1, in_z, in_2 = mate_copies(1 - half)
    out_1.start()
    out_z.start()
    move_inside()

    def z_tile(q, way, v):
        base = 4 * layer + (-4 if way == 0 else 4)
        return gather(zwin, z_row(way, 0) + 8 * v, Z_ROWS, nearby(q, base))

    in_1.wait_recv()
    face_tile, edge_tile = windows(lat_0, z_tile)

    def within(a, q, slot_of):
        out = a
        axes = [axis for axis in range(2) if VEL[q][axis] != 0]
        for axis in axes:
            d = face_of(axis, VEL[q][axis])
            moved = unpack(d, slot_of(d), face_tile(d, slot_of(d) // 8), q)
            out = jnp.where(lo(axis, VEL[q][axis]), moved, out)
        if len(axes) == 2:
            d = edge_face(q)
            mask = lo(0, VEL[q][0]) & lo(1, VEL[q][1])
            out = jnp.where(mask, unpack_edge(d, slot_of(d), edge_tile(q), q), out)
        return out

    def across(a, q, slot_of):
        cx, cy, cz = VEL[q]
        if cz == 0:
            return a
        d = face_of(2, cz)
        slot = slot_of(d)
        moved = unpack(d, slot, face_tile(d, slot // 8), q)
        for axis in range(2):
            if VEL[q][axis] != 0:
                moved = jnp.where(
                    lo(axis, VEL[q][axis]), unpack_edge(d, slot, edge_tile(q), q), moved
                )
        return jnp.where(lo(2, cz), moved, a)

    flow = [pf[0]]
    for q in range(1, 19):
        lq = within(local(alive, q), q, live_slot)
        live_ref[q - 1] = lq
        flow.append(jnp.where(lq > 0.5, within(sf[q], q, flow_slot(q)), pf[OPP[q]]))
        sf[q] = flow[q]

    def total(rows, pick):
        return functools.reduce(jnp.add, [rows[q] for q in range(len(rows)) if pick(VEL[q])])

    level_sum = [
        total(flow, lambda c: c[2] == 0),
        total(flow, lambda c: c[0] == 1 and c[2] == 0)
        - total(flow, lambda c: c[0] == -1 and c[2] == 0),
        total(flow, lambda c: c[1] == 1 and c[2] == 0)
        - total(flow, lambda c: c[1] == -1 and c[2] == 0),
    ]
    parts = [[None] * PART for way in range(2)]

    def put_part(way, tile, m, x):
        packs = [None] * PART
        packs[tile] = parts[way][tile]
        put(packs, 4 + way, 8 * tile + m, x)
        parts[way][tile] = packs[tile]

    for way in range(2):
        rows = FACE_POPS[4 + way]
        for s, q in enumerate(rows):
            put_part(way, 0, s, flow[q])
        out_sum = functools.reduce(jnp.add, [flow[q] for q in rows])
        put_part(way, 0, LIVE_SLOT, level_sum[0] + out_sum)
        put_part(way, 3, 4, out_sum)
        x_sum = flow[rows[slot_at(4 + way, (1, 0))]] - flow[rows[slot_at(4 + way, (-1, 0))]]
        y_sum = flow[rows[slot_at(4 + way, (0, 1))]] - flow[rows[slot_at(4 + way, (0, -1))]]
        put_part(way, 3, 2, level_sum[1] + x_sum)
        put_part(way, 3, 3, level_sum[2] + y_sum)
    for n in range(BINS):
        g = [pg[7 * n]]
        for i in range(1, 7):
            moved = within(sg[6 * n + i - 1], i, bin_slot(n))
            g.append(jnp.where(live_ref[i - 1] > 0.5, moved, 0.0))
            sg[6 * n + i - 1] = g[i]
        flat = functools.reduce(jnp.add, g[:5])
        v, m = (BIN_SLOT + n) // 8, (BIN_SLOT + n) % 8
        for way in range(2):
            put_part(way, v, m, g[5 + way])
            put_part(way, 4 if v == 1 else 3, m, flat + g[5 + way])
    for way in range(2):
        for v in range(PART):
            psend[way, pl.ds(8 * v, 8), :] = parts[way][v]
    send_z(1)

    receive_z(0)
    new = [pf[0]]
    for q in range(1, 19):
        if VEL[q][2] == 0:
            new.append(sf[q])
            continue
        lq = across(live_ref[q - 1], q, live_slot)
        live_ref[q - 1] = lq
        border = lo(2, VEL[q][2])
        moved = across(sf[q], q, flow_slot(q))
        new.append(jnp.where(border & (lq < 0.5), pf[OPP[q]], moved))
    for i in range(1, 7):
        dmask_ref[i - 1] = jnp.where(is_fluid & (live_ref[i - 1] < 0.5), 1.0, 0.0)
    absorb(True)
    x4, y4, z4 = settle_flow(new)
    for n in range(BINS):
        new = [pg[7 * n]] + [sg[6 * n + i] for i in range(4)]
        for i in (5, 6):
            moved = across(sg[6 * n + i - 1], i, bin_slot(n))
            new.append(jnp.where(live_ref[i - 1] > 0.5, moved, 0.0))
        settle_bins(n, new, x4, y4, z4)
    collide(False)
    pack_lateral(lat_1)
    out_2.start()
    move_inside()
    absorb(False)
    table = jnp.zeros((8, 128), jnp.float32)
    for n in range(BINS):
        table = jnp.where(lane == n, jnp.sum(dacc[n], axis=1, keepdims=True), table)
    table = table + roll_rows(table, 2)
    table = table + roll_rows(table, 4)
    dep_ref[...] = table[:2, :BINS]

    place = [
        (
            jnp.where(near_ref[b, 1] >= 0, 1, 0),
            jnp.where(near_ref[b, 3] >= 0, 1, 0),
        )
        for b in range(2)
    ]

    def blocks_by_place(dz, base):
        def pick(wanted):
            ids = [near_ref[0, VEL.index(c) - 1] for c in wanted]
            return jnp.clip(functools.reduce(jnp.maximum, ids) - base, 0, 3)

        here = 2 * half if dz == 0 else pick([(0, 0, dz)])
        along_x = pick([(1, 0, dz), (-1, 0, dz)])
        along_y = pick([(0, 1, dz), (0, -1, dz)])
        last = jnp.clip(6 - here - along_x - along_y, 0, 3)
        px, py = place[0]
        return [
            [
                jnp.where(
                    px == x, jnp.where(py == y, here, along_y), jnp.where(py == y, along_x, last)
                )
                for y in range(2)
            ]
            for x in range(2)
        ]

    in_z.wait_recv()
    mine = blocks_by_place(0, 4 * layer)
    theirs = [blocks_by_place(-1, 4 * layer - 4), blocks_by_place(1, 4 * layer + 4)]
    spots = [(way, y) for way in range(2) for y in range(2)]

    def column(ids, y):
        return [ids[0][y], ids[1][y]]

    arriving, leaving = {}, {}
    for way, y in spots:
        for v in range(PACKS):
            row = own_row(0, 1 - way) + 8 * v
            arriving[way, y, v] = gather(own_z, row, 2 * Z_ROWS, column(mine, y))
        leaving[way, y] = gather(zwin, z_row(way, 0), Z_ROWS, column(theirs[way], y))

    def plane(tile_at, slot_of_way):
        out = None
        for way, y in spots:
            s = 2 * way + y
            moved = roll_lanes(tile_at(way, y), s - slot_of_way(way))
            out = moved if out is None else jnp.where(kk == s, moved, out)
        return out

    at_y = kk & 1

    def plane_shift(x, lateral):
        cx, cy = lateral
        if cx != 0:
            turned = roll_lanes(x, 64)
            edge = lo(0, cx)
            inner = edge & (~even if cx > 0 else even)
            out = jnp.where(inner, roll_rows(turned, 3 * cx), x_shift(turned, cx))
            return out, edge & (even if cx > 0 else ~even)
        if cy != 0:
            edge = lo(1, cy)
            inner = edge & ((at_y == 1) if cy > 0 else (at_y == 0))
            out = jnp.where(inner, roll_lanes(x, -55 * cy), roll_lanes(x, 8 * cy))
            return out, edge & ((at_y == 0) if cy > 0 else (at_y == 1))
        return x, None

    def back(lateral):
        return (-lateral[0], -lateral[1])

    def spread(x, m):
        out = x
        for other in range(8):
            if other != m:
                out = jnp.where(kk == other, roll_lanes(x, other - m), out)
        return out

    source_live = plane(lambda way, y: arriving[way, y, 0], lambda way: LIVE_SLOT)
    came = {}
    for c in LATERAL:
        x = plane(lambda way, y: arriving[way, y, 0], lambda way: slot_at(5 - way, c))
        bounce = plane(lambda way, y: leaving[way, y], lambda way: slot_at(4 + way, back(c)))
        moved, outside = plane_shift(x, c)
        lives, _ = plane_shift(source_live, c)
        lives = lives > 0.5
        if outside is not None:
            lives = lives & ~outside
        came[c] = jnp.where(lives, moved, bounce)
    sums = (
        functools.reduce(jnp.add, came.values()),
        came[1, 0] - came[-1, 0],
        came[0, 1] - came[0, -1],
    )
    for n, (way, y) in enumerate(spots):
        s = 2 * way + y
        for t in range(3):
            came_ref[3 * n + t] = spread(sums[t], s)
        lives = spread(source_live, s) > 0.5
        for v in range(PACKS):
            came_ref[12 + PACKS * n + v] = jnp.where(lives, arriving[way, y, v], 0.0)

    def by_slot(value_of):
        row = jnp.zeros((8, 128), jnp.float32)
        for m in range(8):
            if value_of(m) is not None:
                row = jnp.where(kk == m, value_of(m), row)
        return row

    rate_rows = []
    for v in range(PACKS):
        bins = [8 * v + m - BIN_SLOT for m in range(8)]
        rate_rows.append(by_slot(lambda m: rates_ref[bins[m]] if 0 <= bins[m] < BINS else None))
    weights = by_slot(lambda m: OMEGA * (WEIGHT[1] if m == 0 else WEIGHT[7]) if m < 5 else None)
    leans = [
        [
            by_slot(lambda m: float(VEL[FACE_POPS[4 + way][m]][axis]) if m < 5 else None)
            for axis in range(2)
        ]
        for way in range(2)
    ]

    receive_z(1)
    for n, (way, y) in enumerate(spots):
        partial = [
            gather(pwin, part_row(way, 0) + 8 * v, PART_ROWS, column(theirs[way], y))
            for v in range(PART)
        ]
        came_sum, came_x, came_y = [came_ref[3 * n + t] for t in range(3)]
        rho = spread(partial[0], LIVE_SLOT) + came_sum
        inv = 1.0 / rho
        ux = (spread(partial[3], 2) + came_x) * inv
        uy = (spread(partial[3], 3) + came_y) * inv
        un = (spread(partial[3], 4) - came_sum) * inv
        along = un + leans[way][0] * ux + leans[way][1] * uy
        still = 1.0 - 1.5 * (ux * ux + uy * uy + un * un)
        feq = (weights * rho) * (still + 3.0 * along + 4.5 * along * along)
        lean = 1.0 + 4.0 * un
        for v in range(PACKS):
            conc = partial[4 if v == 1 else 3] + came_ref[12 + PACKS * n + v]
            rate = rate_rows[v]
            tile = (1.0 - rate) * partial[v] + (0.125 * rate) * conc * lean
            if v == 0:
                tile = jnp.where(kk < 5, (1.0 - OMEGA) * partial[0] + feq, tile)
            ghost[pl.ds(z_row(way, y) + 8 * v, 8), :] = tile

    def ghost_tile(q, way, v):
        cx, cy, cz = VEL[q]
        blocks = []
        for px, py in place:
            blocks.append(2 * (1 - py if cy != 0 else py) + (1 - px if cx != 0 else px))
        return gather(ghost, z_row(way, 0) + 8 * v, Z_ROWS, blocks)

    in_2.wait_recv()
    face_tile, edge_tile = windows(lat_1, ghost_tile)
    new = [pf[0]]
    for q in range(1, 19):
        moved = stream(sf[q], q, flow_slot(q), face_tile, edge_tile)
        new.append(jnp.where(live_ref[q - 1] > 0.5, moved, pf[OPP[q]]))
    x4, y4, z4 = settle_flow(new)
    for n in range(BINS):
        new = [pg[7 * n]]
        for i in range(1, 7):
            moved = stream(sg[6 * n + i - 1], i, bin_slot(n), face_tile, edge_tile)
            new.append(jnp.where(live_ref[i - 1] > 0.5, moved, 0.0))
        settle_bins(n, new, x4, y4, z4)

    for copy in (out_1, out_z, out_2):
        copy.wait_send()

    def sent(way):
        for n in range(2):
            for h in range(2):
                z_copy(n, way, h).wait_send()

    each_way(sent)


def write_out(flow, bins, deposit, flow_out, bins_out, dep_out, sem):
    pairs = [(bins, bins_out), (flow, flow_out), (deposit, dep_out)]
    copies = [pltpu.make_async_copy(a, b, sem.at[n]) for n, (a, b) in enumerate(pairs)]
    for copy in copies:
        copy.start()
    for copy in copies:
        copy.wait()


def tiled(x):
    x = x.reshape(2, -1, 4, 128)
    return x.transpose(1, 2, 0, 3).reshape(-1, 8, 128)


def untiled(x):
    return x.reshape(-1, 4, 2, 128).transpose(2, 0, 1, 3).reshape(2, -1, 512)


def on_device(flow_pops, bin_pops, site_kind, neighbours, bin_rates, settle, inlet_conc):
    subs = lax.axis_size("sub")
    layers = lax.axis_size("dom") * subs // 2
    hbm = pl.BlockSpec(memory_space=pltpu.HBM)
    vmem = pl.BlockSpec(memory_space=pltpu.VMEM)
    f32 = jnp.float32
    shapes = (
        jax.ShapeDtypeStruct((19, 8, 128), f32),
        jax.ShapeDtypeStruct((7 * BINS, 8, 128), f32),
        jax.ShapeDtypeStruct((2, BINS), f32),
    )
    done = pl.pallas_call(
        functools.partial(kernel, layers, subs),
        out_shape=shapes,
        in_specs=[hbm] * 7,
        out_specs=(vmem, vmem, vmem),
        scratch_shapes=[
            pltpu.VMEM((8, 128), jnp.int32),
            pltpu.SMEM((2, 18), jnp.int32),
            pltpu.SMEM((BINS,), f32),
            pltpu.SMEM((BINS,), f32),
            pltpu.SMEM((BINS,), f32),
            pltpu.VMEM((19, 8, 128), f32),
            pltpu.VMEM((7 * BINS, 8, 128), f32),
            pltpu.VMEM((19, 8, 128), f32),
            pltpu.VMEM((6 * BINS, 8, 128), f32),
            pltpu.VMEM((18, 8, 128), f32),
            pltpu.VMEM((6, 8, 128), f32),
            pltpu.VMEM((BINS, 8, 128), f32),
            pltpu.VMEM((lat_row(2) + 8, 128), f32),
            pltpu.VMEM((lat_row(2) + 8, 128), f32),
            pltpu.VMEM((own_row(2, 0) + 8, 128), f32),
            pltpu.VMEM((z_row(2, 0) + 8, 128), f32),
            pltpu.VMEM((part_row(2, 0) + 8, 128), f32),
            pltpu.VMEM((2, PART_ROWS, 128), f32),
            pltpu.VMEM((z_row(2, 0) + 8, 128), f32),
            pltpu.VMEM((12 + 4 * PACKS, 8, 128), f32),
            pltpu.SemaphoreType.DMA((7,)),
            pltpu.SemaphoreType.DMA((2, 4)),
            pltpu.SemaphoreType.DMA((2, 4)),
            pltpu.SemaphoreType.DMA((3,)),
            pltpu.SemaphoreType.DMA((3,)),
        ],
        compiler_params=pltpu.CompilerParams(
            collective_id=0, has_side_effects=True, vmem_limit_bytes=16 * 1024 * 1024
        ),
    )(
        *[
            pltpu.with_memory_space_constraint(x, pltpu.HBM)
            for x in (
                tiled(flow_pops),
                tiled(bin_pops),
                tiled(site_kind)[0],
                neighbours,
                bin_rates,
                settle,
                inlet_conc,
            )
        ]
    )
    flow, bins, deposit = pl.pallas_call(
        write_out,
        out_shape=shapes,
        in_specs=[vmem, vmem, vmem],
        out_specs=(hbm, hbm, hbm),
        scratch_shapes=[pltpu.SemaphoreType.DMA((3,))],
        compiler_params=pltpu.CompilerParams(vmem_limit_bytes=16 * 1024 * 1024),
    )(*done)
    return untiled(flow), untiled(bins), deposit


def solution(mesh):
    cut = ("dom", "sub")
    return jax.shard_map(
        on_device,
        mesh=mesh,
        in_specs=(P(cut, None, None), P(cut, None, None), P(cut, None), P(cut, None), P(), P(), P()),
        out_specs=(P(cut, None, None), P(cut, None, None), P(cut, None)),
        check_vma=False,
    )
```

```python
import functools

import jax
import jax.numpy as jnp
from jax import lax
from jax.experimental import pallas as pl
from jax.experimental.pallas import tpu as pltpu
from jax.sharding import PartitionSpec as P

VEL = [
    (0, 0, 0),
    (1, 0, 0),
    (-1, 0, 0),
    (0, 1, 0),
    (0, -1, 0),
    (0, 0, 1),
    (0, 0, -1),
    (1, 1, 0),
    (-1, -1, 0),
    (1, -1, 0),
    (-1, 1, 0),
    (1, 0, 1),
    (-1, 0, -1),
    (1, 0, -1),
    (-1, 0, 1),
    (0, 1, 1),
    (0, -1, -1),
    (0, 1, -1),
    (0, -1, 1),
]
WEIGHT = [1.0 / 3.0] + [1.0 / 18.0] * 6 + [1.0 / 36.0] * 12
OPP = [0, 2, 1, 4, 3, 6, 5, 8, 7, 10, 9, 12, 11, 14, 13, 16, 15, 18, 17]
OMEGA = 1.6
INLET = 0.04
BINS = 12
MESH = pl.DeviceIdType.MESH

FACE_POPS = [
    [q for q in range(1, 19) if VEL[q][d // 2] == 1 - 2 * (d % 2)] for d in range(6)
]
LIVE_SLOT = 5
BIN_SLOT = 6
PACKS = 3
PART = 5
LAT_ROWS, Z_ROWS, PART_ROWS = 2 * PACKS * 8, PACKS * 8, PART * 8
LATERAL = [(0, 0), (1, 0), (-1, 0), (0, 1), (0, -1)]


def lat_row(h):
    return 8 + LAT_ROWS * h


def own_row(h, way):
    return 8 + Z_ROWS * (2 * h + way)


def z_row(way, h):
    return 8 + Z_ROWS * (2 * way + h)


def part_row(way, h):
    return 8 + PART_ROWS * (2 * way + h)


def slot_at(d, lateral):
    return [VEL[q][:2] for q in FACE_POPS[d]].index(lateral)


def add_up(terms):
    terms = list(terms)
    while len(terms) > 1:
        pairs = [a + b for a, b in zip(terms[::2], terms[1::2])]
        terms = pairs + terms[len(pairs) * 2 :]
    return terms[0]


def roll_lanes(x, shift):
    shift %= 128
    return x if shift == 0 else pltpu.roll(x, shift, 1)


def roll_rows(x, shift):
    shift %= 8
    return x if shift == 0 else pltpu.roll(x, shift, 0)


def kernel(
    layers,
    subs,
    flow_in,
    bins_in,
    kind_in,
    near_in,
    rates_in,
    settle_in,
    conc_in,
    fbuf,
    gbuf,
    dep_ref,
    kind_ref,
    near_ref,
    rates_ref,
    settle_ref,
    conc_ref,
    pf,
    pg,
    sf,
    sg,
    live_ref,
    dmask_ref,
    dacc,
    lat_0,
    lat_1,
    own_z,
    zwin,
    pwin,
    psend,
    ghost,
    came_ref,
    in_sem,
    send_sem,
    recv_sem,
    mate_send,
    mate_recv,
):
    lats = (lat_0, lat_1)
    me = lax.axis_index("dom") * subs + lax.axis_index("sub")
    layer = me // 2
    half = me % 2
    mate = 2 * layer + 1 - half
    far = 1 - (me % subs) // 2

    def device(g):
        return (g // subs, g % subs)

    def beyond(way):
        return layer + 1 - 2 * way

    def each_way(do):
        for way in (far, 1 - far):
            there = beyond(way)
            pl.when((there >= 0) & (there < layers))(functools.partial(do, way))

    barrier = pltpu.get_barrier_semaphore()

    def greet(way):
        for h in range(2):
            pl.semaphore_signal(
                barrier, inc=1, device_id=device(2 * beyond(way) + h), device_id_type=MESH
            )

    each_way(greet)
    pl.semaphore_signal(barrier, inc=1, device_id=device(mate), device_id_type=MESH)

    pairs = [
        (flow_in, fbuf),
        (kind_in, kind_ref),
        (bins_in, gbuf),
        (rates_in, rates_ref),
        (settle_in, settle_ref),
        (conc_in, conc_ref),
        (near_in, near_ref),
    ]
    loads = [pltpu.make_async_copy(a, b, in_sem.at[n]) for n, (a, b) in enumerate(pairs)]
    for copy in loads:
        copy.start()

    sub = lax.broadcasted_iota(jnp.int32, (8, 128), 0)
    lane = lax.broadcasted_iota(jnp.int32, (8, 128), 1)
    jj = (lane >> 3) & 7
    kk = lane & 7
    low = lane < 64
    even = (sub & 1) == 0
    quarter = sub >> 1
    at = {
        (0, 0): (quarter == 0) & low,
        (0, 7): (quarter == 3) & (lane >= 64),
        (1, 0): jj == 0,
        (1, 7): jj == 7,
        (2, 0): kk == 0,
        (2, 7): kk == 7,
    }

    loads[0].wait()
    loads[1].wait()
    kind = kind_ref[...]
    alive = jnp.where(kind > 0, 1.0, 0.0)
    is_in = kind == 2
    is_end = kind >= 2
    is_fluid = kind == 1

    def moments(f):
        odd = range(1, 19, 2)
        rho = add_up([f[q] + f[q + 1] for q in odd] + [f[0]])
        inv = 1.0 / rho
        gaps = {q: f[q] - f[q + 1] for q in odd}
        vel = []
        for axis in range(3):
            plus = add_up([gaps[q] for q in odd if VEL[q][axis] == 1])
            minus = [gaps[q] for q in odd if VEL[q][axis] == -1]
            vel.append((plus - add_up(minus) if minus else plus) * inv)
        return rho, vel

    def equilibrium(scale, vel):
        base = 1.0 - 1.5 * (vel[0] * vel[0] + vel[1] * vel[1] + vel[2] * vel[2])
        scaled = {w: scale * w for w in set(WEIGHT)}
        out = [None] * 19
        out[0] = scaled[WEIGHT[0]] * base
        for q in range(1, 19, 2):
            along = None
            for axis in range(3):
                if VEL[q][axis] != 0:
                    term = vel[axis]
                    if along is None:
                        along = term if VEL[q][axis] > 0 else -term
                    else:
                        along = along + term if VEL[q][axis] > 0 else along - term
            even = base + 4.5 * along * along
            odd = 3.0 * along
            out[q] = scaled[WEIGHT[q]] * (even + odd)
            out[q + 1] = scaled[WEIGHT[q]] * (even - odd)
        return out

    def put(packs, d, slot, x):
        axis, minus = d // 2, d % 2
        v, m = slot // 8, slot % 8
        if axis == 0:
            t, h = m // 2, m % 2
            src_row, src_half = (0, 0) if minus else (3, 1)
            x = roll_rows(roll_lanes(x, 64 * (h - src_half)), 2 * (t - src_row))
            mask = (quarter == t) & (low if h == 0 else lane >= 64)
        else:
            src = 0 if minus else 7
            x = roll_lanes(x, (m - src) * (8 if axis == 1 else 1))
            mask = (jj if axis == 1 else kk) == m
        packs[v] = x if packs[v] is None else jnp.where(mask, x, packs[v])

    def gather(ref, row, stride, blocks):
        parts = [
            ref[pl.ds(row + stride * (w >> 1) + (w & 1) - b, 8), :] for b, w in enumerate(blocks)
        ]
        return jnp.where(even, parts[0], parts[1])

    def nearby(q, base):
        return [jnp.clip(near_ref[b, q - 1] - base, 0, 3) for b in range(2)]

    def present(q):
        return jnp.where(even, near_ref[0, q - 1], near_ref[1, q - 1]) >= 0

    def x_shift(r, cx):
        if cx == 0:
            return r
        moved = roll_rows(r, 2 * cx)
        return jnp.where(low, moved, r) if cx > 0 else jnp.where(low, r, moved)

    def local(a, q):
        cx, cy, cz = VEL[q]
        return x_shift(roll_lanes(a, 64 * abs(cx) + 8 * cy + cz), cx)

    def unpack(d, slot, tile, q):
        cx, cy, cz = VEL[q]
        m = slot % 8
        plus = d % 2 == 0
        if d // 2 == 0:
            t, h = m // 2, m % 2
            to_row, to_half = (0, 0) if plus else (3, 1)
            return roll_rows(roll_lanes(tile, 64 * (to_half - h) + 8 * cy + cz), 2 * (to_row - t))
        to = 0 if plus else 7
        if d // 2 == 1:
            return x_shift(roll_lanes(tile, 64 * abs(cx) + 8 * (to - m) + cz), cx)
        return x_shift(roll_lanes(tile, 64 * abs(cx) + 8 * cy + to - m), cx)

    def unpack_edge(d, slot, tile, q):
        cx, cy, cz = VEL[q]
        m = slot % 8
        to = 0 if d % 2 == 0 else 7
        shift = 8 * (to - m) if d // 2 == 1 else to - m
        if cx != 0:
            return roll_rows(roll_lanes(tile, shift + 64), -6 * cx)
        return roll_lanes(tile, shift - 56 * cy)

    def face_of(axis, sign):
        return 2 * axis + (0 if sign > 0 else 1)

    def edge_face(q):
        axis = 2 if VEL[q][2] != 0 else 1
        return face_of(axis, VEL[q][axis])

    def lo(axis, sign):
        return at[(axis, 0 if sign > 0 else 7)]

    def stream(a, q, slot_of, face_tile, edge_tile):
        out = a
        axes = [axis for axis in range(3) if VEL[q][axis] != 0]
        for axis in axes:
            d = face_of(axis, VEL[q][axis])
            slot = slot_of(d)
            out = jnp.where(
                lo(axis, VEL[q][axis]), unpack(d, slot, face_tile(d, slot // 8), q), out
            )
        if len(axes) == 2:
            d = edge_face(q)
            slot = slot_of(d)
            mask = lo(axes[0], VEL[q][axes[0]]) & lo(axes[1], VEL[q][axes[1]])
            out = jnp.where(mask, unpack_edge(d, slot, edge_tile(q), q), out)
        return out

    def mate_copy(n, ref, row, rows, h):
        span = pl.ds(row(h), rows)
        return pltpu.make_async_remote_copy(
            src_ref=ref.at[span],
            dst_ref=ref.at[span],
            send_sem=mate_send.at[n],
            recv_sem=mate_recv.at[n],
            device_id=device(mate),
            device_id_type=MESH,
        )

    def mate_copies(h):
        return (
            mate_copy(0, lat_0, lat_row, LAT_ROWS, h),
            mate_copy(1, own_z, lambda h: own_row(h, 0), 2 * Z_ROWS, h),
            mate_copy(2, lat_1, lat_row, LAT_ROWS, h),
        )

    def z_copy(n, way, h):
        src = (own_z.at[pl.ds(own_row(half, way), Z_ROWS)], psend.at[way])[n]
        dst = (
            zwin.at[pl.ds(z_row(way, half), Z_ROWS)],
            pwin.at[pl.ds(part_row(way, half), PART_ROWS)],
        )[n]
        return pltpu.make_async_remote_copy(
            src_ref=src,
            dst_ref=dst,
            send_sem=send_sem.at[n, 2 * way + h],
            recv_sem=recv_sem.at[n, 2 * way + half],
            device_id=device(2 * beyond(way) + h),
            device_id_type=MESH,
        )

    def z_in(n, way, h):
        src = (own_z.at[pl.ds(own_row(half, way), Z_ROWS)], psend.at[way])[n]
        dst = (
            zwin.at[pl.ds(z_row(way, h), Z_ROWS)],
            pwin.at[pl.ds(part_row(way, h), PART_ROWS)],
        )[n]
        return pltpu.make_async_remote_copy(
            src_ref=src,
            dst_ref=dst,
            send_sem=send_sem.at[n, 2 * way + h],
            recv_sem=recv_sem.at[n, 2 * way + h],
            device_id=device(2 * beyond(1 - way) + h),
            device_id_type=MESH,
        )

    def send_z(n):
        def do(way):
            for h in (half, 1 - half):
                z_copy(n, way, h).start()

        each_way(do)

    def receive_z(n):
        def do(way):
            for h in range(2):
                z_in(n, 1 - way, h).wait_recv()

        each_way(do)

    def collide_bin(n, g, conc, rate, lean4):
        part = (0.125 * rate) * conc
        keep = 1.0 - rate
        pg[7 * n] = keep * g[0] + (part + part)
        x4, y4, z4 = lean4
        for axis, u4 in ((0, x4), (1, y4 - 4.0 * settle_ref[n]), (2, z4)):
            lean = part * u4
            pg[7 * n + 1 + 2 * axis] = keep * g[1 + 2 * axis] + (part + lean)
            pg[7 * n + 2 + 2 * axis] = keep * g[2 + 2 * axis] + (part - lean)

    def collide_inputs():
        f = [fbuf[q] for q in range(19)]
        rho, vel = moments(f)
        target = equilibrium(OMEGA * rho, vel)
        for q in range(19):
            pf[q] = (1.0 - OMEGA) * f[q] + target[q]
        for copy in loads[2:]:
            copy.wait()
        lean4 = [4.0 * u for u in vel]
        for n in range(BINS):
            g = [gbuf[7 * n + i] for i in range(7)]
            collide_bin(n, g, add_up(g), rates_ref[n], lean4)

    def at_ends(vel):
        return [jnp.where(is_in, (0.0, 0.0, INLET)[axis], vel[axis]) for axis in range(3)]

    def collide_moved(flow, bins_of):
        rho, vel = moments(flow)
        vel = at_ends(vel)
        target = equilibrium(jnp.where(is_fluid, OMEGA * rho, 1.0), vel)
        keep = jnp.where(is_fluid, 1.0 - OMEGA, 0.0)
        for q in range(19):
            pf[q] = keep * flow[q] + target[q]
        lean4 = [4.0 * u for u in vel]
        for n in range(BINS):
            g = bins_of(n)
            conc = jnp.where(is_in, conc_ref[n], add_up(g))
            collide_bin(n, g, conc, jnp.where(is_fluid, rates_ref[n], 1.0), lean4)

    def pack_z(way):
        d = 4 + way
        packs = [None] * PACKS
        for s, q in enumerate(FACE_POPS[d]):
            put(packs, d, s, pf[q])
        put(packs, d, LIVE_SLOT, alive)
        for n in range(BINS):
            put(packs, d, BIN_SLOT + n, pg[7 * n + 1 + d])
        for v, tile in enumerate(packs):
            own_z[pl.ds(pl.multiple_of(own_row(half, way) + 8 * v, 8), 8), :] = tile

    def pack_lateral(ref):
        for axis in range(2):
            sides = []
            for d in (2 * axis, 2 * axis + 1):
                packs = [None] * PACKS
                for s, q in enumerate(FACE_POPS[d]):
                    put(packs, d, s, pf[q])
                put(packs, d, LIVE_SLOT, alive)
                for n in range(BINS):
                    put(packs, d, BIN_SLOT + n, pg[7 * n + 1 + d])
                sides.append(packs)
            ahead = present(1 + 2 * axis)
            row = lat_row(half) + 8 * PACKS * axis
            for v in range(PACKS):
                ref[pl.ds(pl.multiple_of(row + 8 * v, 8), 8), :] = jnp.where(
                    ahead, sides[0][v], sides[1][v]
                )

    def absent_as_zero(q, v, tile):
        return jnp.where(present(q), tile, 0.0) if v == 0 else tile

    def windows(lat, z_tile):
        memo = {}

        def tile_of(q, d, v):
            if (q, d, v) not in memo:
                if d >= 4:
                    tile = z_tile(q, d - 4, v)
                else:
                    row = lat_row(0) + 8 * (PACKS * (d // 2) + v)
                    tile = gather(lat, row, LAT_ROWS, nearby(q, 4 * layer))
                memo[(q, d, v)] = absent_as_zero(q, v, tile)
            return memo[(q, d, v)]

        return (
            lambda d, v: tile_of(OPP[1 + d], d, v),
            lambda q: tile_of(OPP[q], edge_face(q), 0),
        )

    def flow_slot(q):
        return lambda d: FACE_POPS[d].index(q)

    def bin_slot(n):
        return lambda d: BIN_SLOT + n

    def live_slot(d):
        return LIVE_SLOT

    def absorb(first):
        masks = [dmask_ref[i] > 0.5 for i in range(6)]
        for n in range(BINS):
            total = add_up([jnp.where(masks[i - 1], pg[7 * n + OPP[i]], 0.0) for i in range(1, 7)])
            dacc[n] = total if first else dacc[n] + total

    def finish(flow, bins_of):
        vel = at_ends(moments(flow)[1])
        target = equilibrium(jnp.ones_like(vel[0]), vel)
        for q in range(19):
            fbuf[q] = jnp.where(is_fluid, flow[q], jnp.where(is_end, target[q], fbuf[q]))
        x4, y4, z4 = [4.0 * u for u in vel]
        for n in range(BINS):
            g = bins_of(n)
            part = 0.125 * jnp.where(is_in, conc_ref[n], add_up(g))
            target = [part + part]
            for u4 in (x4, y4 - 4.0 * settle_ref[n], z4):
                lean = part * u4
                target += [part + lean, part - lean]
            for i in range(7):
                old = gbuf[7 * n + i]
                gbuf[7 * n + i] = jnp.where(is_fluid, g[i], jnp.where(is_end, target[i], old))

    def move_inside():
        for q in range(1, 19):
            sf[q] = local(pf[q], q)
        for n in range(BINS):
            for i in range(1, 7):
                sg[6 * n + i - 1] = local(pg[7 * n + i], i)

    collide_inputs()
    for way in range(2):
        pack_z(way)
    pack_lateral(lat_0)
    ends = jnp.where(layer < layers - 1, 1, 0) + jnp.where(layer > 0, 1, 0)
    pl.semaphore_wait(barrier, 1 + 2 * ends)
    out_1, out_z, out_2 = mate_copies(half)
    in_1, in_z, in_2 = mate_copies(1 - half)
    out_1.start()
    send_z(0)
    move_inside()

    def z_tile(q, way, v):
        base = 4 * layer + (-4 if way == 0 else 4)
        return gather(zwin, z_row(way, 0) + 8 * v, Z_ROWS, nearby(q, base))

    in_1.wait_recv()
    face_tile, edge_tile = windows(lat_0, z_tile)

    def within(a, q, slot_of):
        out = a
        axes = [axis for axis in range(2) if VEL[q][axis] != 0]
        for axis in axes:
            d = face_of(axis, VEL[q][axis])
            moved = unpack(d, slot_of(d), face_tile(d, slot_of(d) // 8), q)
            out = jnp.where(lo(axis, VEL[q][axis]), moved, out)
        if len(axes) == 2:
            d = edge_face(q)
            mask = lo(0, VEL[q][0]) & lo(1, VEL[q][1])
            out = jnp.where(mask, unpack_edge(d, slot_of(d), edge_tile(q), q), out)
        return out

    def across(a, q, slot_of):
        cx, cy, cz = VEL[q]
        if cz == 0:
            return a
        d = face_of(2, cz)
        slot = slot_of(d)
        moved = unpack(d, slot, face_tile(d, slot // 8), q)
        for axis in range(2):
            if VEL[q][axis] != 0:
                moved = jnp.where(
                    lo(axis, VEL[q][axis]), unpack_edge(d, slot, edge_tile(q), q), moved
                )
        return jnp.where(lo(2, cz), moved, a)

    flow = [pf[0]]
    for q in range(1, 19):
        lq = within(local(alive, q), q, live_slot)
        live_ref[q - 1] = lq
        flow.append(jnp.where(lq > 0.5, within(sf[q], q, flow_slot(q)), pf[OPP[q]]))
        sf[q] = flow[q]

    def total(rows, pick):
        return add_up([rows[q] for q in range(len(rows)) if pick(VEL[q])])

    level_sum = [
        total(flow, lambda c: c[2] == 0),
        total(flow, lambda c: c[0] == 1 and c[2] == 0)
        - total(flow, lambda c: c[0] == -1 and c[2] == 0),
        total(flow, lambda c: c[1] == 1 and c[2] == 0)
        - total(flow, lambda c: c[1] == -1 and c[2] == 0),
    ]
    parts = [[None] * PART for way in range(2)]

    def put_part(way, tile, m, x):
        packs = [None] * PART
        packs[tile] = parts[way][tile]
        put(packs, 4 + way, 8 * tile + m, x)
        parts[way][tile] = packs[tile]

    for way in range(2):
        rows = FACE_POPS[4 + way]
        for s, q in enumerate(rows):
            put_part(way, 0, s, flow[q])
        out_sum = add_up([flow[q] for q in rows])
        put_part(way, 0, LIVE_SLOT, level_sum[0] + out_sum)
        put_part(way, 3, 4, out_sum)
        x_sum = flow[rows[slot_at(4 + way, (1, 0))]] - flow[rows[slot_at(4 + way, (-1, 0))]]
        y_sum = flow[rows[slot_at(4 + way, (0, 1))]] - flow[rows[slot_at(4 + way, (0, -1))]]
        put_part(way, 3, 2, level_sum[1] + x_sum)
        put_part(way, 3, 3, level_sum[2] + y_sum)
    for n in range(BINS):
        g = [pg[7 * n]]
        for i in range(1, 7):
            moved = within(sg[6 * n + i - 1], i, bin_slot(n))
            g.append(jnp.where(live_ref[i - 1] > 0.5, moved, 0.0))
            sg[6 * n + i - 1] = g[i]
        flat = add_up(g[:5])
        v, m = (BIN_SLOT + n) // 8, (BIN_SLOT + n) % 8
        for way in range(2):
            put_part(way, v, m, g[5 + way])
            put_part(way, 4 if v == 1 else 3, m, flat + g[5 + way])
    for way in range(2):
        for v in range(PART):
            psend[way, pl.ds(8 * v, 8), :] = parts[way][v]
    send_z(1)
    out_z.start()

    receive_z(0)
    new = [pf[0]]
    for q in range(1, 19):
        if VEL[q][2] == 0:
            new.append(sf[q])
            continue
        lq = across(live_ref[q - 1], q, live_slot)
        live_ref[q - 1] = lq
        border = lo(2, VEL[q][2])
        moved = across(sf[q], q, flow_slot(q))
        new.append(jnp.where(border & (lq < 0.5), pf[OPP[q]], moved))
    for i in range(1, 7):
        dmask_ref[i - 1] = jnp.where(is_fluid & (live_ref[i - 1] < 0.5), 1.0, 0.0)
    absorb(True)

    def bins_across(n):
        new = [pg[7 * n]] + [sg[6 * n + i] for i in range(4)]
        for i in (5, 6):
            moved = across(sg[6 * n + i - 1], i, bin_slot(n))
            new.append(jnp.where(live_ref[i - 1] > 0.5, moved, 0.0))
        return new

    collide_moved(new, bins_across)
    pack_lateral(lat_1)
    out_2.start()
    move_inside()
    absorb(False)
    table = jnp.zeros((8, 128), jnp.float32)
    for n in range(BINS):
        table = jnp.where(lane == n, jnp.sum(dacc[n], axis=1, keepdims=True), table)
    table = table + roll_rows(table, 2)
    table = table + roll_rows(table, 4)
    dep_ref[...] = table[:2, :BINS]

    place = [
        (
            jnp.where(near_ref[b, 1] >= 0, 1, 0),
            jnp.where(near_ref[b, 3] >= 0, 1, 0),
        )
        for b in range(2)
    ]

    def blocks_by_place(dz, base):
        def pick(wanted):
            ids = [near_ref[0, VEL.index(c) - 1] for c in wanted]
            return jnp.clip(functools.reduce(jnp.maximum, ids) - base, 0, 3)

        here = 2 * half if dz == 0 else pick([(0, 0, dz)])
        along_x = pick([(1, 0, dz), (-1, 0, dz)])
        along_y = pick([(0, 1, dz), (0, -1, dz)])
        last = jnp.clip(6 - here - along_x - along_y, 0, 3)
        px, py = place[0]
        return [
            [
                jnp.where(
                    px == x, jnp.where(py == y, here, along_y), jnp.where(py == y, along_x, last)
                )
                for y in range(2)
            ]
            for x in range(2)
        ]

    in_z.wait_recv()
    mine = blocks_by_place(0, 4 * layer)
    theirs = [blocks_by_place(-1, 4 * layer - 4), blocks_by_place(1, 4 * layer + 4)]
    spots = [(way, y) for way in range(2) for y in range(2)]

    def column(ids, y):
        return [ids[0][y], ids[1][y]]

    arriving, leaving = {}, {}
    for way, y in spots:
        for v in range(PACKS):
            row = own_row(0, 1 - way) + 8 * v
            arriving[way, y, v] = gather(own_z, row, 2 * Z_ROWS, column(mine, y))
        leaving[way, y] = gather(zwin, z_row(way, 0), Z_ROWS, column(theirs[way], y))

    def plane(tile_at, slot_of_way):
        out = None
        for way, y in spots:
            s = 2 * way + y
            moved = roll_lanes(tile_at(way, y), s - slot_of_way(way))
            out = moved if out is None else jnp.where(kk == s, moved, out)
        return out

    at_y = kk & 1

    def plane_shift(x, lateral):
        cx, cy = lateral
        if cx != 0:
            turned = roll_lanes(x, 64)
            edge = lo(0, cx)
            inner = edge & (~even if cx > 0 else even)
            out = jnp.where(inner, roll_rows(turned, 3 * cx), x_shift(turned, cx))
            return out, edge & (even if cx > 0 else ~even)
        if cy != 0:
            edge = lo(1, cy)
            inner = edge & ((at_y == 1) if cy > 0 else (at_y == 0))
            out = jnp.where(inner, roll_lanes(x, -55 * cy), roll_lanes(x, 8 * cy))
            return out, edge & ((at_y == 0) if cy > 0 else (at_y == 1))
        return x, None

    def back(lateral):
        return (-lateral[0], -lateral[1])

    def spread(x, m):
        out = x
        for other in range(8):
            if other != m:
                out = jnp.where(kk == other, roll_lanes(x, other - m), out)
        return out

    source_live = plane(lambda way, y: arriving[way, y, 0], lambda way: LIVE_SLOT)
    came = {}
    for c in LATERAL:
        x = plane(lambda way, y: arriving[way, y, 0], lambda way: slot_at(5 - way, c))
        bounce = plane(lambda way, y: leaving[way, y], lambda way: slot_at(4 + way, back(c)))
        moved, outside = plane_shift(x, c)
        lives, _ = plane_shift(source_live, c)
        lives = lives > 0.5
        if outside is not None:
            lives = lives & ~outside
        came[c] = jnp.where(lives, moved, bounce)
    sums = (
        add_up(came.values()),
        came[1, 0] - came[-1, 0],
        came[0, 1] - came[0, -1],
    )
    for n, (way, y) in enumerate(spots):
        s = 2 * way + y
        for t in range(3):
            came_ref[3 * n + t] = spread(sums[t], s)
        lives = spread(source_live, s) > 0.5
        for v in range(PACKS):
            came_ref[12 + PACKS * n + v] = jnp.where(lives, arriving[way, y, v], 0.0)

    def by_slot(value_of):
        row = jnp.zeros((8, 128), jnp.float32)
        for m in range(8):
            if value_of(m) is not None:
                row = jnp.where(kk == m, value_of(m), row)
        return row

    rate_rows = []
    for v in range(PACKS):
        bins = [8 * v + m - BIN_SLOT for m in range(8)]
        rate_rows.append(by_slot(lambda m: rates_ref[bins[m]] if 0 <= bins[m] < BINS else None))
    weights = by_slot(lambda m: OMEGA * (WEIGHT[1] if m == 0 else WEIGHT[7]) if m < 5 else None)
    leans = [
        [
            by_slot(lambda m: float(VEL[FACE_POPS[4 + way][m]][axis]) if m < 5 else None)
            for axis in range(2)
        ]
        for way in range(2)
    ]

    receive_z(1)
    for n, (way, y) in enumerate(spots):
        partial = [
            gather(pwin, part_row(way, 0) + 8 * v, PART_ROWS, column(theirs[way], y))
            for v in range(PART)
        ]
        came_sum, came_x, came_y = [came_ref[3 * n + t] for t in range(3)]
        rho = spread(partial[0], LIVE_SLOT) + came_sum
        inv = 1.0 / rho
        ux = (spread(partial[3], 2) + came_x) * inv
        uy = (spread(partial[3], 3) + came_y) * inv
        un = (spread(partial[3], 4) - came_sum) * inv
        along = un + leans[way][0] * ux + leans[way][1] * uy
        still = 1.0 - 1.5 * (ux * ux + uy * uy + un * un)
        feq = (weights * rho) * (still + 3.0 * along + 4.5 * along * along)
        lean = 1.0 + 4.0 * un
        for v in range(PACKS):
            conc = partial[4 if v == 1 else 3] + came_ref[12 + PACKS * n + v]
            rate = rate_rows[v]
            tile = (1.0 - rate) * partial[v] + (0.125 * rate) * conc * lean
            if v == 0:
                tile = jnp.where(kk < 5, (1.0 - OMEGA) * partial[0] + feq, tile)
            ghost[pl.ds(z_row(way, y) + 8 * v, 8), :] = tile

    def ghost_tile(q, way, v):
        cx, cy, cz = VEL[q]
        blocks = []
        for px, py in place:
            blocks.append(2 * (1 - py if cy != 0 else py) + (1 - px if cx != 0 else px))
        return gather(ghost, z_row(way, 0) + 8 * v, Z_ROWS, blocks)

    in_2.wait_recv()
    face_tile, edge_tile = windows(lat_1, ghost_tile)
    new = [pf[0]]
    for q in range(1, 19):
        moved = stream(sf[q], q, flow_slot(q), face_tile, edge_tile)
        new.append(jnp.where(live_ref[q - 1] > 0.5, moved, pf[OPP[q]]))

    def bins_moved(n):
        new = [pg[7 * n]]
        for i in range(1, 7):
            moved = stream(sg[6 * n + i - 1], i, bin_slot(n), face_tile, edge_tile)
            new.append(jnp.where(live_ref[i - 1] > 0.5, moved, 0.0))
        return new

    finish(new, bins_moved)

    for copy in (out_1, out_z, out_2):
        copy.wait_send()

    def sent(way):
        for n in range(2):
            for h in range(2):
                z_copy(n, way, h).wait_send()

    each_way(sent)


def write_out(flow, bins, deposit, flow_out, bins_out, dep_out, sem):
    pairs = [(bins, bins_out), (flow, flow_out), (deposit, dep_out)]
    copies = [pltpu.make_async_copy(a, b, sem.at[n]) for n, (a, b) in enumerate(pairs)]
    for copy in copies:
        copy.start()
    for copy in copies:
        copy.wait()


def tiled(x):
    x = x.reshape(2, -1, 4, 128)
    return x.transpose(1, 2, 0, 3).reshape(-1, 8, 128)


def untiled(x):
    return x.reshape(-1, 4, 2, 128).transpose(2, 0, 1, 3).reshape(2, -1, 512)


def on_device(flow_pops, bin_pops, site_kind, neighbours, bin_rates, settle, inlet_conc):
    subs = lax.axis_size("sub")
    layers = lax.axis_size("dom") * subs // 2
    hbm = pl.BlockSpec(memory_space=pltpu.HBM)
    vmem = pl.BlockSpec(memory_space=pltpu.VMEM)
    f32 = jnp.float32
    shapes = (
        jax.ShapeDtypeStruct((19, 8, 128), f32),
        jax.ShapeDtypeStruct((7 * BINS, 8, 128), f32),
        jax.ShapeDtypeStruct((2, BINS), f32),
    )
    done = pl.pallas_call(
        functools.partial(kernel, layers, subs),
        out_shape=shapes,
        in_specs=[hbm] * 7,
        out_specs=(vmem, vmem, vmem),
        scratch_shapes=[
            pltpu.VMEM((8, 128), jnp.int32),
            pltpu.SMEM((2, 18), jnp.int32),
            pltpu.SMEM((BINS,), f32),
            pltpu.SMEM((BINS,), f32),
            pltpu.SMEM((BINS,), f32),
            pltpu.VMEM((19, 8, 128), f32),
            pltpu.VMEM((7 * BINS, 8, 128), f32),
            pltpu.VMEM((19, 8, 128), f32),
            pltpu.VMEM((6 * BINS, 8, 128), f32),
            pltpu.VMEM((18, 8, 128), f32),
            pltpu.VMEM((6, 8, 128), f32),
            pltpu.VMEM((BINS, 8, 128), f32),
            pltpu.VMEM((lat_row(2) + 8, 128), f32),
            pltpu.VMEM((lat_row(2) + 8, 128), f32),
            pltpu.VMEM((own_row(2, 0) + 8, 128), f32),
            pltpu.VMEM((z_row(2, 0) + 8, 128), f32),
            pltpu.VMEM((part_row(2, 0) + 8, 128), f32),
            pltpu.VMEM((2, PART_ROWS, 128), f32),
            pltpu.VMEM((z_row(2, 0) + 8, 128), f32),
            pltpu.VMEM((12 + 4 * PACKS, 8, 128), f32),
            pltpu.SemaphoreType.DMA((7,)),
            pltpu.SemaphoreType.DMA((2, 4)),
            pltpu.SemaphoreType.DMA((2, 4)),
            pltpu.SemaphoreType.DMA((3,)),
            pltpu.SemaphoreType.DMA((3,)),
        ],
        compiler_params=pltpu.CompilerParams(
            collective_id=0, has_side_effects=True, vmem_limit_bytes=16 * 1024 * 1024
        ),
    )(
        *[
            pltpu.with_memory_space_constraint(x, pltpu.HBM)
            for x in (
                tiled(flow_pops),
                tiled(bin_pops),
                tiled(site_kind)[0],
                neighbours,
                bin_rates,
                settle,
                inlet_conc,
            )
        ]
    )
    flow, bins, deposit = pl.pallas_call(
        write_out,
        out_shape=shapes,
        in_specs=[vmem, vmem, vmem],
        out_specs=(hbm, hbm, hbm),
        scratch_shapes=[pltpu.SemaphoreType.DMA((3,))],
        compiler_params=pltpu.CompilerParams(vmem_limit_bytes=16 * 1024 * 1024),
    )(*done)
    return untiled(flow), untiled(bins), deposit


def solution(mesh):
    cut = ("dom", "sub")
    return jax.shard_map(
        on_device,
        mesh=mesh,
        in_specs=(P(cut, None, None), P(cut, None, None), P(cut, None), P(cut, None), P(), P(), P()),
        out_specs=(P(cut, None, None), P(cut, None, None), P(cut, None)),
        check_vma=False,
    )
```

```python
import functools

import jax
import jax.numpy as jnp
from jax import lax
from jax.experimental import pallas as pl
from jax.experimental.pallas import tpu as pltpu
from jax.sharding import PartitionSpec as P

VEL = [
    (0, 0, 0),
    (1, 0, 0),
    (-1, 0, 0),
    (0, 1, 0),
    (0, -1, 0),
    (0, 0, 1),
    (0, 0, -1),
    (1, 1, 0),
    (-1, -1, 0),
    (1, -1, 0),
    (-1, 1, 0),
    (1, 0, 1),
    (-1, 0, -1),
    (1, 0, -1),
    (-1, 0, 1),
    (0, 1, 1),
    (0, -1, -1),
    (0, 1, -1),
    (0, -1, 1),
]
WEIGHT = [1.0 / 3.0] + [1.0 / 18.0] * 6 + [1.0 / 36.0] * 12
OPP = [0, 2, 1, 4, 3, 6, 5, 8, 7, 10, 9, 12, 11, 14, 13, 16, 15, 18, 17]
OMEGA = 1.6
INLET = 0.04
BINS = 12
MESH = pl.DeviceIdType.MESH

FACE_POPS = [
    [q for q in range(1, 19) if VEL[q][d // 2] == 1 - 2 * (d % 2)] for d in range(6)
]
LIVE_SLOT = 5
BIN_SLOT = 6
PACKS = 3
PART = 5
LAT_ROWS, Z_ROWS, PART_ROWS = 2 * PACKS * 8, PACKS * 8, PART * 8
LATERAL = [(0, 0), (1, 0), (-1, 0), (0, 1), (0, -1)]


def lat_row(h):
    return 8 + LAT_ROWS * h


def own_row(h, way):
    return 8 + Z_ROWS * (2 * h + way)


def z_row(h):
    return 8 + Z_ROWS * h


def part_row(h):
    return 8 + PART_ROWS * h


def slot_at(d, lateral):
    return [VEL[q][:2] for q in FACE_POPS[d]].index(lateral)


def add_up(terms):
    terms = list(terms)
    while len(terms) > 1:
        pairs = [a + b for a, b in zip(terms[::2], terms[1::2])]
        terms = pairs + terms[len(pairs) * 2 :]
    return terms[0]


def roll_lanes(x, shift):
    shift %= 128
    return x if shift == 0 else pltpu.roll(x, shift, 1)


def roll_rows(x, shift):
    shift %= 8
    return x if shift == 0 else pltpu.roll(x, shift, 0)


def kernel(
    layers,
    subs,
    flow_in,
    bins_in,
    kind_in,
    near_in,
    rates_in,
    settle_in,
    conc_in,
    fbuf,
    gbuf,
    dep_ref,
    kind_ref,
    near_ref,
    rates_ref,
    settle_ref,
    conc_ref,
    pf,
    pg_0,
    pg,
    sf,
    sg,
    live_ref,
    dmask_ref,
    dacc,
    lat_0,
    lat_1,
    own_z,
    zwin_0,
    zwin_1,
    pwin_0,
    pwin_1,
    psend,
    ghost_0,
    ghost_1,
    came_ref,
    in_sem,
    send_sem,
    recv_sem,
    mate_send,
    mate_recv,
):
    zwin, pwin, ghost = (zwin_0, zwin_1), (pwin_0, pwin_1), (ghost_0, ghost_1)
    me = lax.axis_index("dom") * subs + lax.axis_index("sub")
    layer = me // 2
    half = me % 2
    mate = 2 * layer + 1 - half
    far = 1 - (me % subs) // 2

    def device(g):
        return (g // subs, g % subs)

    def beyond(way):
        return layer + 1 - 2 * way

    def each_way(do):
        for order in ((0, 1), (1, 0)):

            @pl.when(far == order[0])
            def _():
                for way in order:
                    there = beyond(way)
                    pl.when((there >= 0) & (there < layers))(functools.partial(do, way))

    barrier = pltpu.get_barrier_semaphore()

    def greet(way):
        for h in range(2):
            pl.semaphore_signal(
                barrier, inc=1, device_id=device(2 * beyond(way) + h), device_id_type=MESH
            )

    each_way(greet)
    pl.semaphore_signal(barrier, inc=1, device_id=device(mate), device_id_type=MESH)

    pairs = [
        (flow_in, fbuf),
        (kind_in, kind_ref),
        (bins_in, gbuf),
        (rates_in, rates_ref),
        (settle_in, settle_ref),
        (conc_in, conc_ref),
        (near_in, near_ref),
    ]
    loads = [pltpu.make_async_copy(a, b, in_sem.at[n]) for n, (a, b) in enumerate(pairs)]
    for copy in loads:
        copy.start()

    sub = lax.broadcasted_iota(jnp.int32, (8, 128), 0)
    lane = lax.broadcasted_iota(jnp.int32, (8, 128), 1)
    jj = (lane >> 3) & 7
    kk = lane & 7
    low = lane < 64
    even = (sub & 1) == 0
    quarter = sub >> 1
    at = {
        (0, 0): (quarter == 0) & low,
        (0, 7): (quarter == 3) & (lane >= 64),
        (1, 0): jj == 0,
        (1, 7): jj == 7,
        (2, 0): kk == 0,
        (2, 7): kk == 7,
    }

    loads[0].wait()
    loads[1].wait()
    kind = kind_ref[...]
    alive = jnp.where(kind > 0, 1.0, 0.0)
    is_in = kind == 2
    is_end = kind >= 2
    is_fluid = kind == 1

    def moments(f):
        odd = range(1, 19, 2)
        rho = add_up([f[q] + f[q + 1] for q in odd] + [f[0]])
        inv = 1.0 / rho
        gaps = {q: f[q] - f[q + 1] for q in odd}
        vel = []
        for axis in range(3):
            plus = add_up([gaps[q] for q in odd if VEL[q][axis] == 1])
            minus = [gaps[q] for q in odd if VEL[q][axis] == -1]
            vel.append((plus - add_up(minus) if minus else plus) * inv)
        return rho, vel

    def equilibrium(scale, vel):
        base = 1.0 - 1.5 * (vel[0] * vel[0] + vel[1] * vel[1] + vel[2] * vel[2])
        scaled = {w: scale * w for w in set(WEIGHT)}
        out = [None] * 19
        out[0] = scaled[WEIGHT[0]] * base
        for q in range(1, 19, 2):
            along = None
            for axis in range(3):
                if VEL[q][axis] != 0:
                    term = vel[axis]
                    if along is None:
                        along = term if VEL[q][axis] > 0 else -term
                    else:
                        along = along + term if VEL[q][axis] > 0 else along - term
            even = base + 4.5 * along * along
            odd = 3.0 * along
            out[q] = scaled[WEIGHT[q]] * (even + odd)
            out[q + 1] = scaled[WEIGHT[q]] * (even - odd)
        return out

    def put(packs, d, slot, x):
        v, m = slot // 8, slot % 8
        x = roll_lanes(x, m - (0 if d % 2 else 7))
        packs[v] = x if packs[v] is None else jnp.where(kk == m, x, packs[v])

    def gather(ref, row, stride, blocks):
        parts = [
            ref[pl.ds(row + stride * (w >> 1) + (w & 1) - b, 8), :] for b, w in enumerate(blocks)
        ]
        return jnp.where(even, parts[0], parts[1])

    def nearby(q, base):
        return [jnp.clip(near_ref[b, q - 1] - base, 0, 3) for b in range(2)]

    def present(q):
        return jnp.where(even, near_ref[0, q - 1], near_ref[1, q - 1]) >= 0

    def x_shift(r, cx):
        if cx == 0:
            return r
        moved = roll_rows(r, 2 * cx)
        return jnp.where(low, moved, r) if cx > 0 else jnp.where(low, r, moved)

    def local(a, q):
        cx, cy, cz = VEL[q]
        return x_shift(roll_lanes(a, 64 * abs(cx) + 8 * cy + cz), cx)

    def unpack(d, slot, tile, q):
        cx, cy, cz = VEL[q]
        m = slot % 8
        if d // 2 == 0:
            t, h = m // 2, m % 2
            turned = roll_lanes(tile, 64 * h + 8 * cy + cz)
            return roll_rows(turned, -2 * t if d % 2 == 0 else 4 - 2 * t)
        if d // 2 == 1:
            return x_shift(roll_lanes(tile, 64 * abs(cx) - 8 * m + (112 if d % 2 else 0) + cz), cx)
        return x_shift(roll_lanes(tile, 64 * abs(cx) + 8 * cy + (7 if d % 2 else 0) - m), cx)

    def unpack_edge(d, slot, tile, q):
        cx, cy, cz = VEL[q]
        m = slot % 8
        if d // 2 == 1:
            shift = (112 if d % 2 else 0) - 8 * m
        else:
            shift = (7 if d % 2 else 0) - m
        if cx != 0:
            return roll_rows(roll_lanes(tile, shift + 64), -6 * cx)
        return roll_lanes(tile, shift - 56 * cy)

    def face_of(axis, sign):
        return 2 * axis + (0 if sign > 0 else 1)

    def edge_face(q):
        axis = 2 if VEL[q][2] != 0 else 1
        return face_of(axis, VEL[q][axis])

    def lo(axis, sign):
        return at[(axis, 0 if sign > 0 else 7)]

    def mate_copy(n, ref, row, rows, h):
        span = pl.ds(row(h), rows)
        return pltpu.make_async_remote_copy(
            src_ref=ref.at[span],
            dst_ref=ref.at[span],
            send_sem=mate_send.at[n],
            recv_sem=mate_recv.at[n],
            device_id=device(mate),
            device_id_type=MESH,
        )

    def mate_copies(h):
        return (
            mate_copy(0, lat_0, lat_row, LAT_ROWS, h),
            mate_copy(1, own_z, lambda h: own_row(h, 0), 2 * Z_ROWS, h),
            mate_copy(2, lat_1, lat_row, LAT_ROWS // 2, h),
            mate_copy(3, lat_1, lambda h: lat_row(h) + LAT_ROWS // 2, LAT_ROWS // 2, h),
        )

    def z_copy(n, way, h):
        src = (own_z.at[pl.ds(own_row(half, way), Z_ROWS)], psend.at[way])[n]
        dst = (
            zwin[way].at[pl.ds(z_row(half), Z_ROWS)],
            pwin[way].at[pl.ds(part_row(half), PART_ROWS)],
        )[n]
        return pltpu.make_async_remote_copy(
            src_ref=src,
            dst_ref=dst,
            send_sem=send_sem.at[n, 2 * way + h],
            recv_sem=recv_sem.at[n, 2 * way + half],
            device_id=device(2 * beyond(way) + h),
            device_id_type=MESH,
        )

    def z_in(n, way, h):
        src = (own_z.at[pl.ds(own_row(half, way), Z_ROWS)], psend.at[way])[n]
        dst = (
            zwin[way].at[pl.ds(z_row(h), Z_ROWS)],
            pwin[way].at[pl.ds(part_row(h), PART_ROWS)],
        )[n]
        return pltpu.make_async_remote_copy(
            src_ref=src,
            dst_ref=dst,
            send_sem=send_sem.at[n, 2 * way + h],
            recv_sem=recv_sem.at[n, 2 * way + h],
            device_id=device(2 * beyond(1 - way) + h),
            device_id_type=MESH,
        )

    def send_z(n):
        def do(way):
            for h in (half, 1 - half):
                z_copy(n, way, h).start()

        each_way(do)

    def receive_z(n, side):
        @pl.when(layer > 0 if side == 0 else layer < layers - 1)
        def _():
            for h in range(2):
                z_in(n, side, h).wait_recv()

    def nearer_first(do):
        for order in ((0, 1), (1, 0)):

            @pl.when(far == order[0])
            def _():
                for side in order:
                    do(side)

    def from_side(side):
        return [q for q in range(1, 19) if VEL[q][2] == 1 - 2 * side]

    def collide_bin(pg, n, g, conc, rate, lean4):
        part = (0.125 * rate) * conc
        keep = 1.0 - rate
        pg[7 * n] = keep * g[0] + (part + part)
        x4, y4, z4 = lean4
        for axis, u4 in ((0, x4), (1, y4 - 4.0 * settle_ref[n]), (2, z4)):
            lean = part * u4
            pg[7 * n + 1 + 2 * axis] = keep * g[1 + 2 * axis] + (part + lean)
            pg[7 * n + 2 + 2 * axis] = keep * g[2 + 2 * axis] + (part - lean)

    def collide_inputs():
        f = [fbuf[q] for q in range(19)]
        rho, vel = moments(f)
        target = equilibrium(OMEGA * rho, vel)
        for q in range(19):
            pf[q] = (1.0 - OMEGA) * f[q] + target[q]
        for copy in loads[2:]:
            copy.wait()
        lean4 = [4.0 * u for u in vel]
        for n in range(BINS):
            g = [gbuf[7 * n + i] for i in range(7)]
            collide_bin(pg_0, n, g, add_up(g), rates_ref[n], lean4)

    def at_ends(vel):
        return [jnp.where(is_in, (0.0, 0.0, INLET)[axis], vel[axis]) for axis in range(3)]

    def collide_moved(flow, bins_of):
        rho, vel = moments(flow)
        vel = at_ends(vel)
        target = equilibrium(jnp.where(is_fluid, OMEGA * rho, 1.0), vel)
        keep = jnp.where(is_fluid, 1.0 - OMEGA, 0.0)
        for q in range(19):
            pf[q] = keep * flow[q] + target[q]
        lean4 = [4.0 * u for u in vel]
        for n in range(BINS):
            g = bins_of(n)
            conc = jnp.where(is_in, conc_ref[n], add_up(g))
            collide_bin(pg, n, g, conc, jnp.where(is_fluid, rates_ref[n], 1.0), lean4)

    def pack_z(way):
        d = 4 + way
        packs = [None] * PACKS
        for s, q in enumerate(FACE_POPS[d]):
            put(packs, d, s, pf[q])
        put(packs, d, LIVE_SLOT, alive)
        for n in range(BINS):
            put(packs, d, BIN_SLOT + n, pg_0[7 * n + 1 + d])
        for v, tile in enumerate(packs):
            own_z[pl.ds(pl.multiple_of(own_row(half, way) + 8 * v, 8), 8), :] = tile

    def pack_lateral(ref, axis, pg):
        ahead = present(1 + 2 * axis)
        if axis == 0:
            spot = 2 * quarter + jnp.where(low, 0, 1)
            spot = jnp.where(ahead, spot, 2 * ((quarter + 3) & 3) + jnp.where(low, 1, 0))
        else:
            spot = jnp.where(ahead, jj, (jj + 7) & 7)
        packs = [None] * PACKS
        rows = [(pf[q], pf[r]) for q, r in zip(FACE_POPS[2 * axis], FACE_POPS[2 * axis + 1])]
        rows.append((alive, alive))
        for n in range(BINS):
            rows.append((pg[7 * n + 1 + 2 * axis], pg[7 * n + 2 + 2 * axis]))
        for slot, (x, y) in enumerate(rows):
            v, m = slot // 8, slot % 8
            x = jnp.where(ahead, x, y)
            if axis == 0:
                x = roll_rows(roll_lanes(x, 64 * (m % 2 - 1)), 2 * (m // 2 - 3))
            else:
                x = roll_lanes(x, 8 * (m - 7))
            packs[v] = x if packs[v] is None else jnp.where(spot == m, x, packs[v])
        row = lat_row(half) + 8 * PACKS * axis
        for v in range(PACKS):
            ref[pl.ds(pl.multiple_of(row + 8 * v, 8), 8), :] = packs[v]

    def absent_as_zero(q, v, tile):
        return jnp.where(present(q), tile, 0.0) if v == 0 else tile

    def windows(lat, z_tile):
        memo = {}

        def tile_of(q, d, v):
            if (q, d, v) not in memo:
                if d >= 4:
                    tile = z_tile(q, d - 4, v)
                else:
                    row = lat_row(0) + 8 * (PACKS * (d // 2) + v)
                    tile = gather(lat, row, LAT_ROWS, nearby(q, 4 * layer))
                memo[(q, d, v)] = absent_as_zero(q, v, tile)
            return memo[(q, d, v)]

        return (
            lambda d, v: tile_of(OPP[1 + d], d, v),
            lambda q: tile_of(OPP[q], edge_face(q), 0),
        )

    def flow_slot(q):
        return lambda d: FACE_POPS[d].index(q)

    def bin_slot(n):
        return lambda d: BIN_SLOT + n

    def live_slot(d):
        return LIVE_SLOT

    def absorb(first, pg):
        masks = [dmask_ref[i] > 0.5 for i in range(6)]
        for n in range(BINS):
            total = add_up([jnp.where(masks[i - 1], pg[7 * n + OPP[i]], 0.0) for i in range(1, 7)])
            dacc[n] = total if first else dacc[n] + total

    def finish(flow, bins_of):
        vel = at_ends(moments(flow)[1])
        target = equilibrium(jnp.ones_like(vel[0]), vel)
        for q in range(19):
            fbuf[q] = jnp.where(is_fluid, flow[q], jnp.where(is_end, target[q], fbuf[q]))
        x4, y4, z4 = [4.0 * u for u in vel]
        for n in range(BINS):
            g = bins_of(n)
            part = 0.125 * jnp.where(is_in, conc_ref[n], add_up(g))
            target = [part + part]
            for u4 in (x4, y4 - 4.0 * settle_ref[n], z4):
                lean = part * u4
                target += [part + lean, part - lean]
            for i in range(7):
                old = gbuf[7 * n + i]
                gbuf[7 * n + i] = jnp.where(is_fluid, g[i], jnp.where(is_end, target[i], old))

    def move_inside(pg):
        for q in range(1, 19):
            sf[q] = local(pf[q], q)
        for n in range(BINS):
            for i in range(1, 7):
                sg[6 * n + i - 1] = local(pg[7 * n + i], i)

    collide_inputs()
    for way in range(2):
        pack_z(way)
    pack_lateral(lat_0, 0, pg_0)
    pack_lateral(lat_0, 1, pg_0)
    ends = jnp.where(layer < layers - 1, 1, 0) + jnp.where(layer > 0, 1, 0)
    pl.semaphore_wait(barrier, 1 + 2 * ends)
    out_1, out_z, out_2, out_3 = mate_copies(half)
    in_1, in_z, in_2, in_3 = mate_copies(1 - half)
    out_1.start()
    send_z(0)
    move_inside(pg_0)
    for q in range(1, 19):
        live_ref[q - 1] = local(alive, q)

    def z_tile(q, way, v):
        base = 4 * layer + (-4 if way == 0 else 4)
        return gather(zwin[way], z_row(0) + 8 * v, Z_ROWS, nearby(q, base))

    in_1.wait_recv()
    face_tile, edge_tile = windows(lat_0, z_tile)

    def within(a, q, slot_of):
        out = a
        axes = [axis for axis in range(2) if VEL[q][axis] != 0]
        for axis in axes:
            d = face_of(axis, VEL[q][axis])
            moved = unpack(d, slot_of(d), face_tile(d, slot_of(d) // 8), q)
            mask = lo(axis, VEL[q][axis])
            if VEL[q][2] != 0:
                mask = mask & ~lo(2, VEL[q][2])
            out = jnp.where(mask, moved, out)
        if len(axes) == 2:
            d = edge_face(q)
            mask = lo(0, VEL[q][0]) & lo(1, VEL[q][1])
            out = jnp.where(mask, unpack_edge(d, slot_of(d), edge_tile(q), q), out)
        return out

    def across(a, q, slot_of):
        cx, cy, cz = VEL[q]
        if cz == 0:
            return a
        d = face_of(2, cz)
        slot = slot_of(d)
        moved = unpack(d, slot, face_tile(d, slot // 8), q)
        for axis in range(2):
            if VEL[q][axis] != 0:
                moved = jnp.where(
                    lo(axis, VEL[q][axis]), unpack_edge(d, slot, edge_tile(q), q), moved
                )
        return jnp.where(lo(2, cz), moved, a)

    flow = [pf[0]]
    for q in range(1, 19):
        lq = within(live_ref[q - 1], q, live_slot)
        live_ref[q - 1] = lq
        flow.append(jnp.where(lq > 0.5, within(sf[q], q, flow_slot(q)), pf[OPP[q]]))
        sf[q] = flow[q]

    def total(rows, pick):
        return add_up([rows[q] for q in range(len(rows)) if pick(VEL[q])])

    level_sum = [
        total(flow, lambda c: c[2] == 0),
        total(flow, lambda c: c[0] == 1 and c[2] == 0)
        - total(flow, lambda c: c[0] == -1 and c[2] == 0),
        total(flow, lambda c: c[1] == 1 and c[2] == 0)
        - total(flow, lambda c: c[1] == -1 and c[2] == 0),
    ]
    parts = [[None] * PART for way in range(2)]

    def put_part(way, tile, m, x):
        packs = [None] * PART
        packs[tile] = parts[way][tile]
        put(packs, 4 + way, 8 * tile + m, x)
        parts[way][tile] = packs[tile]

    for way in range(2):
        rows = FACE_POPS[4 + way]
        for s, q in enumerate(rows):
            put_part(way, 0, s, flow[q])
        out_sum = add_up([flow[q] for q in rows])
        put_part(way, 0, LIVE_SLOT, level_sum[0] + out_sum)
        put_part(way, 3, 4, out_sum)
        x_sum = flow[rows[slot_at(4 + way, (1, 0))]] - flow[rows[slot_at(4 + way, (-1, 0))]]
        y_sum = flow[rows[slot_at(4 + way, (0, 1))]] - flow[rows[slot_at(4 + way, (0, -1))]]
        put_part(way, 3, 2, level_sum[1] + x_sum)
        put_part(way, 3, 3, level_sum[2] + y_sum)
    for n in range(BINS):
        g = [pg_0[7 * n]]
        for i in range(1, 7):
            moved = within(sg[6 * n + i - 1], i, bin_slot(n))
            g.append(jnp.where(live_ref[i - 1] > 0.5, moved, 0.0))
            sg[6 * n + i - 1] = g[i]
        flat = add_up(g[:5])
        v, m = (BIN_SLOT + n) // 8, (BIN_SLOT + n) % 8
        for way in range(2):
            put_part(way, v, m, g[5 + way])
            put_part(way, 4 if v == 1 else 3, m, flat + g[5 + way])
    for way in range(2):
        for v in range(PART):
            psend[way, pl.ds(8 * v, 8), :] = parts[way][v]
    send_z(1)
    out_z.start()

    def cross_1(side):
        nonlocal face_tile, edge_tile
        receive_z(0, side)
        face_tile, edge_tile = windows(lat_0, z_tile)
        for q in from_side(side):
            lq = across(live_ref[q - 1], q, live_slot)
            live_ref[q - 1] = lq
            border = lo(2, VEL[q][2])
            moved = across(sf[q], q, flow_slot(q))
            sf[q] = jnp.where(border & (lq < 0.5), pf[OPP[q]], moved)
        lives = live_ref[4 + side] > 0.5
        for n in range(BINS):
            moved = across(sg[6 * n + 4 + side], 5 + side, bin_slot(n))
            sg[6 * n + 4 + side] = jnp.where(lives, moved, 0.0)

    nearer_first(cross_1)

    def bins_across(n):
        return [pg_0[7 * n]] + [sg[6 * n + i] for i in range(6)]

    new = [pf[0]] + [sf[q] for q in range(1, 19)]
    collide_moved(new, bins_across)
    pack_lateral(lat_1, 0, pg)
    out_2.start()
    pack_lateral(lat_1, 1, pg)
    out_3.start()
    move_inside(pg)
    for i in range(1, 7):
        dmask_ref[i - 1] = jnp.where(is_fluid & (live_ref[i - 1] < 0.5), 1.0, 0.0)
    absorb(True, pg_0)
    absorb(False, pg)
    table = jnp.zeros((8, 128), jnp.float32)
    for n in range(BINS):
        table = jnp.where(lane == n, jnp.sum(dacc[n], axis=1, keepdims=True), table)
    table = table + roll_rows(table, 2)
    table = table + roll_rows(table, 4)
    dep_ref[...] = table[:2, :BINS]

    place = [
        (
            jnp.where(near_ref[b, 1] >= 0, 1, 0),
            jnp.where(near_ref[b, 3] >= 0, 1, 0),
        )
        for b in range(2)
    ]

    def blocks_by_place(dz, base):
        def pick(wanted):
            ids = [near_ref[0, VEL.index(c) - 1] for c in wanted]
            return jnp.clip(functools.reduce(jnp.maximum, ids) - base, 0, 3)

        here = 2 * half if dz == 0 else pick([(0, 0, dz)])
        along_x = pick([(1, 0, dz), (-1, 0, dz)])
        along_y = pick([(0, 1, dz), (0, -1, dz)])
        last = jnp.clip(6 - here - along_x - along_y, 0, 3)
        px, py = place[0]
        return [
            [
                jnp.where(
                    px == x, jnp.where(py == y, here, along_y), jnp.where(py == y, along_x, last)
                )
                for y in range(2)
            ]
            for x in range(2)
        ]

    in_z.wait_recv()
    mine = blocks_by_place(0, 4 * layer)
    theirs = [blocks_by_place(-1, 4 * layer - 4), blocks_by_place(1, 4 * layer + 4)]
    spots = [(way, y) for way in range(2) for y in range(2)]

    def column(ids, y):
        return [ids[0][y], ids[1][y]]

    arriving, leaving = {}, {}
    for way, y in spots:
        for v in range(PACKS):
            row = own_row(0, 1 - way) + 8 * v
            arriving[way, y, v] = gather(own_z, row, 2 * Z_ROWS, column(mine, y))
        leaving[way, y] = gather(zwin[way], z_row(0), Z_ROWS, column(theirs[way], y))

    def plane(tile_at, slot_of_way):
        out = None
        for way, y in spots:
            s = 2 * way + y
            moved = roll_lanes(tile_at(way, y), s - slot_of_way(way))
            out = moved if out is None else jnp.where(kk == s, moved, out)
        return out

    at_y = kk & 1

    def plane_shift(x, lateral):
        cx, cy = lateral
        if cx != 0:
            turned = roll_lanes(x, 64)
            edge = lo(0, cx)
            inner = edge & (~even if cx > 0 else even)
            out = jnp.where(inner, roll_rows(turned, 3 * cx), x_shift(turned, cx))
            return out, edge & (even if cx > 0 else ~even)
        if cy != 0:
            edge = lo(1, cy)
            inner = edge & ((at_y == 1) if cy > 0 else (at_y == 0))
            out = jnp.where(inner, roll_lanes(x, -55 * cy), roll_lanes(x, 8 * cy))
            return out, edge & ((at_y == 0) if cy > 0 else (at_y == 1))
        return x, None

    def back(lateral):
        return (-lateral[0], -lateral[1])

    def spread(x, m):
        out = x
        for other in range(8):
            if other != m:
                out = jnp.where(kk == other, roll_lanes(x, other - m), out)
        return out

    source_live = plane(lambda way, y: arriving[way, y, 0], lambda way: LIVE_SLOT)
    came = {}
    for c in LATERAL:
        x = plane(lambda way, y: arriving[way, y, 0], lambda way: slot_at(5 - way, c))
        bounce = plane(lambda way, y: leaving[way, y], lambda way: slot_at(4 + way, back(c)))
        moved, outside = plane_shift(x, c)
        lives, _ = plane_shift(source_live, c)
        lives = lives > 0.5
        if outside is not None:
            lives = lives & ~outside
        came[c] = jnp.where(lives, moved, bounce)
    sums = (
        add_up(came.values()),
        came[1, 0] - came[-1, 0],
        came[0, 1] - came[0, -1],
    )
    for n, (way, y) in enumerate(spots):
        s = 2 * way + y
        for t in range(3):
            came_ref[3 * n + t] = spread(sums[t], s)
        lives = spread(source_live, s) > 0.5
        for v in range(PACKS):
            came_ref[12 + PACKS * n + v] = jnp.where(lives, arriving[way, y, v], 0.0)

    def by_slot(value_of):
        row = jnp.zeros((8, 128), jnp.float32)
        for m in range(8):
            if value_of(m) is not None:
                row = jnp.where(kk == m, value_of(m), row)
        return row

    rate_rows = []
    for v in range(PACKS):
        bins = [8 * v + m - BIN_SLOT for m in range(8)]
        rate_rows.append(by_slot(lambda m: rates_ref[bins[m]] if 0 <= bins[m] < BINS else None))
    weights = by_slot(lambda m: OMEGA * (WEIGHT[1] if m == 0 else WEIGHT[7]) if m < 5 else None)
    leans = [
        [
            by_slot(lambda m: float(VEL[FACE_POPS[4 + way][m]][axis]) if m < 5 else None)
            for axis in range(2)
        ]
        for way in range(2)
    ]

    def lateral_sites():
        in_2.wait_recv()
        in_3.wait_recv()
        for q in range(1, 19):
            if VEL[q][:2] != (0, 0):
                sf[q] = within(sf[q], q, flow_slot(q))
        for n in range(BINS):
            for i in range(1, 5):
                sg[6 * n + i - 1] = within(sg[6 * n + i - 1], i, bin_slot(n))

    def ghost_tile(q, way, v):
        cx, cy, cz = VEL[q]
        blocks = []
        for px, py in place:
            blocks.append(2 * (1 - py if cy != 0 else py) + (1 - px if cx != 0 else px))
        return gather(ghost[way], z_row(0) + 8 * v, Z_ROWS, blocks)

    core = (me // subs) % 2

    @pl.when(core == 1)
    def _():
        nonlocal face_tile, edge_tile
        face_tile, edge_tile = windows(lat_1, ghost_tile)
        lateral_sites()

    def ghosts(way):
        for y in range(2):
            n = 2 * way + y
            partial = [
                gather(pwin[way], part_row(0) + 8 * v, PART_ROWS, column(theirs[way], y))
                for v in range(PART)
            ]
            came_sum, came_x, came_y = [came_ref[3 * n + t] for t in range(3)]
            rho = spread(partial[0], LIVE_SLOT) + came_sum
            inv = 1.0 / rho
            ux = (spread(partial[3], 2) + came_x) * inv
            uy = (spread(partial[3], 3) + came_y) * inv
            un = (spread(partial[3], 4) - came_sum) * inv
            along = un + leans[way][0] * ux + leans[way][1] * uy
            still = 1.0 - 1.5 * (ux * ux + uy * uy + un * un)
            feq = (weights * rho) * (still + 3.0 * along + 4.5 * along * along)
            lean = 1.0 + 4.0 * un
            for v in range(PACKS):
                conc = partial[4 if v == 1 else 3] + came_ref[12 + PACKS * n + v]
                rate = rate_rows[v]
                tile = (1.0 - rate) * partial[v] + (0.125 * rate) * conc * lean
                if v == 0:
                    tile = jnp.where(kk < 5, (1.0 - OMEGA) * partial[0] + feq, tile)
                ghost[way][pl.ds(z_row(y) + 8 * v, 8), :] = tile

    def cross_2(side):
        nonlocal face_tile, edge_tile
        receive_z(1, side)
        ghosts(side)
        face_tile, edge_tile = windows(lat_1, ghost_tile)
        for q in from_side(side):
            sf[q] = across(sf[q], q, flow_slot(q))
        for n in range(BINS):
            sg[6 * n + 4 + side] = across(sg[6 * n + 4 + side], 5 + side, bin_slot(n))

    nearer_first(cross_2)

    @pl.when(core == 0)
    def _():
        nonlocal face_tile, edge_tile
        face_tile, edge_tile = windows(lat_1, ghost_tile)
        lateral_sites()

    new = [pf[0]]
    for q in range(1, 19):
        new.append(jnp.where(live_ref[q - 1] > 0.5, sf[q], pf[OPP[q]]))

    def bins_moved(n):
        new = [pg[7 * n]]
        for i in range(1, 7):
            new.append(jnp.where(live_ref[i - 1] > 0.5, sg[6 * n + i - 1], 0.0))
        return new

    finish(new, bins_moved)

    for copy in (out_1, out_z, out_2, out_3):
        copy.wait_send()

    def sent(way):
        for n in range(2):
            for h in range(2):
                z_copy(n, way, h).wait_send()

    each_way(sent)


def write_out(flow, bins, deposit, flow_out, bins_out, dep_out, sem):
    pairs = [(bins, bins_out), (flow, flow_out), (deposit, dep_out)]
    copies = [pltpu.make_async_copy(a, b, sem.at[n]) for n, (a, b) in enumerate(pairs)]
    for copy in copies:
        copy.start()
    for copy in copies:
        copy.wait()


def tiled(x):
    x = x.reshape(2, -1, 4, 128)
    return x.transpose(1, 2, 0, 3).reshape(-1, 8, 128)


def untiled(x):
    return x.reshape(-1, 4, 2, 128).transpose(2, 0, 1, 3).reshape(2, -1, 512)


def on_device(flow_pops, bin_pops, site_kind, neighbours, bin_rates, settle, inlet_conc):
    subs = lax.axis_size("sub")
    layers = lax.axis_size("dom") * subs // 2
    hbm = pl.BlockSpec(memory_space=pltpu.HBM)
    vmem = pl.BlockSpec(memory_space=pltpu.VMEM)
    f32 = jnp.float32
    shapes = (
        jax.ShapeDtypeStruct((19, 8, 128), f32),
        jax.ShapeDtypeStruct((7 * BINS, 8, 128), f32),
        jax.ShapeDtypeStruct((2, BINS), f32),
    )
    done = pl.pallas_call(
        functools.partial(kernel, layers, subs),
        out_shape=shapes,
        in_specs=[hbm] * 7,
        out_specs=(vmem, vmem, vmem),
        scratch_shapes=[
            pltpu.VMEM((8, 128), jnp.int32),
            pltpu.SMEM((2, 18), jnp.int32),
            pltpu.SMEM((BINS,), f32),
            pltpu.SMEM((BINS,), f32),
            pltpu.SMEM((BINS,), f32),
            pltpu.VMEM((19, 8, 128), f32),
            pltpu.VMEM((7 * BINS, 8, 128), f32),
            pltpu.VMEM((7 * BINS, 8, 128), f32),
            pltpu.VMEM((19, 8, 128), f32),
            pltpu.VMEM((6 * BINS, 8, 128), f32),
            pltpu.VMEM((18, 8, 128), f32),
            pltpu.VMEM((6, 8, 128), f32),
            pltpu.VMEM((BINS, 8, 128), f32),
            pltpu.VMEM((lat_row(2) + 8, 128), f32),
            pltpu.VMEM((lat_row(2) + 8, 128), f32),
            pltpu.VMEM((own_row(2, 0) + 8, 128), f32),
            pltpu.VMEM((z_row(2) + 8, 128), f32),
            pltpu.VMEM((z_row(2) + 8, 128), f32),
            pltpu.VMEM((part_row(2) + 8, 128), f32),
            pltpu.VMEM((part_row(2) + 8, 128), f32),
            pltpu.VMEM((2, PART_ROWS, 128), f32),
            pltpu.VMEM((z_row(2) + 8, 128), f32),
            pltpu.VMEM((z_row(2) + 8, 128), f32),
            pltpu.VMEM((12 + 4 * PACKS, 8, 128), f32),
            pltpu.SemaphoreType.DMA((7,)),
            pltpu.SemaphoreType.DMA((2, 4)),
            pltpu.SemaphoreType.DMA((2, 4)),
            pltpu.SemaphoreType.DMA((4,)),
            pltpu.SemaphoreType.DMA((4,)),
        ],
        compiler_params=pltpu.CompilerParams(
            collective_id=0, has_side_effects=True, vmem_limit_bytes=16 * 1024 * 1024
        ),
    )(
        *[
            pltpu.with_memory_space_constraint(x, pltpu.HBM)
            for x in (
                tiled(flow_pops),
                tiled(bin_pops),
                tiled(site_kind)[0],
                neighbours,
                bin_rates,
                settle,
                inlet_conc,
            )
        ]
    )
    flow, bins, deposit = pl.pallas_call(
        write_out,
        out_shape=shapes,
        in_specs=[vmem, vmem, vmem],
        out_specs=(hbm, hbm, hbm),
        scratch_shapes=[pltpu.SemaphoreType.DMA((3,))],
        compiler_params=pltpu.CompilerParams(vmem_limit_bytes=16 * 1024 * 1024),
    )(*done)
    return untiled(flow), untiled(bins), deposit


def solution(mesh):
    cut = ("dom", "sub")
    return jax.shard_map(
        on_device,
        mesh=mesh,
        in_specs=(P(cut, None, None), P(cut, None, None), P(cut, None), P(cut, None), P(), P(), P()),
        out_specs=(P(cut, None, None), P(cut, None, None), P(cut, None)),
        check_vma=False,
    )
```

```python
import functools

import jax
import jax.numpy as jnp
from jax import lax
from jax.experimental import pallas as pl
from jax.experimental.pallas import tpu as pltpu
from jax.sharding import PartitionSpec as P

VEL = [
    (0, 0, 0),
    (1, 0, 0),
    (-1, 0, 0),
    (0, 1, 0),
    (0, -1, 0),
    (0, 0, 1),
    (0, 0, -1),
    (1, 1, 0),
    (-1, -1, 0),
    (1, -1, 0),
    (-1, 1, 0),
    (1, 0, 1),
    (-1, 0, -1),
    (1, 0, -1),
    (-1, 0, 1),
    (0, 1, 1),
    (0, -1, -1),
    (0, 1, -1),
    (0, -1, 1),
]
WEIGHT = [1.0 / 3.0] + [1.0 / 18.0] * 6 + [1.0 / 36.0] * 12
OPP = [0, 2, 1, 4, 3, 6, 5, 8, 7, 10, 9, 12, 11, 14, 13, 16, 15, 18, 17]
OMEGA = 1.6
INLET = 0.04
BINS = 12
MESH = pl.DeviceIdType.MESH

FACE_POPS = [
    [q for q in range(1, 19) if VEL[q][d // 2] == 1 - 2 * (d % 2)] for d in range(6)
]
LIVE_SLOT = 5
BIN_SLOT = 6
PACKS = 3
PART = 5
LAT_ROWS, Z_ROWS, PART_ROWS = 2 * PACKS * 8, PACKS * 8, PART * 8
LATERAL = [(0, 0), (1, 0), (-1, 0), (0, 1), (0, -1)]


def lat_row(h):
    return 8 + LAT_ROWS * h


def own_row(h, way):
    return 8 + Z_ROWS * (2 * h + way)


def z_row(h):
    return 8 + Z_ROWS * h


def part_row(h):
    return 8 + PART_ROWS * h


def slot_at(d, lateral):
    return [VEL[q][:2] for q in FACE_POPS[d]].index(lateral)


def add_up(terms):
    terms = list(terms)
    while len(terms) > 1:
        pairs = [a + b for a, b in zip(terms[::2], terms[1::2])]
        terms = pairs + terms[len(pairs) * 2 :]
    return terms[0]


def roll_lanes(x, shift):
    shift %= 128
    return x if shift == 0 else pltpu.roll(x, shift, 1)


def roll_rows(x, shift):
    shift %= 8
    return x if shift == 0 else pltpu.roll(x, shift, 0)


def kernel(
    layers,
    subs,
    flow_in,
    bins_in,
    kind_in,
    near_in,
    rates_in,
    settle_in,
    conc_in,
    fbuf,
    gbuf,
    dep_ref,
    kind_ref,
    near_ref,
    rates_ref,
    settle_ref,
    conc_ref,
    pf,
    pg_0,
    pg,
    sf,
    sg,
    live_ref,
    dmask_ref,
    dacc,
    lat_0,
    lat_1,
    own_z,
    zwin_0,
    zwin_1,
    pwin_0,
    pwin_1,
    psend,
    ghost_0,
    ghost_1,
    came_ref,
    in_sem,
    send_sem,
    recv_sem,
    mate_send,
    mate_recv,
):
    zwin, pwin, ghost = (zwin_0, zwin_1), (pwin_0, pwin_1), (ghost_0, ghost_1)
    me = lax.axis_index("dom") * subs + lax.axis_index("sub")
    layer = me // 2
    half = me % 2
    mate = 2 * layer + 1 - half
    far = 1 - (me % subs) // 2

    def device(g):
        return (g // subs, g % subs)

    def beyond(way):
        return layer + 1 - 2 * way

    def each_way(do, part=slice(None)):
        for order in ((0, 1), (1, 0)):

            @pl.when(far == order[0])
            def _():
                for way in order[part]:
                    there = beyond(way)
                    pl.when((there >= 0) & (there < layers))(functools.partial(do, way))

    barrier = pltpu.get_barrier_semaphore()

    def greet(way):
        for h in range(2):
            pl.semaphore_signal(
                barrier, inc=1, device_id=device(2 * beyond(way) + h), device_id_type=MESH
            )

    each_way(greet)
    pl.semaphore_signal(barrier, inc=1, device_id=device(mate), device_id_type=MESH)

    pairs = [
        (flow_in, fbuf),
        (kind_in, kind_ref),
        (bins_in, gbuf),
        (rates_in, rates_ref),
        (settle_in, settle_ref),
        (conc_in, conc_ref),
        (near_in, near_ref),
    ]
    loads = [pltpu.make_async_copy(a, b, in_sem.at[n]) for n, (a, b) in enumerate(pairs)]
    for copy in loads:
        copy.start()

    sub = lax.broadcasted_iota(jnp.int32, (8, 128), 0)
    lane = lax.broadcasted_iota(jnp.int32, (8, 128), 1)
    jj = (lane >> 3) & 7
    kk = lane & 7
    low = lane < 64
    even = (sub & 1) == 0
    quarter = sub >> 1
    at = {
        (0, 0): (quarter == 0) & low,
        (0, 7): (quarter == 3) & (lane >= 64),
        (1, 0): jj == 0,
        (1, 7): jj == 7,
        (2, 0): kk == 0,
        (2, 7): kk == 7,
    }

    loads[0].wait()
    loads[1].wait()
    kind = kind_ref[...]
    alive = jnp.where(kind > 0, 1.0, 0.0)
    is_in = kind == 2
    is_end = kind >= 2
    is_fluid = kind == 1

    def moments(f):
        odd = range(1, 19, 2)
        rho = add_up([f[q] + f[q + 1] for q in odd] + [f[0]])
        inv = 1.0 / rho
        gaps = {q: f[q] - f[q + 1] for q in odd}
        vel = []
        for axis in range(3):
            plus = add_up([gaps[q] for q in odd if VEL[q][axis] == 1])
            minus = [gaps[q] for q in odd if VEL[q][axis] == -1]
            vel.append((plus - add_up(minus) if minus else plus) * inv)
        return rho, vel

    def equilibrium(scale, vel):
        base = 1.0 - 1.5 * (vel[0] * vel[0] + vel[1] * vel[1] + vel[2] * vel[2])
        scaled = {w: scale * w for w in set(WEIGHT)}
        out = [None] * 19
        out[0] = scaled[WEIGHT[0]] * base
        for q in range(1, 19, 2):
            along = None
            for axis in range(3):
                if VEL[q][axis] != 0:
                    term = vel[axis]
                    if along is None:
                        along = term if VEL[q][axis] > 0 else -term
                    else:
                        along = along + term if VEL[q][axis] > 0 else along - term
            even = base + 4.5 * along * along
            odd = 3.0 * along
            out[q] = scaled[WEIGHT[q]] * (even + odd)
            out[q + 1] = scaled[WEIGHT[q]] * (even - odd)
        return out

    def put(packs, d, slot, x):
        v, m = slot // 8, slot % 8
        x = roll_lanes(x, m - (0 if d % 2 else 7))
        packs[v] = x if packs[v] is None else jnp.where(kk == m, x, packs[v])

    def gather(ref, row, stride, blocks):
        parts = [
            ref[pl.ds(row + stride * (w >> 1) + (w & 1) - b, 8), :] for b, w in enumerate(blocks)
        ]
        return jnp.where(even, parts[0], parts[1])

    def nearby(q, base):
        return [jnp.clip(near_ref[b, q - 1] - base, 0, 3) for b in range(2)]

    def present(q):
        return jnp.where(even, near_ref[0, q - 1], near_ref[1, q - 1]) >= 0

    def x_shift(r, cx):
        if cx == 0:
            return r
        moved = roll_rows(r, 2 * cx)
        return jnp.where(low, moved, r) if cx > 0 else jnp.where(low, r, moved)

    def local(a, q):
        cx, cy, cz = VEL[q]
        return x_shift(roll_lanes(a, 64 * abs(cx) + 8 * cy + cz), cx)

    def unpack(d, slot, tile, q):
        cx, cy, cz = VEL[q]
        m = slot % 8
        if d // 2 == 0:
            t, h = m // 2, m % 2
            turned = roll_lanes(tile, 64 * h + 8 * cy + cz)
            return roll_rows(turned, -2 * t if d % 2 == 0 else 4 - 2 * t)
        if d // 2 == 1:
            return x_shift(roll_lanes(tile, 64 * abs(cx) - 8 * m + (112 if d % 2 else 0) + cz), cx)
        return x_shift(roll_lanes(tile, 64 * abs(cx) + 8 * cy + (7 if d % 2 else 0) - m), cx)

    def unpack_edge(d, slot, tile, q):
        cx, cy, cz = VEL[q]
        m = slot % 8
        if d // 2 == 1:
            shift = (112 if d % 2 else 0) - 8 * m
        else:
            shift = (7 if d % 2 else 0) - m
        if cx != 0:
            return roll_rows(roll_lanes(tile, shift + 64), -6 * cx)
        return roll_lanes(tile, shift - 56 * cy)

    def face_of(axis, sign):
        return 2 * axis + (0 if sign > 0 else 1)

    def edge_face(q):
        axis = 2 if VEL[q][2] != 0 else 1
        return face_of(axis, VEL[q][axis])

    def lo(axis, sign):
        return at[(axis, 0 if sign > 0 else 7)]

    def mate_copy(n, ref, row, rows, h):
        span = pl.ds(row(h), rows)
        return pltpu.make_async_remote_copy(
            src_ref=ref.at[span],
            dst_ref=ref.at[span],
            send_sem=mate_send.at[n],
            recv_sem=mate_recv.at[n],
            device_id=device(mate),
            device_id_type=MESH,
        )

    def mate_copies(h):
        return (
            mate_copy(0, lat_0, lat_row, LAT_ROWS, h),
            mate_copy(1, own_z, lambda h: own_row(h, 0), 2 * Z_ROWS, h),
            mate_copy(2, lat_1, lat_row, LAT_ROWS // 2, h),
            mate_copy(3, lat_1, lambda h: lat_row(h) + LAT_ROWS // 2, LAT_ROWS // 2, h),
        )

    def z_copy(n, way, h):
        src = (own_z.at[pl.ds(own_row(half, way), Z_ROWS)], psend.at[way])[n]
        dst = (
            zwin[way].at[pl.ds(z_row(half), Z_ROWS)],
            pwin[way].at[pl.ds(part_row(half), PART_ROWS)],
        )[n]
        return pltpu.make_async_remote_copy(
            src_ref=src,
            dst_ref=dst,
            send_sem=send_sem.at[n, 2 * way + h],
            recv_sem=recv_sem.at[n, 2 * way + half],
            device_id=device(2 * beyond(way) + h),
            device_id_type=MESH,
        )

    def z_in(n, way, h):
        src = (own_z.at[pl.ds(own_row(half, way), Z_ROWS)], psend.at[way])[n]
        dst = (
            zwin[way].at[pl.ds(z_row(h), Z_ROWS)],
            pwin[way].at[pl.ds(part_row(h), PART_ROWS)],
        )[n]
        return pltpu.make_async_remote_copy(
            src_ref=src,
            dst_ref=dst,
            send_sem=send_sem.at[n, 2 * way + h],
            recv_sem=recv_sem.at[n, 2 * way + h],
            device_id=device(2 * beyond(1 - way) + h),
            device_id_type=MESH,
        )

    def send_z(n, part=slice(None)):
        def do(way):
            for h in (half, 1 - half):
                z_copy(n, way, h).start()

        each_way(do, part)

    def receive_z(n, side):
        @pl.when(layer > 0 if side == 0 else layer < layers - 1)
        def _():
            for h in range(2):
                z_in(n, side, h).wait_recv()

    def nearer_first(do):
        for order in ((0, 1), (1, 0)):

            @pl.when(far == order[0])
            def _():
                for side in order:
                    do(side)

    def from_side(side):
        return [q for q in range(1, 19) if VEL[q][2] == 1 - 2 * side]

    def collide_bin(pg, n, g, conc, rate, lean4):
        part = (0.125 * rate) * conc
        keep = 1.0 - rate
        pg[7 * n] = keep * g[0] + (part + part)
        x4, y4, z4 = lean4
        for axis, u4 in ((0, x4), (1, y4 - 4.0 * settle_ref[n]), (2, z4)):
            lean = part * u4
            pg[7 * n + 1 + 2 * axis] = keep * g[1 + 2 * axis] + (part + lean)
            pg[7 * n + 2 + 2 * axis] = keep * g[2 + 2 * axis] + (part - lean)

    def collide_inputs():
        f = [fbuf[q] for q in range(19)]
        rho, vel = moments(f)
        target = equilibrium(OMEGA * rho, vel)
        for q in range(19):
            pf[q] = (1.0 - OMEGA) * f[q] + target[q]
        for copy in loads[2:]:
            copy.wait()
        lean4 = [4.0 * u for u in vel]
        for n in range(BINS):
            g = [gbuf[7 * n + i] for i in range(7)]
            collide_bin(pg_0, n, g, add_up(g), rates_ref[n], lean4)

    def at_ends(vel):
        return [jnp.where(is_in, (0.0, 0.0, INLET)[axis], vel[axis]) for axis in range(3)]

    def collide_moved(flow, bins_of):
        rho, vel = moments(flow)
        vel = at_ends(vel)
        target = equilibrium(jnp.where(is_fluid, OMEGA * rho, 1.0), vel)
        keep = jnp.where(is_fluid, 1.0 - OMEGA, 0.0)
        for q in range(19):
            pf[q] = keep * flow[q] + target[q]
        lean4 = [4.0 * u for u in vel]
        for n in range(BINS):
            g = bins_of(n)
            conc = jnp.where(is_in, conc_ref[n], add_up(g))
            collide_bin(pg, n, g, conc, jnp.where(is_fluid, rates_ref[n], 1.0), lean4)

    def pack_z(way):
        d = 4 + way
        packs = [None] * PACKS
        for s, q in enumerate(FACE_POPS[d]):
            put(packs, d, s, pf[q])
        put(packs, d, LIVE_SLOT, alive)
        for n in range(BINS):
            put(packs, d, BIN_SLOT + n, pg_0[7 * n + 1 + d])
        for v, tile in enumerate(packs):
            own_z[pl.ds(pl.multiple_of(own_row(half, way) + 8 * v, 8), 8), :] = tile

    def pack_lateral(ref, axis, pg):
        ahead = present(1 + 2 * axis)
        if axis == 0:
            spot = 2 * quarter + jnp.where(low, 0, 1)
            spot = jnp.where(ahead, spot, 2 * ((quarter + 3) & 3) + jnp.where(low, 1, 0))
        else:
            spot = jnp.where(ahead, jj, (jj + 7) & 7)
        packs = [None] * PACKS
        rows = [(pf[q], pf[r]) for q, r in zip(FACE_POPS[2 * axis], FACE_POPS[2 * axis + 1])]
        rows.append((alive, alive))
        for n in range(BINS):
            rows.append((pg[7 * n + 1 + 2 * axis], pg[7 * n + 2 + 2 * axis]))
        for slot, (x, y) in enumerate(rows):
            v, m = slot // 8, slot % 8
            x = jnp.where(ahead, x, y)
            if axis == 0:
                x = roll_rows(roll_lanes(x, 64 * (m % 2 - 1)), 2 * (m // 2 - 3))
            else:
                x = roll_lanes(x, 8 * (m - 7))
            packs[v] = x if packs[v] is None else jnp.where(spot == m, x, packs[v])
        row = lat_row(half) + 8 * PACKS * axis
        for v in range(PACKS):
            ref[pl.ds(pl.multiple_of(row + 8 * v, 8), 8), :] = packs[v]

    def absent_as_zero(q, v, tile):
        return jnp.where(present(q), tile, 0.0) if v == 0 else tile

    def windows(lat, z_tile):
        memo = {}

        def tile_of(q, d, v):
            if (q, d, v) not in memo:
                if d >= 4:
                    tile = z_tile(q, d - 4, v)
                else:
                    row = lat_row(0) + 8 * (PACKS * (d // 2) + v)
                    tile = gather(lat, row, LAT_ROWS, nearby(q, 4 * layer))
                memo[(q, d, v)] = absent_as_zero(q, v, tile)
            return memo[(q, d, v)]

        return (
            lambda d, v: tile_of(OPP[1 + d], d, v),
            lambda q: tile_of(OPP[q], edge_face(q), 0),
        )

    def flow_slot(q):
        return lambda d: FACE_POPS[d].index(q)

    def bin_slot(n):
        return lambda d: BIN_SLOT + n

    def live_slot(d):
        return LIVE_SLOT

    def absorb(first, pg):
        masks = [dmask_ref[i] > 0.5 for i in range(6)]
        for n in range(BINS):
            total = add_up([jnp.where(masks[i - 1], pg[7 * n + OPP[i]], 0.0) for i in range(1, 7)])
            dacc[n] = total if first else dacc[n] + total

    def finish(flow, bins_of):
        vel = at_ends(moments(flow)[1])
        target = equilibrium(jnp.ones_like(vel[0]), vel)
        for q in range(19):
            fbuf[q] = jnp.where(is_fluid, flow[q], jnp.where(is_end, target[q], fbuf[q]))
        x4, y4, z4 = [4.0 * u for u in vel]
        for n in range(BINS):
            g = bins_of(n)
            part = 0.125 * jnp.where(is_in, conc_ref[n], add_up(g))
            target = [part + part]
            for u4 in (x4, y4 - 4.0 * settle_ref[n], z4):
                lean = part * u4
                target += [part + lean, part - lean]
            for i in range(7):
                old = gbuf[7 * n + i]
                gbuf[7 * n + i] = jnp.where(is_fluid, g[i], jnp.where(is_end, target[i], old))

    def move_inside(pg):
        for q in range(1, 19):
            sf[q] = local(pf[q], q)
        for n in range(BINS):
            for i in range(1, 7):
                sg[6 * n + i - 1] = local(pg[7 * n + i], i)

    collide_inputs()
    for way in range(2):
        pack_z(way)
    pack_lateral(lat_0, 0, pg_0)
    pack_lateral(lat_0, 1, pg_0)
    ends = jnp.where(layer < layers - 1, 1, 0) + jnp.where(layer > 0, 1, 0)
    pl.semaphore_wait(barrier, 1 + 2 * ends)
    out_1, out_z, out_2, out_3 = mate_copies(half)
    in_1, in_z, in_2, in_3 = mate_copies(1 - half)
    core = (me // subs) % 2

    @pl.when(core == 1)
    def _():
        send_z(0, slice(0, 1))
        out_1.start()

    @pl.when(core == 0)
    def _():
        out_1.start()
        send_z(0, slice(0, 1))

    send_z(0, slice(1, 2))
    move_inside(pg_0)
    for q in range(1, 19):
        live_ref[q - 1] = local(alive, q)

    def z_tile(q, way, v):
        base = 4 * layer + (-4 if way == 0 else 4)
        return gather(zwin[way], z_row(0) + 8 * v, Z_ROWS, nearby(q, base))

    in_1.wait_recv()
    face_tile, edge_tile = windows(lat_0, z_tile)

    def within(a, q, slot_of):
        out = a
        axes = [axis for axis in range(2) if VEL[q][axis] != 0]
        for axis in axes:
            d = face_of(axis, VEL[q][axis])
            moved = unpack(d, slot_of(d), face_tile(d, slot_of(d) // 8), q)
            mask = lo(axis, VEL[q][axis])
            if VEL[q][2] != 0:
                mask = mask & ~lo(2, VEL[q][2])
            out = jnp.where(mask, moved, out)
        if len(axes) == 2:
            d = edge_face(q)
            mask = lo(0, VEL[q][0]) & lo(1, VEL[q][1])
            out = jnp.where(mask, unpack_edge(d, slot_of(d), edge_tile(q), q), out)
        return out

    def across(a, q, slot_of):
        cx, cy, cz = VEL[q]
        if cz == 0:
            return a
        d = face_of(2, cz)
        slot = slot_of(d)
        moved = unpack(d, slot, face_tile(d, slot // 8), q)
        for axis in range(2):
            if VEL[q][axis] != 0:
                moved = jnp.where(
                    lo(axis, VEL[q][axis]), unpack_edge(d, slot, edge_tile(q), q), moved
                )
        return jnp.where(lo(2, cz), moved, a)

    flow = [pf[0]]
    for q in range(1, 19):
        lq = within(live_ref[q - 1], q, live_slot)
        live_ref[q - 1] = lq
        flow.append(jnp.where(lq > 0.5, within(sf[q], q, flow_slot(q)), pf[OPP[q]]))
        sf[q] = flow[q]

    def total(rows, pick):
        return add_up([rows[q] for q in range(len(rows)) if pick(VEL[q])])

    level_sum = [
        total(flow, lambda c: c[2] == 0),
        total(flow, lambda c: c[0] == 1 and c[2] == 0)
        - total(flow, lambda c: c[0] == -1 and c[2] == 0),
        total(flow, lambda c: c[1] == 1 and c[2] == 0)
        - total(flow, lambda c: c[1] == -1 and c[2] == 0),
    ]
    parts = [[None] * PART for way in range(2)]

    def put_part(way, tile, m, x):
        packs = [None] * PART
        packs[tile] = parts[way][tile]
        put(packs, 4 + way, 8 * tile + m, x)
        parts[way][tile] = packs[tile]

    for way in range(2):
        rows = FACE_POPS[4 + way]
        for s, q in enumerate(rows):
            put_part(way, 0, s, flow[q])
        out_sum = add_up([flow[q] for q in rows])
        put_part(way, 0, LIVE_SLOT, level_sum[0] + out_sum)
        put_part(way, 3, 4, out_sum)
        x_sum = flow[rows[slot_at(4 + way, (1, 0))]] - flow[rows[slot_at(4 + way, (-1, 0))]]
        y_sum = flow[rows[slot_at(4 + way, (0, 1))]] - flow[rows[slot_at(4 + way, (0, -1))]]
        put_part(way, 3, 2, level_sum[1] + x_sum)
        put_part(way, 3, 3, level_sum[2] + y_sum)
    for n in range(BINS):
        g = [pg_0[7 * n]]
        for i in range(1, 7):
            moved = within(sg[6 * n + i - 1], i, bin_slot(n))
            g.append(jnp.where(live_ref[i - 1] > 0.5, moved, 0.0))
            sg[6 * n + i - 1] = g[i]
        flat = add_up(g[:5])
        v, m = (BIN_SLOT + n) // 8, (BIN_SLOT + n) % 8
        for way in range(2):
            put_part(way, v, m, g[5 + way])
            put_part(way, 4 if v == 1 else 3, m, flat + g[5 + way])
    for way in range(2):
        for v in range(PART):
            psend[way, pl.ds(8 * v, 8), :] = parts[way][v]
    send_z(1)
    out_z.start()

    def cross_1(side):
        nonlocal face_tile, edge_tile
        receive_z(0, side)
        face_tile, edge_tile = windows(lat_0, z_tile)
        for q in from_side(side):
            lq = across(live_ref[q - 1], q, live_slot)
            live_ref[q - 1] = lq
            border = lo(2, VEL[q][2])
            moved = across(sf[q], q, flow_slot(q))
            sf[q] = jnp.where(border & (lq < 0.5), pf[OPP[q]], moved)
        lives = live_ref[4 + side] > 0.5
        for n in range(BINS):
            moved = across(sg[6 * n + 4 + side], 5 + side, bin_slot(n))
            sg[6 * n + 4 + side] = jnp.where(lives, moved, 0.0)

    nearer_first(cross_1)

    def bins_across(n):
        return [pg_0[7 * n]] + [sg[6 * n + i] for i in range(6)]

    new = [pf[0]] + [sf[q] for q in range(1, 19)]
    collide_moved(new, bins_across)
    pack_lateral(lat_1, 0, pg)
    out_2.start()
    pack_lateral(lat_1, 1, pg)
    out_3.start()
    move_inside(pg)
    for i in range(1, 7):
        dmask_ref[i - 1] = jnp.where(is_fluid & (live_ref[i - 1] < 0.5), 1.0, 0.0)
    absorb(True, pg_0)
    absorb(False, pg)
    table = jnp.zeros((8, 128), jnp.float32)
    for n in range(BINS):
        table = jnp.where(lane == n, jnp.sum(dacc[n], axis=1, keepdims=True), table)
    table = table + roll_rows(table, 2)
    table = table + roll_rows(table, 4)
    dep_ref[...] = table[:2, :BINS]

    place = [
        (
            jnp.where(near_ref[b, 1] >= 0, 1, 0),
            jnp.where(near_ref[b, 3] >= 0, 1, 0),
        )
        for b in range(2)
    ]

    def blocks_by_place(dz, base):
        def pick(wanted):
            ids = [near_ref[0, VEL.index(c) - 1] for c in wanted]
            return jnp.clip(functools.reduce(jnp.maximum, ids) - base, 0, 3)

        here = 2 * half if dz == 0 else pick([(0, 0, dz)])
        along_x = pick([(1, 0, dz), (-1, 0, dz)])
        along_y = pick([(0, 1, dz), (0, -1, dz)])
        last = jnp.clip(6 - here - along_x - along_y, 0, 3)
        px, py = place[0]
        return [
            [
                jnp.where(
                    px == x, jnp.where(py == y, here, along_y), jnp.where(py == y, along_x, last)
                )
                for y in range(2)
            ]
            for x in range(2)
        ]

    in_z.wait_recv()
    mine = blocks_by_place(0, 4 * layer)
    theirs = [blocks_by_place(-1, 4 * layer - 4), blocks_by_place(1, 4 * layer + 4)]
    spots = [(way, y) for way in range(2) for y in range(2)]

    def column(ids, y):
        return [ids[0][y], ids[1][y]]

    arriving, leaving = {}, {}
    for way, y in spots:
        for v in range(PACKS):
            row = own_row(0, 1 - way) + 8 * v
            arriving[way, y, v] = gather(own_z, row, 2 * Z_ROWS, column(mine, y))
        leaving[way, y] = gather(zwin[way], z_row(0), Z_ROWS, column(theirs[way], y))

    def plane(tile_at, slot_of_way):
        out = None
        for way, y in spots:
            s = 2 * way + y
            moved = roll_lanes(tile_at(way, y), s - slot_of_way(way))
            out = moved if out is None else jnp.where(kk == s, moved, out)
        return out

    at_y = kk & 1

    def plane_shift(x, lateral):
        cx, cy = lateral
        if cx != 0:
            turned = roll_lanes(x, 64)
            edge = lo(0, cx)
            inner = edge & (~even if cx > 0 else even)
            out = jnp.where(inner, roll_rows(turned, 3 * cx), x_shift(turned, cx))
            return out, edge & (even if cx > 0 else ~even)
        if cy != 0:
            edge = lo(1, cy)
            inner = edge & ((at_y == 1) if cy > 0 else (at_y == 0))
            out = jnp.where(inner, roll_lanes(x, -55 * cy), roll_lanes(x, 8 * cy))
            return out, edge & ((at_y == 0) if cy > 0 else (at_y == 1))
        return x, None

    def back(lateral):
        return (-lateral[0], -lateral[1])

    def spread(x, m):
        out = x
        for other in range(8):
            if other != m:
                out = jnp.where(kk == other, roll_lanes(x, other - m), out)
        return out

    source_live = plane(lambda way, y: arriving[way, y, 0], lambda way: LIVE_SLOT)
    came = {}
    for c in LATERAL:
        x = plane(lambda way, y: arriving[way, y, 0], lambda way: slot_at(5 - way, c))
        bounce = plane(lambda way, y: leaving[way, y], lambda way: slot_at(4 + way, back(c)))
        moved, outside = plane_shift(x, c)
        lives, _ = plane_shift(source_live, c)
        lives = lives > 0.5
        if outside is not None:
            lives = lives & ~outside
        came[c] = jnp.where(lives, moved, bounce)
    sums = (
        add_up(came.values()),
        came[1, 0] - came[-1, 0],
        came[0, 1] - came[0, -1],
    )
    for n, (way, y) in enumerate(spots):
        s = 2 * way + y
        for t in range(3):
            came_ref[3 * n + t] = spread(sums[t], s)
        lives = spread(source_live, s) > 0.5
        for v in range(PACKS):
            came_ref[12 + PACKS * n + v] = jnp.where(lives, arriving[way, y, v], 0.0)

    def by_slot(value_of):
        row = jnp.zeros((8, 128), jnp.float32)
        for m in range(8):
            if value_of(m) is not None:
                row = jnp.where(kk == m, value_of(m), row)
        return row

    rate_rows = []
    for v in range(PACKS):
        bins = [8 * v + m - BIN_SLOT for m in range(8)]
        rate_rows.append(by_slot(lambda m: rates_ref[bins[m]] if 0 <= bins[m] < BINS else None))
    weights = by_slot(lambda m: OMEGA * (WEIGHT[1] if m == 0 else WEIGHT[7]) if m < 5 else None)
    leans = [
        [
            by_slot(lambda m: float(VEL[FACE_POPS[4 + way][m]][axis]) if m < 5 else None)
            for axis in range(2)
        ]
        for way in range(2)
    ]

    def lateral_sites():
        in_2.wait_recv()
        in_3.wait_recv()
        for q in range(1, 19):
            if VEL[q][:2] != (0, 0):
                sf[q] = within(sf[q], q, flow_slot(q))
        for n in range(BINS):
            for i in range(1, 5):
                sg[6 * n + i - 1] = within(sg[6 * n + i - 1], i, bin_slot(n))

    def ghost_tile(q, way, v):
        cx, cy, cz = VEL[q]
        blocks = []
        for px, py in place:
            blocks.append(2 * (1 - py if cy != 0 else py) + (1 - px if cx != 0 else px))
        return gather(ghost[way], z_row(0) + 8 * v, Z_ROWS, blocks)

    @pl.when(core == 1)
    def _():
        nonlocal face_tile, edge_tile
        face_tile, edge_tile = windows(lat_1, ghost_tile)
        lateral_sites()

    def ghosts(way):
        for y in range(2):
            n = 2 * way + y
            partial = [
                gather(pwin[way], part_row(0) + 8 * v, PART_ROWS, column(theirs[way], y))
                for v in range(PART)
            ]
            came_sum, came_x, came_y = [came_ref[3 * n + t] for t in range(3)]
            rho = spread(partial[0], LIVE_SLOT) + came_sum
            inv = 1.0 / rho
            ux = (spread(partial[3], 2) + came_x) * inv
            uy = (spread(partial[3], 3) + came_y) * inv
            un = (spread(partial[3], 4) - came_sum) * inv
            along = un + leans[way][0] * ux + leans[way][1] * uy
            still = 1.0 - 1.5 * (ux * ux + uy * uy + un * un)
            feq = (weights * rho) * (still + 3.0 * along + 4.5 * along * along)
            lean = 1.0 + 4.0 * un
            for v in range(PACKS):
                conc = partial[4 if v == 1 else 3] + came_ref[12 + PACKS * n + v]
                rate = rate_rows[v]
                tile = (1.0 - rate) * partial[v] + (0.125 * rate) * conc * lean
                if v == 0:
                    tile = jnp.where(kk < 5, (1.0 - OMEGA) * partial[0] + feq, tile)
                ghost[way][pl.ds(z_row(y) + 8 * v, 8), :] = tile

    def cross_2(side):
        nonlocal face_tile, edge_tile
        receive_z(1, side)
        ghosts(side)
        face_tile, edge_tile = windows(lat_1, ghost_tile)
        for q in from_side(side):
            sf[q] = across(sf[q], q, flow_slot(q))
        for n in range(BINS):
            sg[6 * n + 4 + side] = across(sg[6 * n + 4 + side], 5 + side, bin_slot(n))

    nearer_first(cross_2)

    @pl.when(core == 0)
    def _():
        nonlocal face_tile, edge_tile
        face_tile, edge_tile = windows(lat_1, ghost_tile)
        lateral_sites()

    new = [pf[0]]
    for q in range(1, 19):
        new.append(jnp.where(live_ref[q - 1] > 0.5, sf[q], pf[OPP[q]]))

    def bins_moved(n):
        new = [pg[7 * n]]
        for i in range(1, 7):
            new.append(jnp.where(live_ref[i - 1] > 0.5, sg[6 * n + i - 1], 0.0))
        return new

    finish(new, bins_moved)

    for copy in (out_1, out_z, out_2, out_3):
        copy.wait_send()

    def sent(way):
        for n in range(2):
            for h in range(2):
                z_copy(n, way, h).wait_send()

    each_way(sent)


def write_out(flow, bins, deposit, flow_out, bins_out, dep_out, sem):
    pairs = [(bins, bins_out), (flow, flow_out), (deposit, dep_out)]
    copies = [pltpu.make_async_copy(a, b, sem.at[n]) for n, (a, b) in enumerate(pairs)]
    for copy in copies:
        copy.start()
    for copy in copies:
        copy.wait()


def tiled(x):
    x = x.reshape(2, -1, 4, 128)
    return x.transpose(1, 2, 0, 3).reshape(-1, 8, 128)


def untiled(x):
    return x.reshape(-1, 4, 2, 128).transpose(2, 0, 1, 3).reshape(2, -1, 512)


def on_device(flow_pops, bin_pops, site_kind, neighbours, bin_rates, settle, inlet_conc):
    subs = lax.axis_size("sub")
    layers = lax.axis_size("dom") * subs // 2
    hbm = pl.BlockSpec(memory_space=pltpu.HBM)
    vmem = pl.BlockSpec(memory_space=pltpu.VMEM)
    f32 = jnp.float32
    shapes = (
        jax.ShapeDtypeStruct((19, 8, 128), f32),
        jax.ShapeDtypeStruct((7 * BINS, 8, 128), f32),
        jax.ShapeDtypeStruct((2, BINS), f32),
    )
    done = pl.pallas_call(
        functools.partial(kernel, layers, subs),
        out_shape=shapes,
        in_specs=[hbm] * 7,
        out_specs=(vmem, vmem, vmem),
        scratch_shapes=[
            pltpu.VMEM((8, 128), jnp.int32),
            pltpu.SMEM((2, 18), jnp.int32),
            pltpu.SMEM((BINS,), f32),
            pltpu.SMEM((BINS,), f32),
            pltpu.SMEM((BINS,), f32),
            pltpu.VMEM((19, 8, 128), f32),
            pltpu.VMEM((7 * BINS, 8, 128), f32),
            pltpu.VMEM((7 * BINS, 8, 128), f32),
            pltpu.VMEM((19, 8, 128), f32),
            pltpu.VMEM((6 * BINS, 8, 128), f32),
            pltpu.VMEM((18, 8, 128), f32),
            pltpu.VMEM((6, 8, 128), f32),
            pltpu.VMEM((BINS, 8, 128), f32),
            pltpu.VMEM((lat_row(2) + 8, 128), f32),
            pltpu.VMEM((lat_row(2) + 8, 128), f32),
            pltpu.VMEM((own_row(2, 0) + 8, 128), f32),
            pltpu.VMEM((z_row(2) + 8, 128), f32),
            pltpu.VMEM((z_row(2) + 8, 128), f32),
            pltpu.VMEM((part_row(2) + 8, 128), f32),
            pltpu.VMEM((part_row(2) + 8, 128), f32),
            pltpu.VMEM((2, PART_ROWS, 128), f32),
            pltpu.VMEM((z_row(2) + 8, 128), f32),
            pltpu.VMEM((z_row(2) + 8, 128), f32),
            pltpu.VMEM((12 + 4 * PACKS, 8, 128), f32),
            pltpu.SemaphoreType.DMA((7,)),
            pltpu.SemaphoreType.DMA((2, 4)),
            pltpu.SemaphoreType.DMA((2, 4)),
            pltpu.SemaphoreType.DMA((4,)),
            pltpu.SemaphoreType.DMA((4,)),
        ],
        compiler_params=pltpu.CompilerParams(
            collective_id=0, has_side_effects=True, vmem_limit_bytes=16 * 1024 * 1024
        ),
    )(
        *[
            pltpu.with_memory_space_constraint(x, pltpu.HBM)
            for x in (
                tiled(flow_pops),
                tiled(bin_pops),
                tiled(site_kind)[0],
                neighbours,
                bin_rates,
                settle,
                inlet_conc,
            )
        ]
    )
    flow, bins, deposit = pl.pallas_call(
        write_out,
        out_shape=shapes,
        in_specs=[vmem, vmem, vmem],
        out_specs=(hbm, hbm, hbm),
        scratch_shapes=[pltpu.SemaphoreType.DMA((3,))],
        compiler_params=pltpu.CompilerParams(vmem_limit_bytes=16 * 1024 * 1024),
    )(*done)
    return untiled(flow), untiled(bins), deposit


def solution(mesh):
    cut = ("dom", "sub")
    return jax.shard_map(
        on_device,
        mesh=mesh,
        in_specs=(P(cut, None, None), P(cut, None, None), P(cut, None), P(cut, None), P(), P(), P()),
        out_specs=(P(cut, None, None), P(cut, None, None), P(cut, None)),
        check_vma=False,
    )
```

```python
import functools

import jax
import jax.numpy as jnp
from jax import lax
from jax.experimental import pallas as pl
from jax.experimental.pallas import tpu as pltpu
from jax.sharding import PartitionSpec as P

VEL = [
    (0, 0, 0),
    (1, 0, 0),
    (-1, 0, 0),
    (0, 1, 0),
    (0, -1, 0),
    (0, 0, 1),
    (0, 0, -1),
    (1, 1, 0),
    (-1, -1, 0),
    (1, -1, 0),
    (-1, 1, 0),
    (1, 0, 1),
    (-1, 0, -1),
    (1, 0, -1),
    (-1, 0, 1),
    (0, 1, 1),
    (0, -1, -1),
    (0, 1, -1),
    (0, -1, 1),
]
WEIGHT = [1.0 / 3.0] + [1.0 / 18.0] * 6 + [1.0 / 36.0] * 12
OPP = [0, 2, 1, 4, 3, 6, 5, 8, 7, 10, 9, 12, 11, 14, 13, 16, 15, 18, 17]
OMEGA = 1.6
INLET = 0.04
BINS = 12
MESH = pl.DeviceIdType.MESH

FACE_POPS = [
    [q for q in range(1, 19) if VEL[q][d // 2] == 1 - 2 * (d % 2)] for d in range(6)
]
LIVE_SLOT = 5
BIN_SLOT = 6
PACKS = 3
PART = 5
LAT_ROWS, Z_ROWS, PART_ROWS = (2 * PACKS - 1) * 8, PACKS * 8, PART * 8
LATERAL = [(0, 0), (1, 0), (-1, 0), (0, 1), (0, -1)]


def lat_row(h):
    return 8 + LAT_ROWS * h


def own_row(h, way):
    return 8 + Z_ROWS * (2 * h + way)


def z_row(h):
    return 8 + Z_ROWS * h


def part_row(h):
    return 8 + PART_ROWS * h


def slot_at(d, lateral):
    return [VEL[q][:2] for q in FACE_POPS[d]].index(lateral)


def add_up(terms):
    terms = list(terms)
    while len(terms) > 1:
        pairs = [a + b for a, b in zip(terms[::2], terms[1::2])]
        terms = pairs + terms[len(pairs) * 2 :]
    return terms[0]


def roll_lanes(x, shift):
    shift %= 128
    return x if shift == 0 else pltpu.roll(x, shift, 1)


def roll_rows(x, shift):
    shift %= 8
    return x if shift == 0 else pltpu.roll(x, shift, 0)


def kernel(
    layers,
    subs,
    flow_in,
    bins_in,
    kind_in,
    near_in,
    rates_in,
    settle_in,
    conc_in,
    fbuf,
    gbuf,
    dep_ref,
    kind_ref,
    near_ref,
    rates_ref,
    settle_ref,
    conc_ref,
    pf,
    pg_0,
    pg,
    sf,
    sg,
    live_ref,
    dmask_ref,
    dacc,
    lat_0,
    lat_1,
    own_z,
    zwin_0,
    zwin_1,
    pwin_0,
    pwin_1,
    psend,
    ghost_0,
    ghost_1,
    came_ref,
    in_sem,
    send_sem,
    recv_sem,
    mate_send,
    mate_recv,
):
    zwin, pwin, ghost = (zwin_0, zwin_1), (pwin_0, pwin_1), (ghost_0, ghost_1)
    me = lax.axis_index("dom") * subs + lax.axis_index("sub")
    layer = me // 2
    half = me % 2
    mate = 2 * layer + 1 - half
    far = 1 - (me % subs) // 2

    def device(g):
        return (g // subs, g % subs)

    def beyond(way):
        return layer + 1 - 2 * way

    def each_way(do, part=slice(None)):
        for order in ((0, 1), (1, 0)):

            @pl.when(far == order[0])
            def _():
                for way in order[part]:
                    there = beyond(way)
                    pl.when((there >= 0) & (there < layers))(functools.partial(do, way))

    barrier = pltpu.get_barrier_semaphore()

    def greet(way):
        for h in range(2):
            pl.semaphore_signal(
                barrier, inc=1, device_id=device(2 * beyond(way) + h), device_id_type=MESH
            )

    each_way(greet)
    pl.semaphore_signal(barrier, inc=1, device_id=device(mate), device_id_type=MESH)

    pairs = [
        (flow_in, fbuf),
        (kind_in, kind_ref),
        (bins_in, gbuf),
        (rates_in, rates_ref),
        (settle_in, settle_ref),
        (conc_in, conc_ref),
        (near_in, near_ref),
    ]
    loads = [pltpu.make_async_copy(a, b, in_sem.at[n]) for n, (a, b) in enumerate(pairs)]
    for copy in loads:
        copy.start()

    sub = lax.broadcasted_iota(jnp.int32, (8, 128), 0)
    lane = lax.broadcasted_iota(jnp.int32, (8, 128), 1)
    jj = (lane >> 3) & 7
    kk = lane & 7
    low = lane < 64
    even = (sub & 1) == 0
    quarter = sub >> 1
    at = {
        (0, 0): (quarter == 0) & low,
        (0, 7): (quarter == 3) & (lane >= 64),
        (1, 0): jj == 0,
        (1, 7): jj == 7,
        (2, 0): kk == 0,
        (2, 7): kk == 7,
    }

    loads[0].wait()
    loads[1].wait()
    kind = kind_ref[...]
    alive = jnp.where(kind > 0, 1.0, 0.0)
    is_in = kind == 2
    is_end = kind >= 2
    is_fluid = kind == 1

    def moments(f):
        odd = range(1, 19, 2)
        rho = add_up([f[q] + f[q + 1] for q in odd] + [f[0]])
        inv = 1.0 / rho
        gaps = {q: f[q] - f[q + 1] for q in odd}
        vel = []
        for axis in range(3):
            plus = add_up([gaps[q] for q in odd if VEL[q][axis] == 1])
            minus = [gaps[q] for q in odd if VEL[q][axis] == -1]
            vel.append((plus - add_up(minus) if minus else plus) * inv)
        return rho, vel

    def equilibrium(scale, vel):
        base = 1.0 - 1.5 * (vel[0] * vel[0] + vel[1] * vel[1] + vel[2] * vel[2])
        scaled = {w: scale * w for w in set(WEIGHT)}
        out = [None] * 19
        out[0] = scaled[WEIGHT[0]] * base
        for q in range(1, 19, 2):
            along = None
            for axis in range(3):
                if VEL[q][axis] != 0:
                    term = vel[axis]
                    if along is None:
                        along = term if VEL[q][axis] > 0 else -term
                    else:
                        along = along + term if VEL[q][axis] > 0 else along - term
            even = base + 4.5 * along * along
            odd = 3.0 * along
            out[q] = scaled[WEIGHT[q]] * (even + odd)
            out[q + 1] = scaled[WEIGHT[q]] * (even - odd)
        return out

    def put(packs, d, slot, x):
        v, m = slot // 8, slot % 8
        x = roll_lanes(x, m - (0 if d % 2 else 7))
        packs[v] = x if packs[v] is None else jnp.where(kk == m, x, packs[v])

    def gather(ref, row, stride, blocks):
        parts = [
            ref[pl.ds(row + stride * (w >> 1) + (w & 1) - b, 8), :] for b, w in enumerate(blocks)
        ]
        return jnp.where(even, parts[0], parts[1])

    def nearby(q, base):
        return [jnp.clip(near_ref[b, q - 1] - base, 0, 3) for b in range(2)]

    def present(q):
        return jnp.where(even, near_ref[0, q - 1], near_ref[1, q - 1]) >= 0

    def x_shift(r, cx):
        if cx == 0:
            return r
        moved = roll_rows(r, 2 * cx)
        return jnp.where(low, moved, r) if cx > 0 else jnp.where(low, r, moved)

    def local(a, q):
        cx, cy, cz = VEL[q]
        return x_shift(roll_lanes(a, 64 * abs(cx) + 8 * cy + cz), cx)

    def unpack(d, slot, tile, q):
        cx, cy, cz = VEL[q]
        m = slot % 8
        if d // 2 == 0:
            t, h = m // 2, m % 2
            turned = roll_lanes(tile, 64 * h + 8 * cy + cz)
            return roll_rows(turned, -2 * t if d % 2 == 0 else 4 - 2 * t)
        if d // 2 == 1:
            return x_shift(roll_lanes(tile, 64 * abs(cx) - 8 * m + (112 if d % 2 else 0) + cz), cx)
        return x_shift(roll_lanes(tile, 64 * abs(cx) + 8 * cy + (7 if d % 2 else 0) - m), cx)

    def unpack_edge(d, slot, tile, q):
        cx, cy, cz = VEL[q]
        m = slot % 8
        if d // 2 == 1:
            shift = (112 if d % 2 else 0) - 8 * m
        else:
            shift = (7 if d % 2 else 0) - m
        if cx != 0:
            return roll_rows(roll_lanes(tile, shift + 64), -6 * cx)
        return roll_lanes(tile, shift - 56 * cy)

    def face_of(axis, sign):
        return 2 * axis + (0 if sign > 0 else 1)

    def edge_face(q):
        axis = 2 if VEL[q][2] != 0 else 1
        return face_of(axis, VEL[q][axis])

    def lo(axis, sign):
        return at[(axis, 0 if sign > 0 else 7)]

    def mate_copy(n, ref, row, rows, h):
        span = pl.ds(row(h), rows)
        return pltpu.make_async_remote_copy(
            src_ref=ref.at[span],
            dst_ref=ref.at[span],
            send_sem=mate_send.at[n],
            recv_sem=mate_recv.at[n],
            device_id=device(mate),
            device_id_type=MESH,
        )

    def mate_copies(h):
        return (
            mate_copy(0, lat_0, lat_row, LAT_ROWS, h),
            mate_copy(1, own_z, lambda h: own_row(h, 0), 2 * Z_ROWS, h),
            mate_copy(2, lat_1, lat_row, 16, h),
            mate_copy(3, lat_1, lambda h: lat_row(h) + 16, LAT_ROWS - 16, h),
        )

    def z_copy(n, way, h):
        src = (own_z.at[pl.ds(own_row(half, way), Z_ROWS)], psend.at[way])[n]
        dst = (
            zwin[way].at[pl.ds(z_row(half), Z_ROWS)],
            pwin[way].at[pl.ds(part_row(half), PART_ROWS)],
        )[n]
        return pltpu.make_async_remote_copy(
            src_ref=src,
            dst_ref=dst,
            send_sem=send_sem.at[n, 2 * way + h],
            recv_sem=recv_sem.at[n, 2 * way + half],
            device_id=device(2 * beyond(way) + h),
            device_id_type=MESH,
        )

    def z_in(n, way, h):
        src = (own_z.at[pl.ds(own_row(half, way), Z_ROWS)], psend.at[way])[n]
        dst = (
            zwin[way].at[pl.ds(z_row(h), Z_ROWS)],
            pwin[way].at[pl.ds(part_row(h), PART_ROWS)],
        )[n]
        return pltpu.make_async_remote_copy(
            src_ref=src,
            dst_ref=dst,
            send_sem=send_sem.at[n, 2 * way + h],
            recv_sem=recv_sem.at[n, 2 * way + h],
            device_id=device(2 * beyond(1 - way) + h),
            device_id_type=MESH,
        )

    def send_z(n, part=slice(None)):
        def do(way):
            for h in (half, 1 - half):
                z_copy(n, way, h).start()

        each_way(do, part)

    def receive_z(n, side):
        @pl.when(layer > 0 if side == 0 else layer < layers - 1)
        def _():
            for h in range(2):
                z_in(n, side, h).wait_recv()

    def nearer_first(do):
        for order in ((0, 1), (1, 0)):

            @pl.when(far == order[0])
            def _():
                for side in order:
                    do(side)

    def from_side(side):
        return [q for q in range(1, 19) if VEL[q][2] == 1 - 2 * side]

    def collide_bin(pg, n, g, conc, rate, lean4):
        part = (0.125 * rate) * conc
        keep = 1.0 - rate
        pg[7 * n] = keep * g[0] + (part + part)
        x4, y4, z4 = lean4
        for axis, u4 in ((0, x4), (1, y4 - 4.0 * settle_ref[n]), (2, z4)):
            lean = part * u4
            pg[7 * n + 1 + 2 * axis] = keep * g[1 + 2 * axis] + (part + lean)
            pg[7 * n + 2 + 2 * axis] = keep * g[2 + 2 * axis] + (part - lean)

    def collide_inputs():
        f = [fbuf[q] for q in range(19)]
        rho, vel = moments(f)
        target = equilibrium(OMEGA * rho, vel)
        for q in range(19):
            pf[q] = (1.0 - OMEGA) * f[q] + target[q]
        for copy in loads[2:]:
            copy.wait()
        lean4 = [4.0 * u for u in vel]
        for n in range(BINS):
            g = [gbuf[7 * n + i] for i in range(7)]
            collide_bin(pg_0, n, g, add_up(g), rates_ref[n], lean4)

    def at_ends(vel):
        return [jnp.where(is_in, (0.0, 0.0, INLET)[axis], vel[axis]) for axis in range(3)]

    def collide_moved(flow, bins_of):
        rho, vel = moments(flow)
        vel = at_ends(vel)
        target = equilibrium(jnp.where(is_fluid, OMEGA * rho, 1.0), vel)
        keep = jnp.where(is_fluid, 1.0 - OMEGA, 0.0)
        for q in range(19):
            pf[q] = keep * flow[q] + target[q]
        lean4 = [4.0 * u for u in vel]
        for n in range(BINS):
            g = bins_of(n)
            conc = jnp.where(is_in, conc_ref[n], add_up(g))
            collide_bin(pg, n, g, conc, jnp.where(is_fluid, rates_ref[n], 1.0), lean4)

    def pack_z(way):
        d = 4 + way
        packs = [None] * PACKS
        for s, q in enumerate(FACE_POPS[d]):
            put(packs, d, s, pf[q])
        put(packs, d, LIVE_SLOT, alive)
        for n in range(BINS):
            put(packs, d, BIN_SLOT + n, pg_0[7 * n + 1 + d])
        for v, tile in enumerate(packs):
            own_z[pl.ds(pl.multiple_of(own_row(half, way) + 8 * v, 8), 8), :] = tile

    def pack_lateral(ref, axis, pg, last=None):
        ahead = present(1 + 2 * axis)
        if axis == 0:
            spot = 2 * quarter + jnp.where(low, 0, 1)
            spot = jnp.where(ahead, spot, 2 * ((quarter + 3) & 3) + jnp.where(low, 1, 0))
        else:
            spot = jnp.where(ahead, jj, (jj + 7) & 7)
        packs = [None] * PACKS
        rows = [(pf[q], pf[r]) for q, r in zip(FACE_POPS[2 * axis], FACE_POPS[2 * axis + 1])]
        rows.append((alive, alive))
        for n in range(BINS):
            rows.append((pg[7 * n + 1 + 2 * axis], pg[7 * n + 2 + 2 * axis]))
        for slot, (x, y) in enumerate(rows):
            v, m = slot // 8, slot % 8
            x = jnp.where(ahead, x, y)
            if axis == 0:
                x = roll_rows(roll_lanes(x, 64 * (m % 2 - 1)), 2 * (m // 2 - 3))
            else:
                x = roll_lanes(x, 8 * (m - 7))
            packs[v] = x if packs[v] is None else jnp.where(spot == m, x, packs[v])
        row = lat_row(half) + 16 * axis
        for v in range(2):
            ref[pl.ds(pl.multiple_of(row + 8 * v, 8), 8), :] = packs[v]
        if axis == 0:
            return packs[2]
        folded = jnp.where(jj < 3, packs[2], roll_lanes(roll_rows(packs[2], 4), 24))
        folded = jnp.where(sub < 4, folded, roll_rows(last, 4))
        ref[pl.ds(pl.multiple_of(row + 16, 8), 8), :] = folded

    def absent_as_zero(q, v, tile):
        return jnp.where(present(q), tile, 0.0) if v == 0 else tile

    def windows(lat, z_tile):
        memo = {}

        def tile_of(q, d, v):
            if (q, d, v) not in memo:
                if d >= 4:
                    tile = z_tile(q, d - 4, v)
                else:
                    row = lat_row(0) + (16 * (d // 2) + 8 * v if v < 2 else 32)
                    tile = gather(lat, row, LAT_ROWS, nearby(q, 4 * layer))
                    if v == 2:
                        turned = roll_rows(tile, 4)
                        if d // 2 == 1:
                            turned = jnp.where(sub < 4, tile, roll_lanes(turned, -24))
                        tile = turned
                memo[(q, d, v)] = absent_as_zero(q, v, tile)
            return memo[(q, d, v)]

        return (
            lambda d, v: tile_of(OPP[1 + d], d, v),
            lambda q: tile_of(OPP[q], edge_face(q), 0),
        )

    def flow_slot(q):
        return lambda d: FACE_POPS[d].index(q)

    def bin_slot(n):
        return lambda d: BIN_SLOT + n

    def live_slot(d):
        return LIVE_SLOT

    def absorb(first, pg):
        masks = [dmask_ref[i] > 0.5 for i in range(6)]
        for n in range(BINS):
            total = add_up([jnp.where(masks[i - 1], pg[7 * n + OPP[i]], 0.0) for i in range(1, 7)])
            dacc[n] = total if first else dacc[n] + total

    def finish(flow, bins_of):
        vel = at_ends(moments(flow)[1])
        target = equilibrium(jnp.ones_like(vel[0]), vel)
        for q in range(19):
            fbuf[q] = jnp.where(is_fluid, flow[q], jnp.where(is_end, target[q], fbuf[q]))
        x4, y4, z4 = [4.0 * u for u in vel]
        for n in range(BINS):
            g = bins_of(n)
            part = 0.125 * jnp.where(is_in, conc_ref[n], add_up(g))
            target = [part + part]
            for u4 in (x4, y4 - 4.0 * settle_ref[n], z4):
                lean = part * u4
                target += [part + lean, part - lean]
            for i in range(7):
                old = gbuf[7 * n + i]
                gbuf[7 * n + i] = jnp.where(is_fluid, g[i], jnp.where(is_end, target[i], old))

    def move_inside(pg):
        for q in range(1, 19):
            sf[q] = local(pf[q], q)
        for n in range(BINS):
            for i in range(1, 7):
                sg[6 * n + i - 1] = local(pg[7 * n + i], i)

    collide_inputs()
    for way in range(2):
        pack_z(way)
    pack_lateral(lat_0, 1, pg_0, pack_lateral(lat_0, 0, pg_0))
    ends = jnp.where(layer < layers - 1, 1, 0) + jnp.where(layer > 0, 1, 0)
    pl.semaphore_wait(barrier, 1 + 2 * ends)
    out_1, out_z, out_2, out_3 = mate_copies(half)
    in_1, in_z, in_2, in_3 = mate_copies(1 - half)
    core = (me // subs) % 2

    @pl.when(core == 1)
    def _():
        send_z(0, slice(0, 1))
        out_1.start()

    @pl.when(core == 0)
    def _():
        out_1.start()
        send_z(0, slice(0, 1))

    send_z(0, slice(1, 2))
    move_inside(pg_0)
    for q in range(1, 19):
        live_ref[q - 1] = local(alive, q)

    def z_tile(q, way, v):
        base = 4 * layer + (-4 if way == 0 else 4)
        return gather(zwin[way], z_row(0) + 8 * v, Z_ROWS, nearby(q, base))

    in_1.wait_recv()
    face_tile, edge_tile = windows(lat_0, z_tile)

    def within(a, q, slot_of):
        out = a
        axes = [axis for axis in range(2) if VEL[q][axis] != 0]
        for axis in axes:
            d = face_of(axis, VEL[q][axis])
            moved = unpack(d, slot_of(d), face_tile(d, slot_of(d) // 8), q)
            mask = lo(axis, VEL[q][axis])
            if VEL[q][2] != 0:
                mask = mask & ~lo(2, VEL[q][2])
            out = jnp.where(mask, moved, out)
        if len(axes) == 2:
            d = edge_face(q)
            mask = lo(0, VEL[q][0]) & lo(1, VEL[q][1])
            out = jnp.where(mask, unpack_edge(d, slot_of(d), edge_tile(q), q), out)
        return out

    def across(a, q, slot_of):
        cx, cy, cz = VEL[q]
        if cz == 0:
            return a
        d = face_of(2, cz)
        slot = slot_of(d)
        moved = unpack(d, slot, face_tile(d, slot // 8), q)
        for axis in range(2):
            if VEL[q][axis] != 0:
                moved = jnp.where(
                    lo(axis, VEL[q][axis]), unpack_edge(d, slot, edge_tile(q), q), moved
                )
        return jnp.where(lo(2, cz), moved, a)

    flow = [pf[0]]
    for q in range(1, 19):
        lq = within(live_ref[q - 1], q, live_slot)
        live_ref[q - 1] = lq
        flow.append(jnp.where(lq > 0.5, within(sf[q], q, flow_slot(q)), pf[OPP[q]]))
        sf[q] = flow[q]

    def total(rows, pick):
        return add_up([rows[q] for q in range(len(rows)) if pick(VEL[q])])

    level_sum = [
        total(flow, lambda c: c[2] == 0),
        total(flow, lambda c: c[0] == 1 and c[2] == 0)
        - total(flow, lambda c: c[0] == -1 and c[2] == 0),
        total(flow, lambda c: c[1] == 1 and c[2] == 0)
        - total(flow, lambda c: c[1] == -1 and c[2] == 0),
    ]
    parts = [[None] * PART for way in range(2)]

    def put_part(way, tile, m, x):
        packs = [None] * PART
        packs[tile] = parts[way][tile]
        put(packs, 4 + way, 8 * tile + m, x)
        parts[way][tile] = packs[tile]

    for way in range(2):
        rows = FACE_POPS[4 + way]
        for s, q in enumerate(rows):
            put_part(way, 0, s, flow[q])
        out_sum = add_up([flow[q] for q in rows])
        put_part(way, 0, LIVE_SLOT, level_sum[0] + out_sum)
        put_part(way, 3, 4, out_sum)
        x_sum = flow[rows[slot_at(4 + way, (1, 0))]] - flow[rows[slot_at(4 + way, (-1, 0))]]
        y_sum = flow[rows[slot_at(4 + way, (0, 1))]] - flow[rows[slot_at(4 + way, (0, -1))]]
        put_part(way, 3, 2, level_sum[1] + x_sum)
        put_part(way, 3, 3, level_sum[2] + y_sum)
    for n in range(BINS):
        g = [pg_0[7 * n]]
        for i in range(1, 7):
            moved = within(sg[6 * n + i - 1], i, bin_slot(n))
            g.append(jnp.where(live_ref[i - 1] > 0.5, moved, 0.0))
            sg[6 * n + i - 1] = g[i]
        flat = add_up(g[:5])
        v, m = (BIN_SLOT + n) // 8, (BIN_SLOT + n) % 8
        for way in range(2):
            put_part(way, v, m, g[5 + way])
            put_part(way, 4 if v == 1 else 3, m, flat + g[5 + way])
    for way in range(2):
        for v in range(PART):
            psend[way, pl.ds(8 * v, 8), :] = parts[way][v]
    send_z(1)
    out_z.start()

    def cross_1(side):
        nonlocal face_tile, edge_tile
        receive_z(0, side)
        face_tile, edge_tile = windows(lat_0, z_tile)
        for q in from_side(side):
            lq = across(live_ref[q - 1], q, live_slot)
            live_ref[q - 1] = lq
            border = lo(2, VEL[q][2])
            moved = across(sf[q], q, flow_slot(q))
            sf[q] = jnp.where(border & (lq < 0.5), pf[OPP[q]], moved)
        lives = live_ref[4 + side] > 0.5
        for n in range(BINS):
            moved = across(sg[6 * n + 4 + side], 5 + side, bin_slot(n))
            sg[6 * n + 4 + side] = jnp.where(lives, moved, 0.0)

    nearer_first(cross_1)

    def bins_across(n):
        return [pg_0[7 * n]] + [sg[6 * n + i] for i in range(6)]

    new = [pf[0]] + [sf[q] for q in range(1, 19)]
    collide_moved(new, bins_across)
    last = pack_lateral(lat_1, 0, pg)
    out_2.start()
    pack_lateral(lat_1, 1, pg, last)
    out_3.start()
    move_inside(pg)
    for i in range(1, 7):
        dmask_ref[i - 1] = jnp.where(is_fluid & (live_ref[i - 1] < 0.5), 1.0, 0.0)
    absorb(True, pg_0)
    absorb(False, pg)
    table = jnp.zeros((8, 128), jnp.float32)
    for n in range(BINS):
        table = jnp.where(lane == n, jnp.sum(dacc[n], axis=1, keepdims=True), table)
    table = table + roll_rows(table, 2)
    table = table + roll_rows(table, 4)
    dep_ref[...] = table[:2, :BINS]

    place = [
        (
            jnp.where(near_ref[b, 1] >= 0, 1, 0),
            jnp.where(near_ref[b, 3] >= 0, 1, 0),
        )
        for b in range(2)
    ]

    def blocks_by_place(dz, base):
        def pick(wanted):
            ids = [near_ref[0, VEL.index(c) - 1] for c in wanted]
            return jnp.clip(functools.reduce(jnp.maximum, ids) - base, 0, 3)

        here = 2 * half if dz == 0 else pick([(0, 0, dz)])
        along_x = pick([(1, 0, dz), (-1, 0, dz)])
        along_y = pick([(0, 1, dz), (0, -1, dz)])
        last = jnp.clip(6 - here - along_x - along_y, 0, 3)
        px, py = place[0]
        return [
            [
                jnp.where(
                    px == x, jnp.where(py == y, here, along_y), jnp.where(py == y, along_x, last)
                )
                for y in range(2)
            ]
            for x in range(2)
        ]

    in_z.wait_recv()
    mine = blocks_by_place(0, 4 * layer)
    theirs = [blocks_by_place(-1, 4 * layer - 4), blocks_by_place(1, 4 * layer + 4)]
    spots = [(way, y) for way in range(2) for y in range(2)]

    def column(ids, y):
        return [ids[0][y], ids[1][y]]

    arriving, leaving = {}, {}
    for way, y in spots:
        for v in range(PACKS):
            row = own_row(0, 1 - way) + 8 * v
            arriving[way, y, v] = gather(own_z, row, 2 * Z_ROWS, column(mine, y))
        leaving[way, y] = gather(zwin[way], z_row(0), Z_ROWS, column(theirs[way], y))

    def plane(tile_at, slot_of_way):
        out = None
        for way, y in spots:
            s = 2 * way + y
            moved = roll_lanes(tile_at(way, y), s - slot_of_way(way))
            out = moved if out is None else jnp.where(kk == s, moved, out)
        return out

    at_y = kk & 1

    def plane_shift(x, lateral):
        cx, cy = lateral
        if cx != 0:
            turned = roll_lanes(x, 64)
            edge = lo(0, cx)
            inner = edge & (~even if cx > 0 else even)
            out = jnp.where(inner, roll_rows(turned, 3 * cx), x_shift(turned, cx))
            return out, edge & (even if cx > 0 else ~even)
        if cy != 0:
            edge = lo(1, cy)
            inner = edge & ((at_y == 1) if cy > 0 else (at_y == 0))
            out = jnp.where(inner, roll_lanes(x, -55 * cy), roll_lanes(x, 8 * cy))
            return out, edge & ((at_y == 0) if cy > 0 else (at_y == 1))
        return x, None

    def back(lateral):
        return (-lateral[0], -lateral[1])

    def spread(x, m):
        out = x
        for other in range(8):
            if other != m:
                out = jnp.where(kk == other, roll_lanes(x, other - m), out)
        return out

    source_live = plane(lambda way, y: arriving[way, y, 0], lambda way: LIVE_SLOT)
    came = {}
    for c in LATERAL:
        x = plane(lambda way, y: arriving[way, y, 0], lambda way: slot_at(5 - way, c))
        bounce = plane(lambda way, y: leaving[way, y], lambda way: slot_at(4 + way, back(c)))
        moved, outside = plane_shift(x, c)
        lives, _ = plane_shift(source_live, c)
        lives = lives > 0.5
        if outside is not None:
            lives = lives & ~outside
        came[c] = jnp.where(lives, moved, bounce)
    sums = (
        add_up(came.values()),
        came[1, 0] - came[-1, 0],
        came[0, 1] - came[0, -1],
    )
    for n, (way, y) in enumerate(spots):
        s = 2 * way + y
        for t in range(3):
            came_ref[3 * n + t] = spread(sums[t], s)
        lives = spread(source_live, s) > 0.5
        for v in range(PACKS):
            came_ref[12 + PACKS * n + v] = jnp.where(lives, arriving[way, y, v], 0.0)

    def by_slot(value_of):
        row = jnp.zeros((8, 128), jnp.float32)
        for m in range(8):
            if value_of(m) is not None:
                row = jnp.where(kk == m, value_of(m), row)
        return row

    rate_rows = []
    for v in range(PACKS):
        bins = [8 * v + m - BIN_SLOT for m in range(8)]
        rate_rows.append(by_slot(lambda m: rates_ref[bins[m]] if 0 <= bins[m] < BINS else None))
    weights = by_slot(lambda m: OMEGA * (WEIGHT[1] if m == 0 else WEIGHT[7]) if m < 5 else None)
    leans = [
        [
            by_slot(lambda m: float(VEL[FACE_POPS[4 + way][m]][axis]) if m < 5 else None)
            for axis in range(2)
        ]
        for way in range(2)
    ]

    def lateral_sites():
        in_2.wait_recv()
        in_3.wait_recv()
        for q in range(1, 19):
            if VEL[q][:2] != (0, 0):
                sf[q] = within(sf[q], q, flow_slot(q))
        for n in range(BINS):
            for i in range(1, 5):
                sg[6 * n + i - 1] = within(sg[6 * n + i - 1], i, bin_slot(n))

    def ghost_tile(q, way, v):
        cx, cy, cz = VEL[q]
        blocks = []
        for px, py in place:
            blocks.append(2 * (1 - py if cy != 0 else py) + (1 - px if cx != 0 else px))
        return gather(ghost[way], z_row(0) + 8 * v, Z_ROWS, blocks)

    @pl.when(core == 1)
    def _():
        nonlocal face_tile, edge_tile
        face_tile, edge_tile = windows(lat_1, ghost_tile)
        lateral_sites()

    def ghosts(way):
        for y in range(2):
            n = 2 * way + y
            partial = [
                gather(pwin[way], part_row(0) + 8 * v, PART_ROWS, column(theirs[way], y))
                for v in range(PART)
            ]
            came_sum, came_x, came_y = [came_ref[3 * n + t] for t in range(3)]
            rho = spread(partial[0], LIVE_SLOT) + came_sum
            inv = 1.0 / rho
            ux = (spread(partial[3], 2) + came_x) * inv
            uy = (spread(partial[3], 3) + came_y) * inv
            un = (spread(partial[3], 4) - came_sum) * inv
            along = un + leans[way][0] * ux + leans[way][1] * uy
            still = 1.0 - 1.5 * (ux * ux + uy * uy + un * un)
            feq = (weights * rho) * (still + 3.0 * along + 4.5 * along * along)
            lean = 1.0 + 4.0 * un
            for v in range(PACKS):
                conc = partial[4 if v == 1 else 3] + came_ref[12 + PACKS * n + v]
                rate = rate_rows[v]
                tile = (1.0 - rate) * partial[v] + (0.125 * rate) * conc * lean
                if v == 0:
                    tile = jnp.where(kk < 5, (1.0 - OMEGA) * partial[0] + feq, tile)
                ghost[way][pl.ds(z_row(y) + 8 * v, 8), :] = tile

    def cross_2(side):
        nonlocal face_tile, edge_tile
        receive_z(1, side)
        ghosts(side)
        face_tile, edge_tile = windows(lat_1, ghost_tile)
        for q in from_side(side):
            sf[q] = across(sf[q], q, flow_slot(q))
        for n in range(BINS):
            sg[6 * n + 4 + side] = across(sg[6 * n + 4 + side], 5 + side, bin_slot(n))

    nearer_first(cross_2)

    @pl.when(core == 0)
    def _():
        nonlocal face_tile, edge_tile
        face_tile, edge_tile = windows(lat_1, ghost_tile)
        lateral_sites()

    new = [pf[0]]
    for q in range(1, 19):
        new.append(jnp.where(live_ref[q - 1] > 0.5, sf[q], pf[OPP[q]]))

    def bins_moved(n):
        new = [pg[7 * n]]
        for i in range(1, 7):
            new.append(jnp.where(live_ref[i - 1] > 0.5, sg[6 * n + i - 1], 0.0))
        return new

    finish(new, bins_moved)

    for copy in (out_1, out_z, out_2, out_3):
        copy.wait_send()

    def sent(way):
        for n in range(2):
            for h in range(2):
                z_copy(n, way, h).wait_send()

    each_way(sent)


def write_out(flow, bins, deposit, flow_out, bins_out, dep_out, sem):
    pairs = [(bins, bins_out), (flow, flow_out), (deposit, dep_out)]
    copies = [pltpu.make_async_copy(a, b, sem.at[n]) for n, (a, b) in enumerate(pairs)]
    for copy in copies:
        copy.start()
    for copy in copies:
        copy.wait()


def tiled(x):
    x = x.reshape(2, -1, 4, 128)
    return x.transpose(1, 2, 0, 3).reshape(-1, 8, 128)


def untiled(x):
    return x.reshape(-1, 4, 2, 128).transpose(2, 0, 1, 3).reshape(2, -1, 512)


def on_device(flow_pops, bin_pops, site_kind, neighbours, bin_rates, settle, inlet_conc):
    subs = lax.axis_size("sub")
    layers = lax.axis_size("dom") * subs // 2
    hbm = pl.BlockSpec(memory_space=pltpu.HBM)
    vmem = pl.BlockSpec(memory_space=pltpu.VMEM)
    f32 = jnp.float32
    shapes = (
        jax.ShapeDtypeStruct((19, 8, 128), f32),
        jax.ShapeDtypeStruct((7 * BINS, 8, 128), f32),
        jax.ShapeDtypeStruct((2, BINS), f32),
    )
    done = pl.pallas_call(
        functools.partial(kernel, layers, subs),
        out_shape=shapes,
        in_specs=[hbm] * 7,
        out_specs=(vmem, vmem, vmem),
        scratch_shapes=[
            pltpu.VMEM((8, 128), jnp.int32),
            pltpu.SMEM((2, 18), jnp.int32),
            pltpu.SMEM((BINS,), f32),
            pltpu.SMEM((BINS,), f32),
            pltpu.SMEM((BINS,), f32),
            pltpu.VMEM((19, 8, 128), f32),
            pltpu.VMEM((7 * BINS, 8, 128), f32),
            pltpu.VMEM((7 * BINS, 8, 128), f32),
            pltpu.VMEM((19, 8, 128), f32),
            pltpu.VMEM((6 * BINS, 8, 128), f32),
            pltpu.VMEM((18, 8, 128), f32),
            pltpu.VMEM((6, 8, 128), f32),
            pltpu.VMEM((BINS, 8, 128), f32),
            pltpu.VMEM((lat_row(2) + 8, 128), f32),
            pltpu.VMEM((lat_row(2) + 8, 128), f32),
            pltpu.VMEM((own_row(2, 0) + 8, 128), f32),
            pltpu.VMEM((z_row(2) + 8, 128), f32),
            pltpu.VMEM((z_row(2) + 8, 128), f32),
            pltpu.VMEM((part_row(2) + 8, 128), f32),
            pltpu.VMEM((part_row(2) + 8, 128), f32),
            pltpu.VMEM((2, PART_ROWS, 128), f32),
            pltpu.VMEM((z_row(2) + 8, 128), f32),
            pltpu.VMEM((z_row(2) + 8, 128), f32),
            pltpu.VMEM((12 + 4 * PACKS, 8, 128), f32),
            pltpu.SemaphoreType.DMA((7,)),
            pltpu.SemaphoreType.DMA((2, 4)),
            pltpu.SemaphoreType.DMA((2, 4)),
            pltpu.SemaphoreType.DMA((4,)),
            pltpu.SemaphoreType.DMA((4,)),
        ],
        compiler_params=pltpu.CompilerParams(
            collective_id=0, has_side_effects=True, vmem_limit_bytes=16 * 1024 * 1024
        ),
    )(
        *[
            pltpu.with_memory_space_constraint(x, pltpu.HBM)
            for x in (
                tiled(flow_pops),
                tiled(bin_pops),
                tiled(site_kind)[0],
                neighbours,
                bin_rates,
                settle,
                inlet_conc,
            )
        ]
    )
    flow, bins, deposit = pl.pallas_call(
        write_out,
        out_shape=shapes,
        in_specs=[vmem, vmem, vmem],
        out_specs=(hbm, hbm, hbm),
        scratch_shapes=[pltpu.SemaphoreType.DMA((3,))],
        compiler_params=pltpu.CompilerParams(vmem_limit_bytes=16 * 1024 * 1024),
    )(*done)
    return untiled(flow), untiled(bins), deposit


def solution(mesh):
    cut = ("dom", "sub")
    return jax.shard_map(
        on_device,
        mesh=mesh,
        in_specs=(P(cut, None, None), P(cut, None, None), P(cut, None), P(cut, None), P(), P(), P()),
        out_specs=(P(cut, None, None), P(cut, None, None), P(cut, None)),
        check_vma=False,
    )
```
